32 devices in a mesh: dp: 8 (over z, y), seq: 4 (over x, core).
Axes of the slice: x: 2, y: 2, z: 4, core: 2. Of those that a mesh axis runs over, the one named last changes fastest.
Arguments:
- block_input: bfloat16 [16, 2048, 768], P('dp', 'seq'), may hold values from -6 to 6
- slot_spans: int32 [16, 2], P('dp'), may hold values from 0 to 2048, as said below
- output_adjoint: bfloat16 [16, 2048, 768], P('dp', 'seq'), may hold values from -6 to 6
- opening_scale_factor: bfloat16 [768], P(('dp', 'seq')), may hold values from 0.5 to 1.5
- opening_offset_vector: bfloat16 [768], P(('dp', 'seq')), may hold values from -1.796875 to 1.796875
- intake_coefficients: bfloat16 [768, 2304], P(None, ('dp', 'seq')), may hold values from -0.21875 to 0.21875
- intake_offset: bfloat16 [2304], P(('dp', 'seq')), may hold values from -1.796875 to 1.796875
- brief_filter_coefficients: bfloat16 [3, 2304], P(None, ('dp', 'seq')), may hold values from -3.5 to 3.5
- brief_filter_offset: bfloat16 [2304], P(('dp', 'seq')), may hold values from -1.796875 to 1.796875
- direct_path_factor: bfloat16 [768], P(('dp', 'seq')), may hold values from -4 to 4
- filter_final_coefficients: bfloat16 [64, 768], P(None, ('dp', 'seq')), may hold values from -0.0625 to 0.0625
- mixer_output_coefficients: bfloat16 [768, 768], P(None, ('dp', 'seq')), may hold values from -0.21875 to 0.21875
- mixer_output_offset: bfloat16 [768], P(('dp', 'seq')), may hold values from -1.796875 to 1.796875
- closing_scale_factor: bfloat16 [768], P(('dp', 'seq')), may hold values from 0.5 to 1.5
- closing_offset_vector: bfloat16 [768], P(('dp', 'seq')), may hold values from -1.796875 to 1.796875
- expand_coefficients: bfloat16 [768, 3072], P(None, ('dp', 'seq')), may hold values from -0.21875 to 0.21875
- expand_offset: bfloat16 [3072], P(('dp', 'seq')), may hold values from -1.796875 to 1.796875
- contract_coefficients: bfloat16 [3072, 768], P(None, ('dp', 'seq')), may hold values from -0.109375 to 0.109375
- contract_offset: bfloat16 [768], P(('dp', 'seq')), may hold values from -1.796875 to 1.796875
- filter_entry_coefficients: float32 [33, 64], replicated, may hold values from -1 to 1
- filter_entry_offset: float32 [64], replicated, may hold values from -1 to 1
- filter_second_coefficients: float32 [64, 64], replicated, may hold values from -0.75 to 0.75
- filter_second_offset: float32 [64], replicated, may hold values from -1 to 1
- filter_third_coefficients: float32 [64, 64], replicated, may hold values from -0.75 to 0.75
- filter_third_offset: float32 [64], replicated, may hold values from -1 to 1
- periodic_frequency: float32 [64], replicated, may hold values from 0.1 to 1.9
Outputs:
- output: bfloat16 [16, 2048, 768], P('dp', 'seq')
- tokens_grad: bfloat16 [16, 2048, 768], P('dp', 'seq')
- pregain_grad: float32 [768], P(('dp', 'seq'))
- preshift_grad: float32 [768], P(('dp', 'seq'))
- projection_grad: float32 [768, 2304], P(None, ('dp', 'seq'))
- projbias_grad: float32 [2304], P(('dp', 'seq'))
- shortconv_grad: float32 [3, 2304], P(None, ('dp', 'seq'))
- shortbias_grad: float32 [2304], P(('dp', 'seq'))
- skipgain_grad: float32 [768], P(('dp', 'seq'))
- filterout_grad: float32 [64, 768], P(None, ('dp', 'seq'))
- mixweight_grad: float32 [768, 768], P(None, ('dp', 'seq'))
- mixbias_grad: float32 [768], P(('dp', 'seq'))
- postgain_grad: float32 [768], P(('dp', 'seq'))
- postshift_grad: float32 [768], P(('dp', 'seq'))
- upweight_grad: float32 [768, 3072], P(None, ('dp', 'seq'))
- upbias_grad: float32 [3072], P(('dp', 'seq'))
- downweight_grad: float32 [3072, 768], P(None, ('dp', 'seq'))
- downbias_grad: float32 [768], P(('dp', 'seq'))
- featmap_grad: float32 [33, 64], replicated
- featbias_grad: float32 [64], replicated
- midmap_grad: float32 [64, 64], replicated
- midbias_grad: float32 [64], replicated
- topmap_grad: float32 [64, 64], replicated
- topbias_grad: float32 [64], replicated
- sinescale_grad: float32 [64], replicated
The draws below stay inside these ranges and needn't reach their ends.
Inputs may be any that keep to these rules, and one draw needn't show every extreme that they name: `slot_spans`: column 1 of a row is the slot's count of valid positions, from 512 to 2048, and slot 0 has all 2048; column 0 is its first valid position, and the two add up to at most 2048.
All inputs are finite; a program needn't handle non-finite values.
Results may differ from the reference program's by a relative error of at most 0.013.
Values may be sent and summed in bfloat16 or wider, within the bound.
No kernel may reach another device: no remote copies, remote signals or barrier semaphores. Data moves between devices by JAX's collectives and lax.ppermute only.
A program may use at most 256 MiB of HBM per device.

```python
import math
import jax
import jax.numpy as jnp
from jax import lax

HIDDEN_BREADTH = 768
FF = 3072
FILT = 64
EMB = 33
LEN = 2048
SLOTS = 16


def draw_slot_spans(key, part):
    length_key, start_key = jax.random.split(key)
    counts = jax.random.randint(length_key, (SLOTS,), LEN // 4, LEN + 1)
    counts = counts.at[0].set(LEN)
    room = LEN - counts + 1
    starts = jax.random.randint(start_key, (SLOTS,), 0, 1 << 20) % room
    return jnp.stack([starts, counts], axis=1).astype(jnp.int32)


def raised(array, stream_key, source, target, blocks, factor):
    owner, partner = [(jnp.arange(array.shape[dim]) // (array.shape[dim] // blocks)).reshape([-1 if axis == dim else 1 for axis in range(array.ndim)]) for dim in (source, target)]
    chosen = jax.random.permutation(stream_key, blocks)[partner]
    strong = (owner == chosen) | (owner == (partner + blocks // 2) % blocks)
    return jnp.where(strong, factor * array, array)


def shard_levels(key, dims, pieces, low, top_value):
    def one(axis_at, parts):
        draws = jax.random.uniform(jax.random.fold_in(jax.random.fold_in(key, 6), axis_at), (parts,), jnp.float32, low / len(pieces), top_value / len(pieces))
        return jnp.repeat(jnp.exp(draws), dims[axis_at] // parts).reshape((-1,) + (1,) * (len(dims) - axis_at - 1))

    gain = one(*pieces[0])
    for cut in pieces[1:]:
        gain = gain * one(*cut)
    return gain


def gaussian(own_key, dims, deviation, bound, cuts=(), kind=jnp.bfloat16):
    entries = jax.random.normal(own_key, dims, jnp.float32) * deviation
    if len(cuts) > 0:
        entries = shard_levels(own_key, dims, cuts, -0.22, 0.18) * entries
    return jnp.clip(entries, min=-bound, max=bound).astype(kind)


def noise_with(rng, extent, scale, bound, shards, heavy, held_as=jnp.bfloat16):
    array = scale * jax.random.normal(rng, extent, jnp.float32)
    if shards:
        array = array * shard_levels(rng, extent, shards, -0.22, 0.18)
    return jnp.clip(raised(array, jax.random.fold_in(rng, 3), *heavy), -bound, bound).astype(held_as)


def setup_inputs(seed: int = 0) -> dict:
    keys = jax.random.split(jax.random.key(seed), 27)
    block_input = gaussian(keys[0], (SLOTS, LEN, HIDDEN_BREADTH), 1.0, 6.0, ((0, 8), (1, 4)))
    slot_spans = draw_slot_spans(jax.random.fold_in(keys[26], 71), 0)
    output_adjoint = noise_with(keys[2], (SLOTS, LEN, HIDDEN_BREADTH), 1.0, 6.0, ((0, 8), (1, 4)), (0, 2, 8, 2.0))
    opening_scale_factor = jnp.clip(1.0 + 0.1 * jax.random.normal(keys[3], (HIDDEN_BREADTH,), jnp.float32), 0.5, 1.5).astype(jnp.bfloat16)
    opening_offset_vector = gaussian(keys[4], (HIDDEN_BREADTH,), 0.3, 1.796875, ((0, 32),))
    intake_coefficients = gaussian(keys[5], (HIDDEN_BREADTH, 3 * HIDDEN_BREADTH), HIDDEN_BREADTH ** -0.5, 0.21875, ((1, 32),))
    intake_offset = gaussian(keys[6], (3 * HIDDEN_BREADTH,), 0.3, 1.796875, ((0, 32),))
    brief_filter_coefficients = gaussian(keys[7], (3, 3 * HIDDEN_BREADTH), 3 ** -0.5, 3.5, ((1, 32),))
    brief_filter_offset = gaussian(keys[8], (3 * HIDDEN_BREADTH,), 0.3, 1.796875, ((0, 32),))
    direct_path_factor = gaussian(keys[9], (HIDDEN_BREADTH,), 1.0, 4.0, ((0, 32),))
    filter_final_coefficients = gaussian(keys[10], (FILT, HIDDEN_BREADTH), (FILT * LEN // 16) ** -0.5, 0.0625, ((1, 32),))
    mixer_output_coefficients = gaussian(keys[11], (HIDDEN_BREADTH, HIDDEN_BREADTH), HIDDEN_BREADTH ** -0.5, 0.21875, ((1, 32),))
    mixer_output_offset = gaussian(keys[12], (HIDDEN_BREADTH,), 0.3, 1.796875, ((0, 32),))
    closing_scale_factor = jnp.clip(1.0 + 0.1 * jax.random.normal(keys[13], (HIDDEN_BREADTH,), jnp.float32), 0.5, 1.5).astype(jnp.bfloat16)
    closing_offset_vector = gaussian(keys[14], (HIDDEN_BREADTH,), 0.3, 1.796875, ((0, 32),))
    expand_coefficients = gaussian(keys[15], (HIDDEN_BREADTH, FF), HIDDEN_BREADTH ** -0.5, 0.21875, ((1, 32),))
    expand_offset = gaussian(keys[16], (FF,), 0.3, 1.796875, ((0, 32),))
    contract_coefficients = gaussian(keys[17], (FF, HIDDEN_BREADTH), FF ** -0.5, 0.109375, ((1, 32),))
    contract_offset = gaussian(keys[18], (HIDDEN_BREADTH,), 0.3, 1.796875, ((0, 32),))
    filter_entry_coefficients = gaussian(keys[19], (EMB, FILT), EMB ** -0.5, 1.0, (), jnp.float32)
    filter_entry_offset = jnp.clip(jax.random.uniform(keys[20], (FILT,), jnp.float32, -1.0, 1.0), -1.0, 1.0)
    filter_second_coefficients = gaussian(keys[21], (FILT, FILT), FILT ** -0.5, 0.75, (), jnp.float32)
    filter_second_offset = jnp.clip(jax.random.uniform(keys[22], (FILT,), jnp.float32, -1.0, 1.0), -1.0, 1.0)
    filter_third_coefficients = gaussian(keys[23], (FILT, FILT), FILT ** -0.5, 0.75, (), jnp.float32)
    filter_third_offset = jnp.clip(jax.random.uniform(keys[24], (FILT,), jnp.float32, -1.0, 1.0), -1.0, 1.0)
    periodic_frequency = jnp.clip(1.0 + 0.18 * jax.random.normal(keys[25], (FILT,), jnp.float32), 0.1, 1.9)
    return {"block_input": block_input, "slot_spans": slot_spans, "output_adjoint": output_adjoint, "opening_scale_factor": opening_scale_factor, "opening_offset_vector": opening_offset_vector, "intake_coefficients": intake_coefficients, "intake_offset": intake_offset, "brief_filter_coefficients": brief_filter_coefficients, "brief_filter_offset": brief_filter_offset, "direct_path_factor": direct_path_factor, "filter_final_coefficients": filter_final_coefficients, "mixer_output_coefficients": mixer_output_coefficients, "mixer_output_offset": mixer_output_offset, "closing_scale_factor": closing_scale_factor, "closing_offset_vector": closing_offset_vector, "expand_coefficients": expand_coefficients, "expand_offset": expand_offset, "contract_coefficients": contract_coefficients, "contract_offset": contract_offset, "filter_entry_coefficients": filter_entry_coefficients, "filter_entry_offset": filter_entry_offset, "filter_second_coefficients": filter_second_coefficients, "filter_second_offset": filter_second_offset, "filter_third_coefficients": filter_third_coefficients, "filter_third_offset": filter_third_offset, "periodic_frequency": periodic_frequency}


@jax.custom_vjp
def lowered_precision_twin(v):
    return lax.optimization_barrier(v.astype(jnp.bfloat16)).astype(jnp.float32)

@jax.custom_vjp
def low_back(v):
    return v

def low_keep(v):
    return (lowered_precision_twin(v), None)

def low_pass(kept, grad):
    return (grad,)

def back_keep(v):
    return (v, None)

def back_low(kept, grad):
    return (lowered_precision_twin(grad),)
lowered_precision_twin.defvjp(low_keep, low_pass)
low_back.defvjp(back_keep, back_low)

def product(left, right):
    return jnp.dot(left, right, precision=lax.Precision.HIGHEST, preferred_element_type=jnp.float32)

def standardize_features(values, norm_gain, norm_shift):
    centre = values - lax.optimization_barrier(jnp.mean(values, axis=-1, keepdims=True))
    spread = lax.optimization_barrier(jnp.mean(centre * centre, axis=-1, keepdims=True))
    return centre * lax.rsqrt(spread + 1e-05) * norm_gain + norm_shift

def position_features(length, emb_width):
    band_count = (emb_width - 1) // 2
    places = jnp.arange(length).astype(jnp.float32)
    standardized_values = places / (length - 1)
    angles = 2.0 * math.pi * places / length
    band_rates = 0.0001 + (band_count - 1 - 0.0001) * jnp.arange(band_count).astype(jnp.float32) / (band_count - 1)
    phases = angles[:, None] * band_rates[None, :]
    return jnp.concatenate([standardized_values[:, None], jnp.cos(phases), -jnp.sin(phases)], axis=1)

def filter_hidden(features, filter_entry_coefficients, filter_entry_offset, filter_second_coefficients, filter_second_offset, filter_third_coefficients, filter_third_offset, periodic_frequency):
    first = jnp.sin(periodic_frequency * (product(features, filter_entry_coefficients) + filter_entry_offset))
    middle = jnp.sin(periodic_frequency * (product(first, filter_second_coefficients) + filter_second_offset))
    return jnp.sin(periodic_frequency * (product(middle, filter_third_coefficients) + filter_third_offset))

def modulation(length, model_width, offset, channels):
    standardized_values = jnp.arange(length).astype(jnp.float32) / (length - 1)
    slowest = math.log(0.01) / 1.5
    fastest = math.log(0.01) / 0.3
    columns = (offset + jnp.arange(channels)).astype(jnp.float32)
    decays = slowest + (fastest - slowest) * columns / (model_width - 1)
    return jnp.exp(-standardized_values[:, None] * jnp.abs(decays)[None, :]) + 0.05

def causal_conv(kernel, signal):
    length = signal.shape[0]
    spectra = jnp.fft.rfft(signal, n=2 * length, axis=0) * jnp.fft.rfft(kernel, n=2 * length, axis=0)
    return jnp.fft.irfft(spectra, n=2 * length, axis=0)[:length]

def block(sequence_entries, row_mask, parameter_collection):
    opening_scale_factor, opening_offset_vector, intake_coefficients, intake_offset, brief_filter_coefficients, brief_filter_offset, direct_path_factor, filter_final_coefficients, mixer_output_coefficients, mixer_output_offset, closing_scale_factor, closing_offset_vector, expand_coefficients, expand_offset, contract_coefficients, contract_offset, filter_entry_coefficients, filter_entry_offset, filter_second_coefficients, filter_second_offset, filter_third_coefficients, filter_third_offset, periodic_frequency = parameter_collection
    length = sequence_entries.shape[0]
    model_width = sequence_entries.shape[1]
    column = row_mask[:, None]
    standardized_values = lowered_precision_twin(standardize_features(sequence_entries, opening_scale_factor, opening_offset_vector))
    projected = column * (low_back(product(standardized_values, intake_coefficients)) + intake_offset)
    padded = jnp.pad(projected, ((2, 0), (0, 0)))
    conv_out = brief_filter_offset + brief_filter_coefficients[0] * padded[:length] + brief_filter_coefficients[1] * padded[1:length + 1] + brief_filter_coefficients[2] * padded[2:]
    outer_gate = conv_out[:, :model_width]
    inner_gate = conv_out[:, model_width:2 * model_width]
    values = conv_out[:, 2 * model_width:]
    signal = lowered_precision_twin(column * inner_gate * values)
    features = position_features(length, filter_entry_coefficients.shape[0])
    hidden = filter_hidden(features, filter_entry_coefficients, filter_entry_offset, filter_second_coefficients, filter_second_offset, filter_third_coefficients, filter_third_offset, periodic_frequency)
    kernel = product(hidden, filter_final_coefficients) * modulation(length, model_width, 0, model_width)
    carried = lowered_precision_twin(low_back(causal_conv(kernel, low_back(signal))))
    gated_mix = lowered_precision_twin((carried + direct_path_factor * signal) * outer_gate)
    residual = sequence_entries + low_back(product(gated_mix, mixer_output_coefficients)) + mixer_output_offset
    second = lowered_precision_twin(standardize_features(residual, closing_scale_factor, closing_offset_vector))
    up_proj = low_back(product(second, expand_coefficients)) + expand_offset
    active = lowered_precision_twin(jax.nn.gelu(up_proj, approximate=True))
    down_proj = low_back(product(active, contract_coefficients)) + contract_offset
    return column * (residual + down_proj)

def reference(block_input, slot_spans, output_adjoint, opening_scale_factor, opening_offset_vector, intake_coefficients, intake_offset, brief_filter_coefficients, brief_filter_offset, direct_path_factor, filter_final_coefficients, mixer_output_coefficients, mixer_output_offset, closing_scale_factor, closing_offset_vector, expand_coefficients, expand_offset, contract_coefficients, contract_offset, filter_entry_coefficients, filter_entry_offset, filter_second_coefficients, filter_second_offset, filter_third_coefficients, filter_third_offset, periodic_frequency):
    parameter_collection = tuple((parameter_array.astype(jnp.float32) for parameter_array in (opening_scale_factor, opening_offset_vector, intake_coefficients, intake_offset, brief_filter_coefficients, brief_filter_offset, direct_path_factor, filter_final_coefficients, mixer_output_coefficients, mixer_output_offset, closing_scale_factor, closing_offset_vector, expand_coefficients, expand_offset, contract_coefficients, contract_offset, filter_entry_coefficients, filter_entry_offset, filter_second_coefficients, filter_second_offset, filter_third_coefficients, filter_third_offset, periodic_frequency)))
    length = block_input.shape[1]
    places = jnp.arange(length).astype(jnp.int32)

    def per_slot(totals, slot_data):
        slot_tokens, slot_extent, slot_cotangent = slot_data
        first_pos = slot_extent[0].astype(jnp.int32)
        pos_count = slot_extent[1].astype(jnp.int32)
        row_mask = ((places >= first_pos) & (places < first_pos + pos_count)).astype(jnp.float32)

        def forward(slot_rows, *params):
            return block(slot_rows, row_mask, params)
        result, pullback = jax.vjp(forward, slot_tokens.astype(jnp.float32), *parameter_collection)
        gradients = pullback(slot_cotangent.astype(jnp.float32))
        totals = tuple((running_total + partial_term for running_total, partial_term in zip(totals, gradients[1:])))
        return (totals, (result.astype(jnp.bfloat16), gradients[0].astype(jnp.bfloat16)))
    initial = tuple((jnp.zeros_like(parameter_array) for parameter_array in parameter_collection))
    totals, (outputs, input_grads) = lax.scan(per_slot, initial, (block_input, slot_spans, output_adjoint))
    return (outputs, input_grads, totals[0], totals[1], totals[2], totals[3], totals[4], totals[5], totals[6], totals[7], totals[8], totals[9], totals[10], totals[11], totals[12], totals[13], totals[14], totals[15], totals[16], totals[17], totals[18], totals[19], totals[20], totals[21], totals[22])
```

```python
import math

import jax
import jax.numpy as jnp
import ml_dtypes
import numpy as np
from jax import lax
from jax.experimental import pallas as pl
from jax.experimental.pallas import tpu as pltpu
from jax.sharding import PartitionSpec as P

AXES = ("dp", "seq")

F32=jnp.float32; BF=jnp.bfloat16
RADIX=16

def dft_tables(length):
    padded = 2*length
    inner = padded//RADIX
    pairs = RADIX//4
    half = RADIX//2
    m = np.arange(inner)
    mats=[]
    for p in range(pairs):
        for s in (p, half-1-p):
            k2 = 2*(RADIX*m+s)+1
            ang = np.pi*((k2[:,None]*m[None,:])%(2*padded))/padded
            c,sn=np.cos(ang),np.sin(ang)
            mats.append(np.block([[c,sn],[-sn,c]]))
    fwd=np.stack(mats).reshape(pairs,2,2*inner,2*inner)
    inv=np.swapaxes(fwd,-1,-2)/length
    r=np.arange(half)
    th=np.pi*(r[None,:]*(2*np.arange(pairs)[:,None]+1))/RADIX
    coef=np.concatenate([np.cos(th),np.sin(th)],axis=1).astype(np.float32)
    return fwd.astype(ml_dtypes.bfloat16),inv.astype(ml_dtypes.bfloat16),coef

def split_rows(x_ref,coef_ref,p,z_ref,inner):
    step=16
    @pl.loop(0,inner//step)
    def _(i):
        lo=pl.multiple_of(i*step,step)
        rows=pl.ds(lo,step); low=pl.ds(pl.multiple_of(inner+i*step,step),step)
        xs=[x_ref[r,rows,:].astype(F32) for r in range(8)]
        c=[coef_ref[p,r] for r in range(8)]; s=[coef_ref[p,8+r] for r in range(8)]
        ce=xs[0]+c[2]*xs[2]+c[4]*xs[4]+c[6]*xs[6]
        co=c[1]*xs[1]+c[3]*xs[3]+c[5]*xs[5]+c[7]*xs[7]
        se=s[2]*xs[2]+s[4]*xs[4]+s[6]*xs[6]
        so=s[1]*xs[1]+s[3]*xs[3]+s[5]*xs[5]+s[7]*xs[7]
        z_ref[0,rows,:]=(ce+co).astype(BF)
        z_ref[1,rows,:]=(ce-co).astype(BF)
        z_ref[0,low,:]=(-(se+so)).astype(BF)
        z_ref[1,low,:]=(se-so).astype(BF)

def join_rows(w_ref,coef_ref,p,acc_ref,inner,lanes):
    step=16
    @pl.loop(0,inner//step)
    def _(i):
        lo=pl.multiple_of(i*step,step)
        rows=pl.ds(lo,step); low=pl.ds(pl.multiple_of(inner+i*step,step),step)
        r0=w_ref[0,rows,lanes]; r1=w_ref[1,rows,lanes]
        i0=w_ref[0,low,lanes]; i1=w_ref[1,low,lanes]
        rs=(r0+r1,r0-r1); im=(i0-i1,i0+i1)
        for r in range(8):
            if r==0: term=rs[0]
            else: term=coef_ref[p,r]*rs[r%2]-coef_ref[p,8+r]*im[r%2]
            acc_ref[r,rows,:]=jnp.where(p==0,0.0,acc_ref[r,rows,:])+term

def spec_kernel(coef_ref,x_ref,f_ref,o_ref,z_ref):
    p=pl.program_id(0); inner=x_ref.shape[1]
    split_rows(x_ref,coef_ref,p,z_ref,inner)
    for j in range(2):
        o_ref[0,j]=jnp.dot(f_ref[0,j],z_ref[j],preferred_element_type=F32).astype(o_ref.dtype)

def conv_kernel(coef_ref,x_ref,k_ref,f_ref,b_ref,s_ref,y_ref,z_ref,w_ref,acc_ref):
    p=pl.program_id(0); inner=x_ref.shape[1]
    split_rows(x_ref,coef_ref,p,z_ref,inner)
    for j in range(2):
        w_ref[j]=jnp.dot(f_ref[0,j],z_ref[j],preferred_element_type=F32)
    step=16
    for j in range(2):
        @pl.loop(0,inner//step)
        def _(i):
            rows=pl.ds(pl.multiple_of(i*step,step),step); low=pl.ds(pl.multiple_of(inner+i*step,step),step)
            xr=w_ref[j,rows,:]; xi=w_ref[j,low,:]
            kr=k_ref[0,j,rows,:].astype(F32); ki=k_ref[0,j,low,:].astype(F32)
            s_ref[0,j,rows,:]=xr.astype(BF); s_ref[0,j,low,:]=xi.astype(BF)
            z_ref[j,rows,:]=(xr*kr-xi*ki).astype(BF)
            z_ref[j,low,:]=(xr*ki+xi*kr).astype(BF)
    for j in range(2):
        w_ref[j]=jnp.dot(b_ref[0,j],z_ref[j],preferred_element_type=F32)
    join_rows(w_ref,coef_ref,p,acc_ref,inner,slice(None))
    @pl.when(p==pl.num_programs(0)-1)
    def _():
        @pl.loop(0,inner//step)
        def _(i):
            rows=pl.ds(pl.multiple_of(i*step,step),step)
            for r in range(8):
                y_ref[r,rows,:]=acc_ref[r,rows,:].astype(y_ref.dtype)

def back_kernel(coef_ref,g_ref,k_ref,s_ref,f_ref,b_ref,y_ref,kg_ref,z_ref,w_ref,q_ref,v_ref,acc_ref):
    p=pl.program_id(0); inner=g_ref.shape[1]; chans=g_ref.shape[2]
    split_rows(g_ref,coef_ref,p,z_ref,inner)
    for j in range(2):
        w_ref[j]=jnp.dot(f_ref[0,j],z_ref[j],preferred_element_type=F32)
    step=16
    for j in range(2):
        @pl.loop(0,inner//step)
        def _(i):
            rows=pl.ds(pl.multiple_of(i*step,step),step); low=pl.ds(pl.multiple_of(inner+i*step,step),step)
            gr=w_ref[j,rows,:]; gi=w_ref[j,low,:]
            kr=k_ref[0,j,rows,:].astype(F32); ki=k_ref[0,j,low,:].astype(F32)
            q_ref[j,rows,0:chans]=(gr*kr+gi*ki).astype(BF)
            q_ref[j,low,0:chans]=(gi*kr-gr*ki).astype(BF)
            kr=s_ref[0,j,rows,:].astype(F32); ki=s_ref[0,j,low,:].astype(F32)
            q_ref[j,rows,chans:2*chans]=(gr*kr+gi*ki).astype(BF)
            q_ref[j,low,chans:2*chans]=(gi*kr-gr*ki).astype(BF)
    for j in range(2):
        v_ref[j]=jnp.dot(b_ref[0,j],q_ref[j],preferred_element_type=F32)
    join_rows(v_ref,coef_ref,p,acc_ref,inner,slice(0,chans))
    join_rows(v_ref,coef_ref,p,kg_ref,inner,slice(chans,2*chans))
    @pl.when(p==pl.num_programs(0)-1)
    def _():
        @pl.loop(0,inner//step)
        def _(i):
            rows=pl.ds(pl.multiple_of(i*step,step),step)
            for r in range(8):
                y_ref[r,rows,:]=acc_ref[r,rows,:].astype(y_ref.dtype)

PAR=pltpu.CompilerParams(vmem_limit_bytes=52<<20)
SM=pl.BlockSpec(memory_space=pltpu.SMEM)
def whole(shape): return pl.BlockSpec(shape,lambda p:(0,)*len(shape))
def step_of(shape): return pl.BlockSpec((1,)+shape,lambda p:(p,)+(0,)*len(shape))

def spectrum(x,tables):
    fwd,inv,coef=tables
    length,ch=x.shape; inner=2*length//RADIX
    return pl.pallas_call(spec_kernel,grid=(RADIX//4,),
        in_specs=[SM,whole((8,inner,ch)),step_of((2,2*inner,2*inner))],
        out_specs=step_of((2,2*inner,ch)),
        out_shape=jax.ShapeDtypeStruct((RADIX//4,2,2*inner,ch),F32),
        scratch_shapes=[pltpu.VMEM((2,2*inner,ch),BF)],compiler_params=PAR)(coef,x.reshape(8,inner,ch),fwd)

def long_conv(x,kspec,tables):
    fwd,inv,coef=tables
    length,ch=x.shape; inner=2*length//RADIX
    s,y=pl.pallas_call(conv_kernel,grid=(RADIX//4,),
        in_specs=[SM,whole((8,inner,ch)),step_of((2,2*inner,ch)),step_of((2,2*inner,2*inner)),step_of((2,2*inner,2*inner))],
        out_specs=[step_of((2,2*inner,ch)),whole((8,inner,ch))],
        out_shape=[jax.ShapeDtypeStruct((RADIX//4,2,2*inner,ch),BF),jax.ShapeDtypeStruct((8,inner,ch),F32)],
        scratch_shapes=[pltpu.VMEM((2,2*inner,ch),BF),pltpu.VMEM((2,2*inner,ch),F32),pltpu.VMEM((8,inner,ch),F32)],compiler_params=PAR)(coef,x.reshape(8,inner,ch),kspec,fwd,inv)
    return s,y.reshape(length,ch)

def long_back(g,kspec,sspec,tables):
    fwd,inv,coef=tables
    length,ch=g.shape; inner=2*length//RADIX
    y,kg=pl.pallas_call(back_kernel,grid=(RADIX//4,),
        in_specs=[SM,whole((8,inner,ch)),step_of((2,2*inner,ch)),step_of((2,2*inner,ch)),step_of((2,2*inner,2*inner)),step_of((2,2*inner,2*inner))],
        out_specs=[whole((8,inner,ch)),whole((8,inner,ch))],
        out_shape=[jax.ShapeDtypeStruct((8,inner,ch),F32),jax.ShapeDtypeStruct((8,inner,ch),F32)],
        scratch_shapes=[pltpu.VMEM((2,2*inner,ch),BF),pltpu.VMEM((2,2*inner,ch),F32),pltpu.VMEM((2,2*inner,2*ch),BF),pltpu.VMEM((2,2*inner,2*ch),F32),pltpu.VMEM((8,inner,ch),F32)],compiler_params=PAR)(coef,g.reshape(8,inner,ch),kspec,sspec,fwd,inv)
    return y.reshape(length,ch),kg.reshape(length,ch)

def product(left, right):
    return jnp.dot(left, right, precision=lax.Precision.HIGHEST, preferred_element_type=jnp.float32)

def gelu_tanh(values):
    return jax.nn.gelu(values, approximate=True)

def filter_hidden(
    features,
    filter_entry_coefficients,
    filter_entry_offset,
    filter_second_coefficients,
    filter_second_offset,
    filter_third_coefficients,
    filter_third_offset,
    periodic_frequency,
):
    first = jnp.sin(
        periodic_frequency * (product(features, filter_entry_coefficients) + filter_entry_offset)
    )
    middle = jnp.sin(
        periodic_frequency * (product(first, filter_second_coefficients) + filter_second_offset)
    )
    return jnp.sin(
        periodic_frequency * (product(middle, filter_third_coefficients) + filter_third_offset)
    )

def modulation(length, model_width, offset, channels):
    standardized_values = jnp.arange(length).astype(jnp.float32) / (length - 1)
    slowest = math.log(0.01) / 1.5
    fastest = math.log(0.01) / 0.3
    columns = (offset + jnp.arange(channels)).astype(jnp.float32)
    decays = slowest + (fastest - slowest) * columns / (model_width - 1)
    return jnp.exp(-standardized_values[:, None] * jnp.abs(decays)[None, :]) + 0.05

def position_features(length, emb_width):
    band_count = (emb_width - 1) // 2
    places = np.arange(length, dtype=np.float64)
    band_rates = 0.0001 + (band_count - 1 - 0.0001) * np.arange(band_count) / (band_count - 1)
    phases = (2.0 * math.pi * places / length)[:, None] * band_rates[None, :]
    return np.concatenate(
        [(places / (length - 1))[:, None], np.cos(phases), -np.sin(phases)], axis=1
    ).astype(np.float32)


def swap_bit(value, me, bit, count):
    return lax.ppermute(value, AXES, [(i, i ^ (1 << bit)) for i in range(count)])


def bit_of(me, bit):
    return (me >> bit) & 1


def gather_shards(value, me, count, order):
    held = value
    for bit in order[:-1]:
        held = jnp.concatenate([held, swap_bit(held, me, bit, count)], axis=0)
    other = swap_bit(held, me, order[-1], count)
    return place_shards(held, other, me, count, order)


def place_shards(near, other, me, count, order):
    rows = near.shape[0] * 2 // count
    half = count // 2

    def spread(i):
        return sum(((i >> p) & 1) << bit for p, bit in enumerate(order[:-1]))

    def kernel(me_ref, near_ref, other_ref, out_ref, sems):
        own = me_ref[0]
        copies = []
        for i in range(half):
            at = jnp.bitwise_xor(own, spread(i))
            copies.append(pltpu.make_async_copy(near_ref.at[i], out_ref.at[at], sems.at[i]))
            flip = jnp.bitwise_xor(own, spread(i) | (1 << order[-1]))
            copies.append(
                pltpu.make_async_copy(other_ref.at[i], out_ref.at[flip], sems.at[half + i])
            )
        for copy in copies:
            copy.start()
        for copy in copies:
            copy.wait()

    hbm = pl.BlockSpec(memory_space=pl.ANY)
    shape = (count, rows) + near.shape[1:]
    return pl.pallas_call(
        kernel,
        in_specs=[SM, hbm, hbm],
        out_specs=hbm,
        out_shape=jax.ShapeDtypeStruct(shape, near.dtype),
        scratch_shapes=[pltpu.SemaphoreType.DMA((count,))],
    )(
        me.reshape(1).astype(jnp.int32),
        near.reshape((half, rows) + near.shape[1:]),
        other.reshape((half, rows) + near.shape[1:]),
    )


def scatter_sum(value, me, count, order, keep):
    rows, columns = value.shape[1:]
    left = list(range(count.bit_length() - 1))
    for place, bit in enumerate(order):
        low = 1 << sum(1 for b in left if b < bit)
        cut = value.reshape(-1, 2, low * rows, columns)
        mine = lax.dynamic_index_in_dim(cut, bit_of(me, bit), 1, keepdims=False)
        given = lax.dynamic_index_in_dim(cut, 1 - bit_of(me, bit), 1, keepdims=False)
        value = mine.astype(F32) + swap_bit(given, me, bit, count).astype(F32)
        if place < len(order) - 1:
            value = value.astype(keep)
        left.remove(bit)
    return value.reshape(rows, columns)


def sum_everywhere(value, me, count):
    for bit in range(count.bit_length() - 1):
        value = value + swap_bit(value, me, bit, count)
    return value


def orders_of(count):
    bits = count.bit_length() - 1
    first = list(range(bits))
    second = list(range(bits))
    second[1], second[2] = second[2], second[1]
    return first, second


def normalise(values):
    centre = values - jnp.mean(values, axis=-1, keepdims=True)
    spread = jnp.mean(centre * centre, axis=-1, keepdims=True)
    rstd = lax.rsqrt(spread + 1e-05)
    return centre * rstd, rstd


def normalise_back(unit, rstd, incoming):
    return rstd * (
        incoming
        - jnp.mean(incoming, axis=-1, keepdims=True)
        - unit * jnp.mean(incoming * unit, axis=-1, keepdims=True)
    )


def dot_nt(left, right):
    return lax.dot_general(left, right, (((1,), (1,)), ((), ())), preferred_element_type=F32)


def dot_nn(left, right):
    return lax.dot_general(left, right, (((1,), (0,)), ((), ())), preferred_element_type=F32)


def dot_tn(left, right):
    return lax.dot_general(left, right, (((0,), (0,)), ((), ())), preferred_element_type=F32)


def per_device(
    block_input,
    slot_spans,
    output_adjoint,
    opening_scale_factor,
    opening_offset_vector,
    intake_coefficients,
    intake_offset,
    brief_filter_coefficients,
    brief_filter_offset,
    direct_path_factor,
    filter_final_coefficients,
    mixer_output_coefficients,
    mixer_output_offset,
    closing_scale_factor,
    closing_offset_vector,
    expand_coefficients,
    expand_offset,
    contract_coefficients,
    contract_offset,
    filter_entry_coefficients,
    filter_entry_offset,
    filter_second_coefficients,
    filter_second_offset,
    filter_third_coefficients,
    filter_third_offset,
    periodic_frequency,
):
    width = block_input.shape[2]
    local = block_input.shape[1]
    seq_count = lax.axis_size("seq")
    count = lax.axis_size("dp") * seq_count
    seq_index = lax.axis_index("seq")
    me = lax.axis_index("dp") * seq_count + seq_index
    half = seq_count // 2
    group_bits = half.bit_length() - 1
    rank = seq_index % half
    side = seq_index // half
    length = local * seq_count
    channels = width // half
    chan_start = rank * channels
    up, across = orders_of(count)
    down, back = up[::-1], across[::-1]
    tables = tuple(jnp.asarray(t) for t in dft_tables(length))

    vectors = (
        opening_scale_factor,
        opening_offset_vector,
        direct_path_factor,
        mixer_output_offset,
        closing_scale_factor,
        closing_offset_vector,
        contract_offset,
        intake_offset,
        brief_filter_offset,
        brief_filter_coefficients,
        expand_offset,
        filter_final_coefficients,
    )
    pack = jnp.concatenate([v.reshape(-1) for v in vectors])
    pad = -pack.size % 1024
    pack = jnp.concatenate([pack, jnp.zeros((pad,), pack.dtype)]).reshape(8, -1).astype(F32)
    pack_full = gather_shards(pack, me, count, down).reshape(count, -1)
    fields = []
    at = 0
    for v in vectors:
        part = pack_full[:, at : at + v.size]
        at += v.size
        if v.ndim == 1:
            fields.append(part.reshape(-1).astype(F32))
        else:
            rows = v.shape[0]
            fields.append(
                part.reshape(count, rows, -1).transpose(1, 0, 2).reshape(rows, -1).astype(F32)
            )
    (
        gain_one,
        shift_one,
        skip_gain,
        mix_bias,
        gain_two,
        shift_two,
        down_bias,
        intake_bias,
        conv_bias,
        conv_taps,
        up_bias,
        filter_final,
    ) = fields

    intake_shard = intake_coefficients.T
    middle = width // 2
    intake_t = jnp.concatenate(
        [
            gather_shards(intake_shard[:, :middle], me, count, down).reshape(-1, middle),
            gather_shards(intake_shard[:, middle:], me, count, back).reshape(-1, middle),
        ],
        axis=1,
    )

    far = half.bit_length() - 1
    own_rows = lax.dynamic_index_in_dim(block_input, side, 0, keepdims=False)
    far_rows = swap_bit(
        lax.dynamic_index_in_dim(block_input, 1 - side, 0, keepdims=False), me, far, count
    )
    tokens_low = jnp.concatenate([own_rows, far_rows], axis=0)

    intake_t, mix_own, up_own, down_own = lax.optimization_barrier(
        (
            intake_t,
            mixer_output_coefficients.T,
            expand_coefficients.T,
            contract_coefficients.T,
        )
    )
    mix_t = gather_shards(mix_own, me, count, down).reshape(-1, width)
    up_t = gather_shards(up_own, me, count, back).reshape(-1, width)
    down_t = gather_shards(down_own, me, count, down).reshape(width, -1)

    own_adj = lax.dynamic_index_in_dim(output_adjoint, side, 0, keepdims=False)
    far_adj = swap_bit(
        lax.dynamic_index_in_dim(output_adjoint, 1 - side, 0, keepdims=False), me, far, count
    )
    adjoint = jnp.concatenate([own_adj, far_adj], axis=0)

    features = jnp.asarray(position_features(length, filter_entry_coefficients.shape[0]))
    net = (
        filter_entry_coefficients,
        filter_entry_offset,
        filter_second_coefficients,
        filter_second_offset,
        filter_third_coefficients,
        filter_third_offset,
        periodic_frequency,
    )
    hidden, filter_pull = jax.vjp(lambda *w: filter_hidden(features, *w), *net)
    shaping = modulation(length, width, chan_start, channels)
    columns = lax.dynamic_slice_in_dim(filter_final, chan_start, channels, 1)
    kernel_spec = spectrum(product(hidden, columns) * shaping, tables)

    own_base = seq_index * local
    far_base = ((1 - side) * half + rank) * local
    places = jnp.concatenate(
        [own_base + jnp.arange(local), far_base + jnp.arange(local)]
    ).astype(jnp.int32)
    span = lax.dynamic_index_in_dim(slot_spans, side, 0, keepdims=False)
    row_mask = ((places >= span[0]) & (places < span[0] + span[1])).astype(F32)[:, None]
    tokens = tokens_low.astype(F32)
    unit_one, rstd_one = normalise(tokens)
    normed_low = (unit_one * gain_one + shift_one).astype(BF)
    projected = row_mask * (dot_nt(normed_low, intake_t) + intake_bias)
    blocks = projected.reshape(2, local, -1)

    def ring(value, by):
        pairs = []
        for i in range(count):
            group, r = divmod(i, half)
            pairs.append((i, group * half + (r + by) % half))
        return lax.ppermute(value, AXES, pairs)

    ends = ring(blocks[:, local - 2 :], 1)
    wrapped = jnp.stack(
        [jnp.where(side == 1, ends[1], 0.0), jnp.where(side == 0, ends[0], 0.0)]
    )
    before = jnp.where(rank == 0, wrapped, ends)
    extended = jnp.concatenate([before, blocks], axis=1)
    rows = 2 * local

    def shifted(by):
        return extended[:, by : by + local].reshape(rows, -1)

    conv_out = (
        conv_bias
        + conv_taps[0] * shifted(0)
        + conv_taps[1] * shifted(1)
        + conv_taps[2] * shifted(2)
    )
    outer_gate = conv_out[:, :width]
    inner_gate = conv_out[:, width : 2 * width]
    values = conv_out[:, 2 * width :]
    signal = (row_mask * inner_gate * values).astype(BF)

    def traded(near, give):
        got = [near]
        for k in range(1, half):
            got.append(lax.ppermute(give(k), AXES, [(i, i ^ k) for i in range(count)]))
        if half == 2:
            return jnp.where(rank == 0, got[0], got[1]), jnp.where(rank == 0, got[1], got[0])
        stacked = jnp.take(jnp.stack(got), jnp.arange(half) ^ rank, axis=0)
        return tuple(stacked[k] for k in range(half))

    def to_channels(value):
        def give(k):
            return lax.dynamic_slice_in_dim(value, (rank ^ k) * channels, channels, 1)

        pieces = traded(give(0), give)
        first = [jnp.where(side == 0, p[:local], p[local:]) for p in pieces]
        second = [jnp.where(side == 0, p[local:], p[:local]) for p in pieces]
        return jnp.concatenate(first + second, axis=0)

    def to_rows(value):
        def give(k):
            first = lax.dynamic_slice_in_dim(value, (rank ^ k) * local, local, 0)
            second = lax.dynamic_slice_in_dim(value, (half + (rank ^ k)) * local, local, 0)
            return jnp.concatenate(
                [jnp.where(side == 0, first, second), jnp.where(side == 0, second, first)], axis=0
            )

        return jnp.concatenate(traded(give(0), give), axis=1)

    sig_spec, carried_cols = long_conv(to_channels(signal), kernel_spec, tables)
    carried = to_rows(carried_cols.astype(BF)).astype(F32)
    signal_wide = signal.astype(F32)
    joined = carried + skip_gain * signal_wide
    gated_mix = (joined * outer_gate).astype(BF)
    residual = tokens + dot_nt(gated_mix, mix_t) + mix_bias
    unit_two, rstd_two = normalise(residual)
    second_low = (unit_two * gain_two + shift_two).astype(BF)
    up_proj = dot_nt(second_low, up_t) + up_bias
    active_low, gelu_pull = jax.vjp(gelu_tanh, up_proj)
    active_low = active_low.astype(BF)
    output = (row_mask * (residual + dot_nt(active_low, down_t) + down_bias)).astype(BF)

    def to_home(value):
        far_part = swap_bit(value[local:], me, far, count)
        near = value[:local]
        return jnp.where(side == 0, jnp.stack([near, far_part]), jnp.stack([far_part, near]))

    output_home = to_home(output)

    grad_out = row_mask * adjoint.astype(F32)
    grad_low = grad_out.astype(BF)
    down_bias_grad = jnp.sum(grad_out, axis=0)
    down_grad = dot_tn(grad_low, active_low).astype(BF)
    grad_up = gelu_pull(dot_nn(grad_low, down_t))[0]
    up_bias_grad = jnp.sum(grad_up, axis=0)
    grad_up_low = grad_up.astype(BF)
    up_grad = dot_tn(grad_up_low, second_low).astype(BF)
    grad_second = dot_nn(grad_up_low, up_t)
    gain_two_grad = jnp.sum(grad_second * unit_two, axis=0)
    shift_two_grad = jnp.sum(grad_second, axis=0)
    grad_residual = grad_out + normalise_back(unit_two, rstd_two, grad_second * gain_two)
    mix_bias_grad = jnp.sum(grad_residual, axis=0)
    resid_low = grad_residual.astype(BF)
    mix_grad = dot_tn(resid_low, gated_mix).astype(BF)
    down_shard = scatter_sum(down_grad.reshape(count, -1, down_grad.shape[1]), me, count, up, BF)
    up_shard = scatter_sum(up_grad.reshape(count, -1, width), me, count, across, BF)
    mix_shard = scatter_sum(mix_grad.reshape(count, -1, width), me, count, up, BF)

    grad_gated = dot_nn(resid_low, mix_t)
    grad_joined = grad_gated * outer_gate
    skip_grad = jnp.sum(grad_joined * signal_wide, axis=0)
    conv_back_cols, kernel_grad = long_back(
        to_channels(grad_joined.astype(BF)), kernel_spec, sig_spec, tables
    )
    conv_back = to_rows(conv_back_cols.astype(BF)).astype(F32)
    grad_signal = row_mask * (conv_back + skip_gain * grad_joined)
    grad_conv = jnp.concatenate(
        [grad_gated * joined, grad_signal * values, grad_signal * inner_gate], axis=1
    )
    conv_bias_grad = jnp.sum(grad_conv, axis=0)
    taps_grad = jnp.stack([jnp.sum(grad_conv * shifted(k), axis=0) for k in range(3)])
    conv_blocks = grad_conv.reshape(2, local, -1)
    starts = ring(conv_blocks[:, :2], -1)
    wrapped_after = jnp.stack(
        [jnp.where(side == 0, starts[1], 0.0), jnp.where(side == 1, starts[0], 0.0)]
    )
    after = jnp.where(rank == half - 1, wrapped_after, starts)
    grad_extended = jnp.concatenate([conv_blocks, after], axis=1)

    def ahead(by):
        return grad_extended[:, by : by + local].reshape(rows, -1)

    grad_projected = row_mask * (
        conv_taps[2] * ahead(0) + conv_taps[1] * ahead(1) + conv_taps[0] * ahead(2)
    )
    intake_bias_grad = jnp.sum(grad_projected, axis=0)
    projected_low = grad_projected.astype(BF)
    intake_grad = dot_tn(projected_low, normed_low).astype(BF).reshape(count, -1, width)
    intake_shard_grad = jnp.concatenate(
        [
            scatter_sum(intake_grad[:, :, :middle], me, count, up, BF),
            scatter_sum(intake_grad[:, :, middle:], me, count, across, BF),
        ],
        axis=1,
    )
    grad_normed = dot_nn(projected_low, intake_t)
    gain_one_grad = jnp.sum(grad_normed * unit_one, axis=0)
    shift_one_grad = jnp.sum(grad_normed, axis=0)
    tokens_grad = (
        grad_residual + normalise_back(unit_one, rstd_one, grad_normed * gain_one)
    ).astype(BF)
    tokens_home = to_home(tokens_grad)

    shaped_grad = kernel_grad * shaping
    column_grad = product(hidden.T, shaped_grad)
    filter_full = lax.dynamic_update_slice_in_dim(
        jnp.zeros((hidden.shape[1], width), F32), column_grad, chan_start, 1
    )
    net_grads = filter_pull(product(shaped_grad, columns.T))

    vector_grads = (
        gain_one_grad,
        shift_one_grad,
        skip_grad,
        mix_bias_grad,
        gain_two_grad,
        shift_two_grad,
        down_bias_grad,
        intake_bias_grad,
        conv_bias_grad,
        taps_grad,
        up_bias_grad,
        filter_full,
    )
    pieces = []
    for g in vector_grads:
        if g.ndim == 1:
            pieces.append(g.reshape(count, -1))
        else:
            pieces.append(
                g.reshape(g.shape[0], count, -1).transpose(1, 0, 2).reshape(count, -1)
            )
    packed = jnp.concatenate(pieces + [jnp.zeros((count, pad), F32)], axis=1)
    summed = scatter_sum(packed.reshape(count, 8, -1), me, count, up, F32).reshape(-1)
    small = []
    at = 0
    for v in vectors:
        small.append(summed[at : at + v.size].reshape(v.shape))
        at += v.size
    net_flat = sum_everywhere(
        jnp.concatenate([g.reshape(-1) for g in net_grads]), me, count
    )
    net_out = []
    at = 0
    for g in net_grads:
        net_out.append(net_flat[at : at + g.size].reshape(g.shape))
        at += g.size
    return (
        output_home,
        tokens_home,
        small[0],
        small[1],
        intake_shard_grad.T,
        small[7],
        small[9],
        small[8],
        small[2],
        small[11],
        mix_shard.T,
        small[3],
        small[4],
        small[5],
        up_shard.T,
        small[10],
        down_shard.T,
        small[6],
    ) + tuple(net_out)

def solution(mesh):
    in_specs = (
        P("dp", "seq", None),
        P("dp", None),
        P("dp", "seq", None),
        P(("dp", "seq")),
        P(("dp", "seq")),
        P(None, ("dp", "seq")),
        P(("dp", "seq")),
        P(None, ("dp", "seq")),
        P(("dp", "seq")),
        P(("dp", "seq")),
        P(None, ("dp", "seq")),
        P(None, ("dp", "seq")),
        P(("dp", "seq")),
        P(("dp", "seq")),
        P(("dp", "seq")),
        P(None, ("dp", "seq")),
        P(("dp", "seq")),
        P(None, ("dp", "seq")),
        P(("dp", "seq")),
        P(),
        P(),
        P(),
        P(),
        P(),
        P(),
        P(),
    )
    out_specs = (
        P("dp", "seq", None),
        P("dp", "seq", None),
        P(("dp", "seq")),
        P(("dp", "seq")),
        P(None, ("dp", "seq")),
        P(("dp", "seq")),
        P(None, ("dp", "seq")),
        P(("dp", "seq")),
        P(("dp", "seq")),
        P(None, ("dp", "seq")),
        P(None, ("dp", "seq")),
        P(("dp", "seq")),
        P(("dp", "seq")),
        P(("dp", "seq")),
        P(None, ("dp", "seq")),
        P(("dp", "seq")),
        P(None, ("dp", "seq")),
        P(("dp", "seq")),
        P(),
        P(),
        P(),
        P(),
        P(),
        P(),
        P(),
    )
    return jax.shard_map(
        per_device, mesh=mesh, in_specs=in_specs, out_specs=out_specs, check_vma=False
    )
```

```python
import math

import jax
import jax.numpy as jnp
import ml_dtypes
import numpy as np
from jax import lax
from jax.experimental import pallas as pl
from jax.experimental.pallas import tpu as pltpu
from jax.sharding import PartitionSpec as P

AXES = ("dp", "seq")

F32=jnp.float32; BF=jnp.bfloat16
RADIX=16

def dft_tables(length):
    padded = 2*length
    inner = padded//RADIX
    pairs = RADIX//4
    half = RADIX//2
    m = np.arange(inner)
    mats=[]
    for p in range(pairs):
        for s in (p, half-1-p):
            k2 = 2*(RADIX*m+s)+1
            ang = np.pi*((k2[:,None]*m[None,:])%(2*padded))/padded
            c,sn=np.cos(ang),np.sin(ang)
            mats.append(np.block([[c,sn],[-sn,c]]))
    fwd=np.stack(mats).reshape(pairs,2,2*inner,2*inner)
    inv=np.swapaxes(fwd,-1,-2)/length
    r=np.arange(half)
    th=np.pi*(r[None,:]*(2*np.arange(pairs)[:,None]+1))/RADIX
    coef=np.concatenate([np.cos(th),np.sin(th)],axis=1).astype(np.float32)
    return fwd.astype(ml_dtypes.bfloat16),inv.astype(ml_dtypes.bfloat16),coef

def split_rows(x_ref,coef_ref,p,z_ref,inner):
    step=16
    @pl.loop(0,inner//step)
    def _(i):
        lo=pl.multiple_of(i*step,step)
        rows=pl.ds(lo,step); low=pl.ds(pl.multiple_of(inner+i*step,step),step)
        xs=[x_ref[r,rows,:].astype(F32) for r in range(8)]
        c=[coef_ref[p,r] for r in range(8)]; s=[coef_ref[p,8+r] for r in range(8)]
        ce=xs[0]+c[2]*xs[2]+c[4]*xs[4]+c[6]*xs[6]
        co=c[1]*xs[1]+c[3]*xs[3]+c[5]*xs[5]+c[7]*xs[7]
        se=s[2]*xs[2]+s[4]*xs[4]+s[6]*xs[6]
        so=s[1]*xs[1]+s[3]*xs[3]+s[5]*xs[5]+s[7]*xs[7]
        z_ref[0,rows,:]=(ce+co).astype(BF)
        z_ref[1,rows,:]=(ce-co).astype(BF)
        z_ref[0,low,:]=(-(se+so)).astype(BF)
        z_ref[1,low,:]=(se-so).astype(BF)

def join_rows(w_ref,coef_ref,p,acc_ref,inner,lanes):
    step=16
    @pl.loop(0,inner//step)
    def _(i):
        lo=pl.multiple_of(i*step,step)
        rows=pl.ds(lo,step); low=pl.ds(pl.multiple_of(inner+i*step,step),step)
        r0=w_ref[0,rows,lanes]; r1=w_ref[1,rows,lanes]
        i0=w_ref[0,low,lanes]; i1=w_ref[1,low,lanes]
        rs=(r0+r1,r0-r1); im=(i0-i1,i0+i1)
        for r in range(8):
            if r==0: term=rs[0]
            else: term=coef_ref[p,r]*rs[r%2]-coef_ref[p,8+r]*im[r%2]
            acc_ref[r,rows,:]=jnp.where(p==0,0.0,acc_ref[r,rows,:])+term

def spec_kernel(coef_ref,x_ref,f_ref,o_ref,z_ref):
    p=pl.program_id(0); inner=x_ref.shape[1]
    split_rows(x_ref,coef_ref,p,z_ref,inner)
    for j in range(2):
        o_ref[0,j]=jnp.dot(f_ref[0,j],z_ref[j],preferred_element_type=F32).astype(o_ref.dtype)

def conv_kernel(coef_ref,x_ref,k_ref,f_ref,b_ref,s_ref,y_ref,z_ref,w_ref,acc_ref):
    p=pl.program_id(0); inner=x_ref.shape[1]
    split_rows(x_ref,coef_ref,p,z_ref,inner)
    for j in range(2):
        w_ref[j]=jnp.dot(f_ref[0,j],z_ref[j],preferred_element_type=F32)
    step=16
    for j in range(2):
        @pl.loop(0,inner//step)
        def _(i):
            rows=pl.ds(pl.multiple_of(i*step,step),step); low=pl.ds(pl.multiple_of(inner+i*step,step),step)
            xr=w_ref[j,rows,:]; xi=w_ref[j,low,:]
            kr=k_ref[0,j,rows,:].astype(F32); ki=k_ref[0,j,low,:].astype(F32)
            s_ref[0,j,rows,:]=xr.astype(BF); s_ref[0,j,low,:]=xi.astype(BF)
            z_ref[j,rows,:]=(xr*kr-xi*ki).astype(BF)
            z_ref[j,low,:]=(xr*ki+xi*kr).astype(BF)
    for j in range(2):
        w_ref[j]=jnp.dot(b_ref[0,j],z_ref[j],preferred_element_type=F32)
    join_rows(w_ref,coef_ref,p,acc_ref,inner,slice(None))
    @pl.when(p==pl.num_programs(0)-1)
    def _():
        @pl.loop(0,inner//step)
        def _(i):
            rows=pl.ds(pl.multiple_of(i*step,step),step)
            for r in range(8):
                y_ref[r,rows,:]=acc_ref[r,rows,:].astype(y_ref.dtype)

def back_kernel(coef_ref,g_ref,k_ref,s_ref,f_ref,b_ref,y_ref,kg_ref,z_ref,w_ref,q_ref,v_ref,acc_ref):
    p=pl.program_id(0); inner=g_ref.shape[1]; chans=g_ref.shape[2]
    split_rows(g_ref,coef_ref,p,z_ref,inner)
    for j in range(2):
        w_ref[j]=jnp.dot(f_ref[0,j],z_ref[j],preferred_element_type=F32)
    step=16
    for j in range(2):
        @pl.loop(0,inner//step)
        def _(i):
            rows=pl.ds(pl.multiple_of(i*step,step),step); low=pl.ds(pl.multiple_of(inner+i*step,step),step)
            gr=w_ref[j,rows,:]; gi=w_ref[j,low,:]
            kr=k_ref[0,j,rows,:].astype(F32); ki=k_ref[0,j,low,:].astype(F32)
            q_ref[j,rows,0:chans]=(gr*kr+gi*ki).astype(BF)
            q_ref[j,low,0:chans]=(gi*kr-gr*ki).astype(BF)
            kr=s_ref[0,j,rows,:].astype(F32); ki=s_ref[0,j,low,:].astype(F32)
            q_ref[j,rows,chans:2*chans]=(gr*kr+gi*ki).astype(BF)
            q_ref[j,low,chans:2*chans]=(gi*kr-gr*ki).astype(BF)
    for j in range(2):
        v_ref[j]=jnp.dot(b_ref[0,j],q_ref[j],preferred_element_type=F32)
    join_rows(v_ref,coef_ref,p,acc_ref,inner,slice(0,chans))
    join_rows(v_ref,coef_ref,p,kg_ref,inner,slice(chans,2*chans))
    @pl.when(p==pl.num_programs(0)-1)
    def _():
        @pl.loop(0,inner//step)
        def _(i):
            rows=pl.ds(pl.multiple_of(i*step,step),step)
            for r in range(8):
                y_ref[r,rows,:]=acc_ref[r,rows,:].astype(y_ref.dtype)

PAR=pltpu.CompilerParams(vmem_limit_bytes=52<<20)
SM=pl.BlockSpec(memory_space=pltpu.SMEM)
def whole(shape): return pl.BlockSpec(shape,lambda p:(0,)*len(shape))
def step_of(shape): return pl.BlockSpec((1,)+shape,lambda p:(p,)+(0,)*len(shape))

def spectrum(x,tables):
    fwd,inv,coef=tables
    length,ch=x.shape; inner=2*length//RADIX
    return pl.pallas_call(spec_kernel,grid=(RADIX//4,),
        in_specs=[SM,whole((8,inner,ch)),step_of((2,2*inner,2*inner))],
        out_specs=step_of((2,2*inner,ch)),
        out_shape=jax.ShapeDtypeStruct((RADIX//4,2,2*inner,ch),F32),
        scratch_shapes=[pltpu.VMEM((2,2*inner,ch),BF)],compiler_params=PAR)(coef,x.reshape(8,inner,ch),fwd)

def long_conv(x,kspec,tables):
    fwd,inv,coef=tables
    length,ch=x.shape; inner=2*length//RADIX
    s,y=pl.pallas_call(conv_kernel,grid=(RADIX//4,),
        in_specs=[SM,whole((8,inner,ch)),step_of((2,2*inner,ch)),step_of((2,2*inner,2*inner)),step_of((2,2*inner,2*inner))],
        out_specs=[step_of((2,2*inner,ch)),whole((8,inner,ch))],
        out_shape=[jax.ShapeDtypeStruct((RADIX//4,2,2*inner,ch),BF),jax.ShapeDtypeStruct((8,inner,ch),F32)],
        scratch_shapes=[pltpu.VMEM((2,2*inner,ch),BF),pltpu.VMEM((2,2*inner,ch),F32),pltpu.VMEM((8,inner,ch),F32)],compiler_params=PAR)(coef,x.reshape(8,inner,ch),kspec,fwd,inv)
    return s,y.reshape(length,ch)

def long_back(g,kspec,sspec,tables):
    fwd,inv,coef=tables
    length,ch=g.shape; inner=2*length//RADIX
    y,kg=pl.pallas_call(back_kernel,grid=(RADIX//4,),
        in_specs=[SM,whole((8,inner,ch)),step_of((2,2*inner,ch)),step_of((2,2*inner,ch)),step_of((2,2*inner,2*inner)),step_of((2,2*inner,2*inner))],
        out_specs=[whole((8,inner,ch)),whole((8,inner,ch))],
        out_shape=[jax.ShapeDtypeStruct((8,inner,ch),F32),jax.ShapeDtypeStruct((8,inner,ch),F32)],
        scratch_shapes=[pltpu.VMEM((2,2*inner,ch),BF),pltpu.VMEM((2,2*inner,ch),F32),pltpu.VMEM((2,2*inner,2*ch),BF),pltpu.VMEM((2,2*inner,2*ch),F32),pltpu.VMEM((8,inner,ch),F32)],compiler_params=PAR)(coef,g.reshape(8,inner,ch),kspec,sspec,fwd,inv)
    return y.reshape(length,ch),kg.reshape(length,ch)

def ff_kernel(x_ref,g_ref,wu_ref,wd_ref,bu_ref,down_ref,gsec_ref,dwu_ref,dwd_ref,dbu_ref,a_ref,gu_ref):
    f=pl.program_id(0); rows=x_ref.shape[0]; step=256 if rows%256==0 else rows
    wu=wu_ref[...]; wd=wd_ref[...]
    total=jnp.zeros(dbu_ref.shape[1:],F32)
    for r in range(rows//step):
        at=pl.ds(r*step,step)
        up=lax.dot_general(x_ref[at,:],wu,(((1,),(1,)),((),())),preferred_element_type=F32)+bu_ref[0]
        ga=jnp.dot(g_ref[at,:],wd,preferred_element_type=F32)
        sq=up*up
        th=jnp.tanh(up*(GELU_A+(GELU_A*GELU_B)*sq))
        half_one=0.5+0.5*th
        a_ref[at,:]=(up*half_one).astype(BF)
        slope=half_one+(up*half_one*(1.0-th))*(GELU_A+(3.0*GELU_A*GELU_B)*sq)
        gu=ga*slope
        total=total+jnp.sum(gu,axis=0,keepdims=True)
        gu_ref[at,:]=gu.astype(BF)
        down=lax.dot_general(a_ref[at,:],wd,(((1,),(1,)),((),())),preferred_element_type=F32)
        gsec=jnp.dot(gu_ref[at,:],wu,preferred_element_type=F32)
        @pl.when(f==0)
        def _():
            down_ref[at,:]=down
            gsec_ref[at,:]=gsec
        @pl.when(f>0)
        def _():
            down_ref[at,:]+=down
            gsec_ref[at,:]+=gsec
    dbu_ref[0]=total
    dwu_ref[...]=lax.dot_general(gu_ref[...],x_ref[...],(((0,),(0,)),((),())),preferred_element_type=F32).astype(BF)
    dwd_ref[...]=lax.dot_general(g_ref[...],a_ref[...],(((0,),(0,)),((),())),preferred_element_type=F32).astype(BF)

GELU_A=0.7978845608
GELU_B=0.044715

def feed_forward(x,g,wu,wd,bu):
    rows,width=x.shape; hid=wu.shape[0]; blk=512 if hid%512==0 else hid
    n=hid//blk
    return pl.pallas_call(ff_kernel,grid=(n,),
        in_specs=[whole((rows,width)),whole((rows,width)),pl.BlockSpec((blk,width),lambda f:(f,0)),pl.BlockSpec((width,blk),lambda f:(0,f)),pl.BlockSpec((1,1,blk),lambda f:(f,0,0))],
        out_specs=[whole((rows,width)),whole((rows,width)),pl.BlockSpec((blk,width),lambda f:(f,0)),pl.BlockSpec((width,blk),lambda f:(0,f)),pl.BlockSpec((1,1,blk),lambda f:(f,0,0))],
        out_shape=[jax.ShapeDtypeStruct((rows,width),F32),jax.ShapeDtypeStruct((rows,width),F32),jax.ShapeDtypeStruct((hid,width),BF),jax.ShapeDtypeStruct((width,hid),BF),jax.ShapeDtypeStruct((n,1,blk),F32)],
        scratch_shapes=[pltpu.VMEM((rows,blk),BF),pltpu.VMEM((rows,blk),BF)],
        cost_estimate=pl.CostEstimate(flops=12*rows*width*hid,bytes_accessed=8*width*hid+12*rows*width,transcendentals=rows*hid),
        compiler_params=PAR)(x,g,wu,wd,bu.reshape(n,1,blk))

def tail_kernel(p_ref,gg_ref,jo_ref,cb_ref,gj_ref,af_ref,mk_ref,tap_ref,cbias_ref,skip_ref,
                gp_ref,sums_ref,pw_ref,gc_ref):
    b=pl.program_id(0); local=gg_ref.shape[1]; width=gg_ref.shape[2]; wide=3*width
    step=64 if local%64==0 else local; lanes=128
    @pl.when(b==0)
    def _():
        sums_ref[...]=jnp.zeros_like(sums_ref)
    @pl.loop(0,width//lanes)
    def _(j):
        def cols(s): return pl.ds(pl.multiple_of(s*width+j*lanes,lanes),lanes)
        c0=cols(0)
        for s in range(3):
            for r in range(-1,local//step):
                if r<0: pw_ref[s,0:16,:]=p_ref[0,0:16,cols(s)].astype(F32)
                else: pw_ref[s,16+r*step:16+(r+1)*step,:]=p_ref[0,16+r*step:16+(r+1)*step,cols(s)].astype(F32)
        tap=[[tap_ref[k:k+1,cols(s)] for k in range(3)] for s in range(3)]
        cbias=[cbias_ref[0:1,cols(s)] for s in range(3)]
        skip=skip_ref[0:1,c0]
        acc=[[jnp.zeros((8,lanes),F32) for _ in range(5)] for s in range(3)]
        def fold(v): return jnp.sum(v.reshape(-1,8,lanes),axis=0)
        for r in range(local//step):
            lo=r*step
            at=pl.ds(lo,step)
            sh=[[pw_ref[s,14+lo+k:14+lo+k+step,:] for k in range(3)] for s in range(3)]
            gate=[None]+[cbias[s]+tap[s][0]*sh[s][0]+tap[s][1]*sh[s][1]+tap[s][2]*sh[s][2] for s in (1,2)]
            gg=gg_ref[0,at,c0]
            gs=mk_ref[0,at,:]*(cb_ref[0,at,c0].astype(F32)+skip*gj_ref[0,at,c0].astype(F32))
            gc=[gg*jo_ref[0,at,c0].astype(F32),gs*gate[2],gs*gate[1]]
            for s in range(3):
                gc_ref[s,at,:]=gc[s]
                acc[s][0]=acc[s][0]+fold(gc[s])
                for k in range(3):
                    acc[s][1+k]=acc[s][1+k]+fold(gc[s]*sh[s][k])
        for s in range(3):
            gc_ref[s,local:local+8,:]=af_ref[0,:,cols(s)]
        for r in range(local//step):
            lo=r*step
            at=pl.ds(lo,step)
            mk=mk_ref[0,at,:]
            for s in range(3):
                gp=mk*(tap[s][2]*gc_ref[s,at,:]+tap[s][1]*gc_ref[s,lo+1:lo+1+step,:]+tap[s][0]*gc_ref[s,lo+2:lo+2+step,:])
                acc[s][4]=acc[s][4]+fold(gp)
                gp_ref[0,at,cols(s)]=gp.astype(BF)
        for s in range(3):
            for q in range(5):
                sums_ref[q:q+1,cols(s)]+=jnp.sum(acc[s][q],axis=0,keepdims=True)

def tail_back(p,gg,jo,cb,gj,af,mk,taps,cbias,skip):
    blocks,local,width=gg.shape; wide=3*width
    def blk(rows,cols): return pl.BlockSpec((1,rows,cols),lambda b:(b,0,0))
    return pl.pallas_call(tail_kernel,grid=(blocks,),
        in_specs=[blk(local+16,wide),blk(local,width),blk(local,width),blk(local,width),blk(local,width),blk(8,wide),blk(local,1),whole((3,wide)),whole((1,wide)),whole((1,width))],
        out_specs=[blk(local,wide),whole((8,wide))],
        out_shape=[jax.ShapeDtypeStruct((blocks,local,wide),BF),jax.ShapeDtypeStruct((8,wide),F32)],
        scratch_shapes=[pltpu.VMEM((3,local+16,128),F32),pltpu.VMEM((3,local+8,128),F32)],
        compiler_params=PAR)(p,gg,jo,cb,gj,af,mk,taps,cbias,skip)

def product(left, right):
    return jnp.dot(left, right, precision=lax.Precision.HIGHEST, preferred_element_type=jnp.float32)

def gelu_tanh(values):
    return jax.nn.gelu(values, approximate=True)

def filter_hidden(
    features,
    filter_entry_coefficients,
    filter_entry_offset,
    filter_second_coefficients,
    filter_second_offset,
    filter_third_coefficients,
    filter_third_offset,
    periodic_frequency,
):
    first = jnp.sin(
        periodic_frequency * (product(features, filter_entry_coefficients) + filter_entry_offset)
    )
    middle = jnp.sin(
        periodic_frequency * (product(first, filter_second_coefficients) + filter_second_offset)
    )
    return jnp.sin(
        periodic_frequency * (product(middle, filter_third_coefficients) + filter_third_offset)
    )

def modulation(length, model_width, offset, channels):
    standardized_values = jnp.arange(length).astype(jnp.float32) / (length - 1)
    slowest = math.log(0.01) / 1.5
    fastest = math.log(0.01) / 0.3
    columns = (offset + jnp.arange(channels)).astype(jnp.float32)
    decays = slowest + (fastest - slowest) * columns / (model_width - 1)
    return jnp.exp(-standardized_values[:, None] * jnp.abs(decays)[None, :]) + 0.05

def position_features(length, emb_width):
    band_count = (emb_width - 1) // 2
    places = np.arange(length, dtype=np.float64)
    band_rates = 0.0001 + (band_count - 1 - 0.0001) * np.arange(band_count) / (band_count - 1)
    phases = (2.0 * math.pi * places / length)[:, None] * band_rates[None, :]
    return np.concatenate(
        [(places / (length - 1))[:, None], np.cos(phases), -np.sin(phases)], axis=1
    ).astype(np.float32)


def swap_bit(value, me, bit, count):
    return lax.ppermute(value, AXES, [(i, i ^ (1 << bit)) for i in range(count)])


def bit_of(me, bit):
    return (me >> bit) & 1


def gather_shards(value, me, count, order):
    held = value
    for bit in order[:-1]:
        held = jnp.concatenate([held, swap_bit(held, me, bit, count)], axis=0)
    other = swap_bit(held, me, order[-1], count)
    return place_shards(held, other, me, count, order)


def place_shards(near, other, me, count, order):
    rows = near.shape[0] * 2 // count
    half = count // 2

    def spread(i):
        return sum(((i >> p) & 1) << bit for p, bit in enumerate(order[:-1]))

    def kernel(me_ref, near_ref, other_ref, out_ref):
        own = me_ref[0]
        for i in range(half):
            out_ref[jnp.bitwise_xor(own, spread(i))] = near_ref[i]
            out_ref[jnp.bitwise_xor(own, spread(i) | (1 << order[-1]))] = other_ref[i]

    vmem = pl.BlockSpec(memory_space=pltpu.VMEM)
    shape = (count, rows) + near.shape[1:]
    return pl.pallas_call(
        kernel,
        in_specs=[SM, vmem, vmem],
        out_specs=vmem,
        out_shape=jax.ShapeDtypeStruct(shape, near.dtype),
        compiler_params=PAR,
    )(
        me.reshape(1).astype(jnp.int32),
        near.reshape((half, rows) + near.shape[1:]),
        other.reshape((half, rows) + near.shape[1:]),
    )


def scatter_sum(value, me, count, order, keep):
    rows, columns = value.shape[1:]
    left = list(range(count.bit_length() - 1))
    for place, bit in enumerate(order):
        low = 1 << sum(1 for b in left if b < bit)
        cut = value.reshape(-1, 2, low * rows, columns)
        mine = lax.dynamic_index_in_dim(cut, bit_of(me, bit), 1, keepdims=False)
        given = lax.dynamic_index_in_dim(cut, 1 - bit_of(me, bit), 1, keepdims=False)
        value = mine.astype(F32) + swap_bit(given, me, bit, count).astype(F32)
        if place < len(order) - 1:
            value = value.astype(keep)
        left.remove(bit)
    return value.reshape(rows, columns)


def sum_everywhere(value, me, count):
    for bit in range(count.bit_length() - 1):
        value = value + swap_bit(value, me, bit, count)
    return value


def orders_of(count):
    bits = count.bit_length() - 1
    first = list(range(bits))
    second = list(range(bits))
    second[1], second[2] = second[2], second[1]
    return first, second


def normalise(values):
    centre = values - jnp.mean(values, axis=-1, keepdims=True)
    spread = jnp.mean(centre * centre, axis=-1, keepdims=True)
    rstd = lax.rsqrt(spread + 1e-05)
    return centre * rstd, rstd


def normalise_back(unit, rstd, incoming):
    return rstd * (
        incoming
        - jnp.mean(incoming, axis=-1, keepdims=True)
        - unit * jnp.mean(incoming * unit, axis=-1, keepdims=True)
    )


def dot_nt(left, right):
    return lax.dot_general(left, right, (((1,), (1,)), ((), ())), preferred_element_type=F32)


def dot_nn(left, right):
    return lax.dot_general(left, right, (((1,), (0,)), ((), ())), preferred_element_type=F32)


def dot_tn(left, right):
    return lax.dot_general(left, right, (((0,), (0,)), ((), ())), preferred_element_type=F32)


def per_device(
    block_input,
    slot_spans,
    output_adjoint,
    opening_scale_factor,
    opening_offset_vector,
    intake_coefficients,
    intake_offset,
    brief_filter_coefficients,
    brief_filter_offset,
    direct_path_factor,
    filter_final_coefficients,
    mixer_output_coefficients,
    mixer_output_offset,
    closing_scale_factor,
    closing_offset_vector,
    expand_coefficients,
    expand_offset,
    contract_coefficients,
    contract_offset,
    filter_entry_coefficients,
    filter_entry_offset,
    filter_second_coefficients,
    filter_second_offset,
    filter_third_coefficients,
    filter_third_offset,
    periodic_frequency,
):
    width = block_input.shape[2]
    local = block_input.shape[1]
    seq_count = lax.axis_size("seq")
    count = lax.axis_size("dp") * seq_count
    seq_index = lax.axis_index("seq")
    me = lax.axis_index("dp") * seq_count + seq_index
    half = seq_count // 2
    group_bits = half.bit_length() - 1
    rank = seq_index % half
    side = seq_index // half
    length = local * seq_count
    channels = width // half
    chan_start = rank * channels
    up, across = orders_of(count)
    down, back = up[::-1], across[::-1]
    tables = tuple(jnp.asarray(t) for t in dft_tables(length))

    vectors = (
        opening_scale_factor,
        opening_offset_vector,
        direct_path_factor,
        mixer_output_offset,
        closing_scale_factor,
        closing_offset_vector,
        contract_offset,
        intake_offset,
        brief_filter_offset,
        brief_filter_coefficients,
        expand_offset,
        filter_final_coefficients,
    )
    pack = jnp.concatenate([v.reshape(-1) for v in vectors])
    pad = -pack.size % 1024
    pack = jnp.concatenate([pack, jnp.zeros((pad,), pack.dtype)]).reshape(8, -1).astype(F32)
    pack_full = gather_shards(pack, me, count, down).reshape(count, -1)
    fields = []
    at = 0
    for v in vectors:
        part = pack_full[:, at : at + v.size]
        at += v.size
        if v.ndim == 1:
            fields.append(part.reshape(-1).astype(F32))
        else:
            rows = v.shape[0]
            fields.append(
                part.reshape(count, rows, -1).transpose(1, 0, 2).reshape(rows, -1).astype(F32)
            )
    (
        gain_one,
        shift_one,
        skip_gain,
        mix_bias,
        gain_two,
        shift_two,
        down_bias,
        intake_bias,
        conv_bias,
        conv_taps,
        up_bias,
        filter_final,
    ) = fields

    intake_shard = intake_coefficients.T
    middle = width // 2
    intake_t = jnp.concatenate(
        [
            gather_shards(intake_shard[:, :middle], me, count, down).reshape(-1, middle),
            gather_shards(intake_shard[:, middle:], me, count, back).reshape(-1, middle),
        ],
        axis=1,
    )

    far = half.bit_length() - 1
    own_rows = lax.dynamic_index_in_dim(block_input, side, 0, keepdims=False)
    far_rows = swap_bit(
        lax.dynamic_index_in_dim(block_input, 1 - side, 0, keepdims=False), me, far, count
    )
    tokens_low = jnp.concatenate([own_rows, far_rows], axis=0)

    intake_t, mix_own, up_own, down_own = lax.optimization_barrier(
        (
            intake_t,
            mixer_output_coefficients.T,
            expand_coefficients.T,
            contract_coefficients.T,
        )
    )
    mix_t = gather_shards(mix_own, me, count, down).reshape(-1, width)
    up_t = gather_shards(up_own, me, count, back).reshape(-1, width)
    down_t = gather_shards(down_own, me, count, down).reshape(width, -1)

    own_adj = lax.dynamic_index_in_dim(output_adjoint, side, 0, keepdims=False)
    far_adj = swap_bit(
        lax.dynamic_index_in_dim(output_adjoint, 1 - side, 0, keepdims=False), me, far, count
    )
    adjoint = jnp.concatenate([own_adj, far_adj], axis=0)

    features = jnp.asarray(position_features(length, filter_entry_coefficients.shape[0]))
    net = (
        filter_entry_coefficients,
        filter_entry_offset,
        filter_second_coefficients,
        filter_second_offset,
        filter_third_coefficients,
        filter_third_offset,
        periodic_frequency,
    )
    hidden, filter_pull = jax.vjp(lambda *w: filter_hidden(features, *w), *net)
    shaping = modulation(length, width, chan_start, channels)
    columns = lax.dynamic_slice_in_dim(filter_final, chan_start, channels, 1)
    kernel_spec = spectrum(product(hidden, columns) * shaping, tables)

    own_base = seq_index * local
    far_base = ((1 - side) * half + rank) * local
    places = jnp.concatenate(
        [own_base + jnp.arange(local), far_base + jnp.arange(local)]
    ).astype(jnp.int32)
    span = lax.dynamic_index_in_dim(slot_spans, side, 0, keepdims=False)
    row_mask = ((places >= span[0]) & (places < span[0] + span[1])).astype(F32)[:, None]
    tokens = tokens_low.astype(F32)
    unit_one, rstd_one = normalise(tokens)
    normed_low = (unit_one * gain_one + shift_one).astype(BF)
    projected = row_mask * (dot_nt(normed_low, intake_t) + intake_bias)
    blocks = projected.reshape(2, local, -1)

    def ring(value, by):
        pairs = []
        for i in range(count):
            group, r = divmod(i, half)
            pairs.append((i, group * half + (r + by) % half))
        return lax.ppermute(value, AXES, pairs)

    ends = ring(blocks[:, local - 2 :], 1)
    wrapped = jnp.stack(
        [jnp.where(side == 1, ends[1], 0.0), jnp.where(side == 0, ends[0], 0.0)]
    )
    before = jnp.where(rank == 0, wrapped, ends)
    extended = jnp.concatenate([before, blocks], axis=1)
    rows = 2 * local

    def shifted(by):
        return extended[:, by : by + local].reshape(rows, -1)

    conv_out = (
        conv_bias
        + conv_taps[0] * shifted(0)
        + conv_taps[1] * shifted(1)
        + conv_taps[2] * shifted(2)
    )
    outer_gate = conv_out[:, :width]
    inner_gate = conv_out[:, width : 2 * width]
    values = conv_out[:, 2 * width :]
    signal = (row_mask * inner_gate * values).astype(BF)

    def traded(near, give):
        got = [near]
        for k in range(1, half):
            got.append(lax.ppermute(give(k), AXES, [(i, i ^ k) for i in range(count)]))
        if half == 2:
            return jnp.where(rank == 0, got[0], got[1]), jnp.where(rank == 0, got[1], got[0])
        stacked = jnp.take(jnp.stack(got), jnp.arange(half) ^ rank, axis=0)
        return tuple(stacked[k] for k in range(half))

    def to_channels(value):
        def give(k):
            return lax.dynamic_slice_in_dim(value, (rank ^ k) * channels, channels, 1)

        pieces = traded(give(0), give)
        first = [jnp.where(side == 0, p[:local], p[local:]) for p in pieces]
        second = [jnp.where(side == 0, p[local:], p[:local]) for p in pieces]
        return jnp.concatenate(first + second, axis=0)

    def to_rows(value):
        def give(k):
            first = lax.dynamic_slice_in_dim(value, (rank ^ k) * local, local, 0)
            second = lax.dynamic_slice_in_dim(value, (half + (rank ^ k)) * local, local, 0)
            return jnp.concatenate(
                [jnp.where(side == 0, first, second), jnp.where(side == 0, second, first)], axis=0
            )

        return jnp.concatenate(traded(give(0), give), axis=1)

    def blocks_of(value):
        return value.reshape(2, local, -1)

    projected_low_all = jnp.concatenate(
        [jnp.zeros((2, 14, before.shape[2]), BF), before.astype(BF), blocks.astype(BF)], axis=1
    )
    sig_spec, carried_cols = long_conv(to_channels(signal), kernel_spec, tables)
    carried = to_rows(carried_cols.astype(BF)).astype(F32)
    signal_wide = signal.astype(F32)
    joined = carried + skip_gain * signal_wide
    joined_low = joined.astype(BF)
    gated_mix = (joined * outer_gate).astype(BF)
    residual = tokens + dot_nt(gated_mix, mix_t) + mix_bias
    unit_two, rstd_two = normalise(residual)
    second_low = (unit_two * gain_two + shift_two).astype(BF)
    grad_out = row_mask * adjoint.astype(F32)
    grad_low = grad_out.astype(BF)
    down_proj, grad_second, up_grad, down_grad, up_bias_grad = feed_forward(
        second_low, grad_low, up_t, down_t, up_bias
    )
    up_bias_grad = up_bias_grad.reshape(-1)
    output = (row_mask * (residual + down_proj + down_bias)).astype(BF)

    def to_home(value):
        far_part = swap_bit(value[local:], me, far, count)
        near = value[:local]
        return jnp.where(side == 0, jnp.stack([near, far_part]), jnp.stack([far_part, near]))

    output_home = to_home(output)

    down_bias_grad = jnp.sum(grad_out, axis=0)
    gain_two_grad = jnp.sum(grad_second * unit_two, axis=0)
    shift_two_grad = jnp.sum(grad_second, axis=0)
    grad_residual = grad_out + normalise_back(unit_two, rstd_two, grad_second * gain_two)
    mix_bias_grad = jnp.sum(grad_residual, axis=0)
    resid_low = grad_residual.astype(BF)
    mix_grad = dot_tn(resid_low, gated_mix).astype(BF)
    down_shard = scatter_sum(down_grad.reshape(count, -1, down_grad.shape[1]), me, count, up, BF)
    up_shard = scatter_sum(up_grad.reshape(count, -1, width), me, count, across, BF)
    mix_shard = scatter_sum(mix_grad.reshape(count, -1, width), me, count, up, BF)

    grad_gated = dot_nn(resid_low, mix_t)
    grad_joined = grad_gated * outer_gate
    grad_joined_low = grad_joined.astype(BF)
    skip_grad = jnp.sum(grad_joined * signal_wide, axis=0)
    conv_back_cols, kernel_grad = long_back(
        to_channels(grad_joined_low), kernel_spec, sig_spec, tables
    )
    conv_back_low = to_rows(conv_back_cols.astype(BF))
    conv_back = conv_back_low.astype(F32)
    first = blocks_of(grad_gated)[:, :2]
    first_signal = blocks_of(row_mask)[:, :2] * (
        blocks_of(conv_back)[:, :2] + skip_gain * blocks_of(grad_joined_low)[:, :2].astype(F32)
    )
    starts = ring(
        jnp.concatenate(
            [
                first * blocks_of(joined_low)[:, :2].astype(F32),
                first_signal * blocks_of(values)[:, :2],
                first_signal * blocks_of(inner_gate)[:, :2],
            ],
            axis=2,
        ),
        -1,
    )
    wrapped_after = jnp.stack(
        [jnp.where(side == 0, starts[1], 0.0), jnp.where(side == 1, starts[0], 0.0)]
    )
    after = jnp.where(rank == half - 1, wrapped_after, starts)
    after = jnp.concatenate([after, jnp.zeros((2, 6, after.shape[2]), F32)], axis=1)
    grad_projected, sums = tail_back(
        projected_low_all,
        blocks_of(grad_gated),
        blocks_of(joined_low),
        blocks_of(conv_back_low),
        blocks_of(grad_joined_low),
        after,
        blocks_of(row_mask),
        conv_taps,
        conv_bias.reshape(1, -1),
        skip_gain.reshape(1, -1),
    )
    conv_bias_grad = sums[0]
    taps_grad = sums[1:4]
    intake_bias_grad = sums[4]
    projected_low = grad_projected.reshape(rows, -1)
    intake_grad = dot_tn(projected_low, normed_low).astype(BF).reshape(count, -1, width)
    intake_shard_grad = jnp.concatenate(
        [
            scatter_sum(intake_grad[:, :, :middle], me, count, up, BF),
            scatter_sum(intake_grad[:, :, middle:], me, count, across, BF),
        ],
        axis=1,
    )
    grad_normed = dot_nn(projected_low, intake_t)
    gain_one_grad = jnp.sum(grad_normed * unit_one, axis=0)
    shift_one_grad = jnp.sum(grad_normed, axis=0)
    tokens_grad = (
        grad_residual + normalise_back(unit_one, rstd_one, grad_normed * gain_one)
    ).astype(BF)
    tokens_home = to_home(tokens_grad)

    shaped_grad = kernel_grad * shaping
    column_grad = product(hidden.T, shaped_grad)
    filter_full = lax.dynamic_update_slice_in_dim(
        jnp.zeros((hidden.shape[1], width), F32), column_grad, chan_start, 1
    )
    net_grads = filter_pull(product(shaped_grad, columns.T))

    vector_grads = (
        gain_one_grad,
        shift_one_grad,
        skip_grad,
        mix_bias_grad,
        gain_two_grad,
        shift_two_grad,
        down_bias_grad,
        intake_bias_grad,
        conv_bias_grad,
        taps_grad,
        up_bias_grad,
        filter_full,
    )
    pieces = []
    for g in vector_grads:
        if g.ndim == 1:
            pieces.append(g.reshape(count, -1))
        else:
            pieces.append(
                g.reshape(g.shape[0], count, -1).transpose(1, 0, 2).reshape(count, -1)
            )
    packed = jnp.concatenate(pieces + [jnp.zeros((count, pad), F32)], axis=1)
    summed = scatter_sum(packed.reshape(count, 8, -1), me, count, up, F32).reshape(-1)
    small = []
    at = 0
    for v in vectors:
        small.append(summed[at : at + v.size].reshape(v.shape))
        at += v.size
    net_flat = sum_everywhere(
        jnp.concatenate([g.reshape(-1) for g in net_grads]), me, count
    )
    net_out = []
    at = 0
    for g in net_grads:
        net_out.append(net_flat[at : at + g.size].reshape(g.shape))
        at += g.size
    return (
        output_home,
        tokens_home,
        small[0],
        small[1],
        intake_shard_grad.T,
        small[7],
        small[9],
        small[8],
        small[2],
        small[11],
        mix_shard.T,
        small[3],
        small[4],
        small[5],
        up_shard.T,
        small[10],
        down_shard.T,
        small[6],
    ) + tuple(net_out)

def solution(mesh):
    in_specs = (
        P("dp", "seq", None),
        P("dp", None),
        P("dp", "seq", None),
        P(("dp", "seq")),
        P(("dp", "seq")),
        P(None, ("dp", "seq")),
        P(("dp", "seq")),
        P(None, ("dp", "seq")),
        P(("dp", "seq")),
        P(("dp", "seq")),
        P(None, ("dp", "seq")),
        P(None, ("dp", "seq")),
        P(("dp", "seq")),
        P(("dp", "seq")),
        P(("dp", "seq")),
        P(None, ("dp", "seq")),
        P(("dp", "seq")),
        P(None, ("dp", "seq")),
        P(("dp", "seq")),
        P(),
        P(),
        P(),
        P(),
        P(),
        P(),
        P(),
    )
    out_specs = (
        P("dp", "seq", None),
        P("dp", "seq", None),
        P(("dp", "seq")),
        P(("dp", "seq")),
        P(None, ("dp", "seq")),
        P(("dp", "seq")),
        P(None, ("dp", "seq")),
        P(("dp", "seq")),
        P(("dp", "seq")),
        P(None, ("dp", "seq")),
        P(None, ("dp", "seq")),
        P(("dp", "seq")),
        P(("dp", "seq")),
        P(("dp", "seq")),
        P(None, ("dp", "seq")),
        P(("dp", "seq")),
        P(None, ("dp", "seq")),
        P(("dp", "seq")),
        P(),
        P(),
        P(),
        P(),
        P(),
        P(),
        P(),
    )
    return jax.shard_map(
        per_device, mesh=mesh, in_specs=in_specs, out_specs=out_specs, check_vma=False
    )
```

```python
import math

import jax
import jax.numpy as jnp
import ml_dtypes
import numpy as np
from jax import lax
from jax.experimental import pallas as pl
from jax.experimental.pallas import tpu as pltpu
from jax.sharding import PartitionSpec as P

AXES = ("dp", "seq")

F32=jnp.float32; BF=jnp.bfloat16
RADIX=16

def dft_tables(length):
    padded = 2*length
    inner = padded//RADIX
    pairs = RADIX//4
    half = RADIX//2
    m = np.arange(inner)
    mats=[]
    for p in range(pairs):
        for s in (p, half-1-p):
            k2 = 2*(RADIX*m+s)+1
            ang = np.pi*((k2[:,None]*m[None,:])%(2*padded))/padded
            c,sn=np.cos(ang),np.sin(ang)
            mats.append(np.block([[c,sn],[-sn,c]]))
    fwd=np.stack(mats).reshape(pairs,2,2*inner,2*inner)
    inv=np.swapaxes(fwd,-1,-2)/length
    r=np.arange(half)
    th=np.pi*(r[None,:]*(2*np.arange(pairs)[:,None]+1))/RADIX
    coef=np.concatenate([np.cos(th),np.sin(th)],axis=1).astype(np.float32)
    return fwd.astype(ml_dtypes.bfloat16),inv.astype(ml_dtypes.bfloat16),coef

def split_rows(x_ref,coef_ref,p,z_ref,inner):
    step=16
    @pl.loop(0,inner//step)
    def _(i):
        lo=pl.multiple_of(i*step,step)
        rows=pl.ds(lo,step); low=pl.ds(pl.multiple_of(inner+i*step,step),step)
        xs=[x_ref[r,rows,:].astype(F32) for r in range(8)]
        c=[coef_ref[p,r] for r in range(8)]; s=[coef_ref[p,8+r] for r in range(8)]
        ce=xs[0]+c[2]*xs[2]+c[4]*xs[4]+c[6]*xs[6]
        co=c[1]*xs[1]+c[3]*xs[3]+c[5]*xs[5]+c[7]*xs[7]
        se=s[2]*xs[2]+s[4]*xs[4]+s[6]*xs[6]
        so=s[1]*xs[1]+s[3]*xs[3]+s[5]*xs[5]+s[7]*xs[7]
        z_ref[0,rows,:]=(ce+co).astype(BF)
        z_ref[1,rows,:]=(ce-co).astype(BF)
        z_ref[0,low,:]=(-(se+so)).astype(BF)
        z_ref[1,low,:]=(se-so).astype(BF)

def join_rows(w_ref,coef_ref,p,acc_ref,inner,lanes):
    step=16
    @pl.loop(0,inner//step)
    def _(i):
        lo=pl.multiple_of(i*step,step)
        rows=pl.ds(lo,step); low=pl.ds(pl.multiple_of(inner+i*step,step),step)
        r0=w_ref[0,rows,lanes]; r1=w_ref[1,rows,lanes]
        i0=w_ref[0,low,lanes]; i1=w_ref[1,low,lanes]
        rs=(r0+r1,r0-r1); im=(i0-i1,i0+i1)
        for r in range(8):
            if r==0: term=rs[0]
            else: term=coef_ref[p,r]*rs[r%2]-coef_ref[p,8+r]*im[r%2]
            acc_ref[r,rows,:]=jnp.where(p==0,0.0,acc_ref[r,rows,:])+term

def spec_kernel(coef_ref,x_ref,f_ref,o_ref,z_ref):
    p=pl.program_id(0); inner=x_ref.shape[1]
    split_rows(x_ref,coef_ref,p,z_ref,inner)
    for j in range(2):
        o_ref[0,j]=jnp.dot(f_ref[0,j],z_ref[j],preferred_element_type=F32).astype(o_ref.dtype)

def conv_kernel(coef_ref,x_ref,k_ref,f_ref,b_ref,s_ref,y_ref,z_ref,w_ref,acc_ref):
    p=pl.program_id(0); inner=x_ref.shape[1]
    split_rows(x_ref,coef_ref,p,z_ref,inner)
    for j in range(2):
        w_ref[j]=jnp.dot(f_ref[0,j],z_ref[j],preferred_element_type=F32)
    step=16
    for j in range(2):
        @pl.loop(0,inner//step)
        def _(i):
            rows=pl.ds(pl.multiple_of(i*step,step),step); low=pl.ds(pl.multiple_of(inner+i*step,step),step)
            xr=w_ref[j,rows,:]; xi=w_ref[j,low,:]
            kr=k_ref[0,j,rows,:].astype(F32); ki=k_ref[0,j,low,:].astype(F32)
            s_ref[0,j,rows,:]=xr.astype(BF); s_ref[0,j,low,:]=xi.astype(BF)
            z_ref[j,rows,:]=(xr*kr-xi*ki).astype(BF)
            z_ref[j,low,:]=(xr*ki+xi*kr).astype(BF)
    for j in range(2):
        w_ref[j]=jnp.dot(b_ref[0,j],z_ref[j],preferred_element_type=F32)
    join_rows(w_ref,coef_ref,p,acc_ref,inner,slice(None))
    @pl.when(p==pl.num_programs(0)-1)
    def _():
        @pl.loop(0,inner//step)
        def _(i):
            rows=pl.ds(pl.multiple_of(i*step,step),step)
            for r in range(8):
                y_ref[r,rows,:]=acc_ref[r,rows,:].astype(y_ref.dtype)

def back_kernel(coef_ref,g_ref,k_ref,s_ref,f_ref,b_ref,y_ref,kg_ref,z_ref,w_ref,q_ref,v_ref,acc_ref):
    p=pl.program_id(0); inner=g_ref.shape[1]; chans=g_ref.shape[2]
    split_rows(g_ref,coef_ref,p,z_ref,inner)
    for j in range(2):
        w_ref[j]=jnp.dot(f_ref[0,j],z_ref[j],preferred_element_type=F32)
    step=16
    for j in range(2):
        @pl.loop(0,inner//step)
        def _(i):
            rows=pl.ds(pl.multiple_of(i*step,step),step); low=pl.ds(pl.multiple_of(inner+i*step,step),step)
            gr=w_ref[j,rows,:]; gi=w_ref[j,low,:]
            kr=k_ref[0,j,rows,:].astype(F32); ki=k_ref[0,j,low,:].astype(F32)
            q_ref[j,rows,0:chans]=(gr*kr+gi*ki).astype(BF)
            q_ref[j,low,0:chans]=(gi*kr-gr*ki).astype(BF)
            kr=s_ref[0,j,rows,:].astype(F32); ki=s_ref[0,j,low,:].astype(F32)
            q_ref[j,rows,chans:2*chans]=(gr*kr+gi*ki).astype(BF)
            q_ref[j,low,chans:2*chans]=(gi*kr-gr*ki).astype(BF)
    for j in range(2):
        v_ref[j]=jnp.dot(b_ref[0,j],q_ref[j],preferred_element_type=F32)
    join_rows(v_ref,coef_ref,p,acc_ref,inner,slice(0,chans))
    join_rows(v_ref,coef_ref,p,kg_ref,inner,slice(chans,2*chans))
    @pl.when(p==pl.num_programs(0)-1)
    def _():
        @pl.loop(0,inner//step)
        def _(i):
            rows=pl.ds(pl.multiple_of(i*step,step),step)
            for r in range(8):
                y_ref[r,rows,:]=acc_ref[r,rows,:].astype(y_ref.dtype)

PAR=pltpu.CompilerParams(vmem_limit_bytes=52<<20)
SM=pl.BlockSpec(memory_space=pltpu.SMEM)
def whole(shape): return pl.BlockSpec(shape,lambda p:(0,)*len(shape))
def step_of(shape): return pl.BlockSpec((1,)+shape,lambda p:(p,)+(0,)*len(shape))

def spectrum(x,tables):
    fwd,inv,coef=tables
    length,ch=x.shape; inner=2*length//RADIX
    return pl.pallas_call(spec_kernel,grid=(RADIX//4,),
        in_specs=[SM,whole((8,inner,ch)),step_of((2,2*inner,2*inner))],
        out_specs=step_of((2,2*inner,ch)),
        out_shape=jax.ShapeDtypeStruct((RADIX//4,2,2*inner,ch),F32),
        scratch_shapes=[pltpu.VMEM((2,2*inner,ch),BF)],compiler_params=PAR)(coef,x.reshape(8,inner,ch),fwd)

def long_conv(x,kspec,tables):
    fwd,inv,coef=tables
    length,ch=x.shape; inner=2*length//RADIX
    s,y=pl.pallas_call(conv_kernel,grid=(RADIX//4,),
        in_specs=[SM,whole((8,inner,ch)),step_of((2,2*inner,ch)),step_of((2,2*inner,2*inner)),step_of((2,2*inner,2*inner))],
        out_specs=[step_of((2,2*inner,ch)),whole((8,inner,ch))],
        out_shape=[jax.ShapeDtypeStruct((RADIX//4,2,2*inner,ch),BF),jax.ShapeDtypeStruct((8,inner,ch),F32)],
        scratch_shapes=[pltpu.VMEM((2,2*inner,ch),BF),pltpu.VMEM((2,2*inner,ch),F32),pltpu.VMEM((8,inner,ch),F32)],compiler_params=PAR)(coef,x.reshape(8,inner,ch),kspec,fwd,inv)
    return s,y.reshape(length,ch)

def long_back(g,kspec,sspec,tables):
    fwd,inv,coef=tables
    length,ch=g.shape; inner=2*length//RADIX
    y,kg=pl.pallas_call(back_kernel,grid=(RADIX//4,),
        in_specs=[SM,whole((8,inner,ch)),step_of((2,2*inner,ch)),step_of((2,2*inner,ch)),step_of((2,2*inner,2*inner)),step_of((2,2*inner,2*inner))],
        out_specs=[whole((8,inner,ch)),whole((8,inner,ch))],
        out_shape=[jax.ShapeDtypeStruct((8,inner,ch),F32),jax.ShapeDtypeStruct((8,inner,ch),F32)],
        scratch_shapes=[pltpu.VMEM((2,2*inner,ch),BF),pltpu.VMEM((2,2*inner,ch),F32),pltpu.VMEM((2,2*inner,2*ch),BF),pltpu.VMEM((2,2*inner,2*ch),F32),pltpu.VMEM((8,inner,ch),F32)],compiler_params=PAR)(coef,g.reshape(8,inner,ch),kspec,sspec,fwd,inv)
    return y.reshape(length,ch),kg.reshape(length,ch)

def ff_kernel(x_ref,g_ref,wu_ref,wd_ref,bu_ref,down_ref,gsec_ref,dwu_ref,dwd_ref,dbu_ref,a_ref,gu_ref):
    f=pl.program_id(0); rows=x_ref.shape[0]; step=256 if rows%256==0 else rows
    wu=wu_ref[...]; wd=wd_ref[0]
    total=jnp.zeros(dbu_ref.shape[1:],F32)
    for r in range(rows//step):
        at=pl.ds(r*step,step)
        up=lax.dot_general(x_ref[at,:],wu,(((1,),(1,)),((),())),preferred_element_type=F32)+bu_ref[0]
        ga=jnp.dot(g_ref[at,:],wd,preferred_element_type=F32)
        sq=up*up
        th=jnp.tanh(up*(GELU_A+(GELU_A*GELU_B)*sq))
        half_one=0.5+0.5*th
        a_ref[at,:]=(up*half_one).astype(BF)
        slope=half_one+(up*half_one*(1.0-th))*(GELU_A+(3.0*GELU_A*GELU_B)*sq)
        gu=ga*slope
        total=total+jnp.sum(gu,axis=0,keepdims=True)
        gu_ref[at,:]=gu.astype(BF)
        down=lax.dot_general(a_ref[at,:],wd,(((1,),(1,)),((),())),preferred_element_type=F32)
        gsec=jnp.dot(gu_ref[at,:],wu,preferred_element_type=F32)
        @pl.when(f==0)
        def _():
            down_ref[at,:]=down
            gsec_ref[at,:]=gsec
        @pl.when(f>0)
        def _():
            down_ref[at,:]+=down
            gsec_ref[at,:]+=gsec
    dbu_ref[0]=total
    dwu_ref[...]=lax.dot_general(gu_ref[...],x_ref[...],(((0,),(0,)),((),())),preferred_element_type=F32).astype(BF)
    dwd_ref[...]=lax.dot_general(g_ref[...],a_ref[...],(((0,),(0,)),((),())),preferred_element_type=F32).astype(BF)

GELU_A=0.7978845608
GELU_B=0.044715

def feed_forward(x,g,wu,wd,bu):
    rows,width=x.shape; hid=wu.shape[0]; blk=width
    n=hid//blk
    return pl.pallas_call(ff_kernel,grid=(n,),
        in_specs=[whole((rows,width)),whole((rows,width)),pl.BlockSpec((blk,width),lambda f:(f,0)),pl.BlockSpec((1,width,blk),lambda f:(f,0,0)),pl.BlockSpec((1,1,blk),lambda f:(f,0,0))],
        out_specs=[whole((rows,width)),whole((rows,width)),pl.BlockSpec((blk,width),lambda f:(f,0)),pl.BlockSpec((width,blk),lambda f:(0,f)),pl.BlockSpec((1,1,blk),lambda f:(f,0,0))],
        out_shape=[jax.ShapeDtypeStruct((rows,width),F32),jax.ShapeDtypeStruct((rows,width),F32),jax.ShapeDtypeStruct((hid,width),BF),jax.ShapeDtypeStruct((width,hid),BF),jax.ShapeDtypeStruct((n,1,blk),F32)],
        scratch_shapes=[pltpu.VMEM((rows,blk),BF),pltpu.VMEM((rows,blk),BF)],
        cost_estimate=pl.CostEstimate(flops=12*rows*width*hid,bytes_accessed=8*width*hid+12*rows*width,transcendentals=rows*hid),
        compiler_params=PAR)(x,g,wu,wd,bu.reshape(n,1,blk))

def tail_kernel(p_ref,gg_ref,jo_ref,cb_ref,gj_ref,af_ref,mk_ref,tap_ref,cbias_ref,skip_ref,
                gp_ref,sums_ref,pw_ref,gc_ref):
    b=pl.program_id(0); local=gg_ref.shape[1]; width=gg_ref.shape[2]; wide=3*width
    step=64 if local%64==0 else local; lanes=128
    @pl.when(b==0)
    def _():
        sums_ref[...]=jnp.zeros_like(sums_ref)
    @pl.loop(0,width//lanes)
    def _(j):
        def cols(s): return pl.ds(pl.multiple_of(s*width+j*lanes,lanes),lanes)
        c0=cols(0)
        for s in range(3):
            for r in range(-1,local//step):
                if r<0: pw_ref[s,0:16,:]=p_ref[0,0:16,cols(s)].astype(F32)
                else: pw_ref[s,16+r*step:16+(r+1)*step,:]=p_ref[0,16+r*step:16+(r+1)*step,cols(s)].astype(F32)
        tap=[[tap_ref[k:k+1,cols(s)] for k in range(3)] for s in range(3)]
        cbias=[cbias_ref[0:1,cols(s)] for s in range(3)]
        skip=skip_ref[0:1,c0]
        acc=[[jnp.zeros((8,lanes),F32) for _ in range(5)] for s in range(3)]
        def fold(v): return jnp.sum(v.reshape(-1,8,lanes),axis=0)
        for r in range(local//step):
            lo=r*step
            at=pl.ds(lo,step)
            sh=[[pw_ref[s,14+lo+k:14+lo+k+step,:] for k in range(3)] for s in range(3)]
            gate=[None]+[cbias[s]+tap[s][0]*sh[s][0]+tap[s][1]*sh[s][1]+tap[s][2]*sh[s][2] for s in (1,2)]
            gg=gg_ref[0,at,c0]
            gs=mk_ref[0,at,:]*(cb_ref[0,at,c0].astype(F32)+skip*gj_ref[0,at,c0].astype(F32))
            gc=[gg*jo_ref[0,at,c0].astype(F32),gs*gate[2],gs*gate[1]]
            for s in range(3):
                gc_ref[s,at,:]=gc[s]
                acc[s][0]=acc[s][0]+fold(gc[s])
                for k in range(3):
                    acc[s][1+k]=acc[s][1+k]+fold(gc[s]*sh[s][k])
        for s in range(3):
            gc_ref[s,local:local+8,:]=af_ref[0,:,cols(s)]
        for r in range(local//step):
            lo=r*step
            at=pl.ds(lo,step)
            mk=mk_ref[0,at,:]
            for s in range(3):
                gp=mk*(tap[s][2]*gc_ref[s,at,:]+tap[s][1]*gc_ref[s,lo+1:lo+1+step,:]+tap[s][0]*gc_ref[s,lo+2:lo+2+step,:])
                acc[s][4]=acc[s][4]+fold(gp)
                gp_ref[0,at,cols(s)]=gp.astype(BF)
        for s in range(3):
            for q in range(5):
                sums_ref[q:q+1,cols(s)]+=jnp.sum(acc[s][q],axis=0,keepdims=True)

def tail_back(p,gg,jo,cb,gj,af,mk,taps,cbias,skip):
    blocks,local,width=gg.shape; wide=3*width
    def blk(rows,cols): return pl.BlockSpec((1,rows,cols),lambda b:(b,0,0))
    return pl.pallas_call(tail_kernel,grid=(blocks,),
        in_specs=[blk(local+16,wide),blk(local,width),blk(local,width),blk(local,width),blk(local,width),blk(8,wide),blk(local,1),whole((3,wide)),whole((1,wide)),whole((1,width))],
        out_specs=[blk(local,wide),whole((8,wide))],
        out_shape=[jax.ShapeDtypeStruct((blocks,local,wide),BF),jax.ShapeDtypeStruct((8,wide),F32)],
        scratch_shapes=[pltpu.VMEM((3,local+16,128),F32),pltpu.VMEM((3,local+8,128),F32)],
        compiler_params=PAR)(p,gg,jo,cb,gj,af,mk,taps,cbias,skip)

def product(left, right):
    return jnp.dot(left, right, precision=lax.Precision.HIGHEST, preferred_element_type=jnp.float32)

def gelu_tanh(values):
    return jax.nn.gelu(values, approximate=True)

def filter_hidden(
    features,
    filter_entry_coefficients,
    filter_entry_offset,
    filter_second_coefficients,
    filter_second_offset,
    filter_third_coefficients,
    filter_third_offset,
    periodic_frequency,
):
    first = jnp.sin(
        periodic_frequency * (product(features, filter_entry_coefficients) + filter_entry_offset)
    )
    middle = jnp.sin(
        periodic_frequency * (product(first, filter_second_coefficients) + filter_second_offset)
    )
    return jnp.sin(
        periodic_frequency * (product(middle, filter_third_coefficients) + filter_third_offset)
    )

def modulation(length, model_width, offset, channels):
    standardized_values = jnp.arange(length).astype(jnp.float32) / (length - 1)
    slowest = math.log(0.01) / 1.5
    fastest = math.log(0.01) / 0.3
    columns = (offset + jnp.arange(channels)).astype(jnp.float32)
    decays = slowest + (fastest - slowest) * columns / (model_width - 1)
    return jnp.exp(-standardized_values[:, None] * jnp.abs(decays)[None, :]) + 0.05

def position_features(length, emb_width):
    band_count = (emb_width - 1) // 2
    places = np.arange(length, dtype=np.float64)
    band_rates = 0.0001 + (band_count - 1 - 0.0001) * np.arange(band_count) / (band_count - 1)
    phases = (2.0 * math.pi * places / length)[:, None] * band_rates[None, :]
    return np.concatenate(
        [(places / (length - 1))[:, None], np.cos(phases), -np.sin(phases)], axis=1
    ).astype(np.float32)


def swap_bit(value, me, bit, count):
    return lax.ppermute(value, AXES, [(i, i ^ (1 << bit)) for i in range(count)])


def bit_of(me, bit):
    return (me >> bit) & 1


class Gather:
    flight = None

    def __init__(self, value, me, count, order):
        self.held, self.me, self.count, self.order = value, me, count, list(order)
        self.at = 0

    def send(self):
        self.flight = [swap_bit(self.held, self.me, self.order[self.at], self.count)]

    def receive(self, got):
        self.at += 1
        if self.at < len(self.order):
            self.held = jnp.concatenate([self.held, got[0]], axis=0)
        else:
            self.held = place_shards(self.held, got[0], self.me, self.count, self.order)

    @property
    def open(self):
        return self.at < len(self.order)


class Scatter:
    flight = None

    def __init__(self, value, me, count, order, keep):
        self.value, self.me, self.count, self.order, self.keep = value, me, count, list(order), keep
        self.rows, self.columns = value.shape[1:]
        self.left = list(range(len(self.order)))
        self.at = 0

    def send(self):
        bit = self.order[self.at]
        low = 1 << sum(1 for b in self.left if b < bit)
        cut = self.value.reshape(-1, 2, low * self.rows, self.columns)
        mine = bit_of(self.me, bit)
        self.mine = lax.dynamic_index_in_dim(cut, mine, 1, keepdims=False)
        given = lax.dynamic_index_in_dim(cut, 1 - mine, 1, keepdims=False)
        self.flight = [swap_bit(given, self.me, bit, self.count)]
        self.left.remove(bit)

    def receive(self, got):
        self.at += 1
        self.value = self.mine.astype(F32) + got[0].astype(F32)
        if self.open:
            self.value = self.value.astype(self.keep)
        else:
            self.value = self.value.reshape(self.rows, self.columns)

    @property
    def open(self):
        return self.at < len(self.order)


class Swap:
    flight = None

    def __init__(self, value, me, count, bit):
        self.value, self.me, self.count, self.bit = value, me, count, bit
        self.open = True

    def send(self):
        self.flight = [swap_bit(self.value, self.me, self.bit, self.count)]

    def receive(self, got):
        self.value = got[0]
        self.open = False


class Total:
    flight = None

    def __init__(self, value, me, count):
        self.value, self.me, self.count = value, me, count
        bits = list(range(count.bit_length() - 1))
        self.groups = [bits[i : i + 2] for i in range(0, len(bits), 2)]
        self.at = 0

    def send(self):
        group = self.groups[self.at]
        masks = [sum(1 << b for j, b in enumerate(group) if (m >> j) & 1) for m in range(1, 1 << len(group))]
        self.flight = [
            lax.ppermute(self.value, AXES, [(i, i ^ m) for i in range(self.count)]) for m in masks
        ]

    def receive(self, got):
        self.at += 1
        for v in got:
            self.value = self.value + v

    @property
    def open(self):
        return self.at < len(self.groups)


def send(*chains):
    for c in chains:
        if c.open:
            c.send()


def meet(state, *chains):
    chains = [c for c in chains if c.flight]
    sizes = [len(c.flight) for c in chains]
    tied = lax.optimization_barrier(tuple(state) + tuple(v for c in chains for v in c.flight))
    at = len(state)
    for c, n in zip(chains, sizes):
        c.receive(tied[at : at + n])
        c.flight = None
        at += n
    return tied[: len(state)]


def drain(*chains):
    meet((), *chains)
    while any(c.open for c in chains):
        send(*chains)
        meet((), *chains)


def place_shards(near, other, me, count, order):
    rows = near.shape[0] * 2 // count
    half = count // 2

    def spread(i):
        return sum(((i >> p) & 1) << bit for p, bit in enumerate(order[:-1]))

    def kernel(me_ref, near_ref, other_ref, out_ref):
        own = me_ref[0]
        for i in range(half):
            out_ref[jnp.bitwise_xor(own, spread(i))] = near_ref[i]
            out_ref[jnp.bitwise_xor(own, spread(i) | (1 << order[-1]))] = other_ref[i]

    vmem = pl.BlockSpec(memory_space=pltpu.VMEM)
    shape = (count, rows) + near.shape[1:]
    return pl.pallas_call(
        kernel,
        in_specs=[SM, vmem, vmem],
        out_specs=vmem,
        out_shape=jax.ShapeDtypeStruct(shape, near.dtype),
        compiler_params=PAR,
    )(
        me.reshape(1).astype(jnp.int32),
        near.reshape((half, rows) + near.shape[1:]),
        other.reshape((half, rows) + near.shape[1:]),
    )


def orders_of(count):
    bits = count.bit_length() - 1
    first = list(range(bits))
    second = list(range(bits))
    second[1], second[2] = second[2], second[1]
    return first, second


def normalise(values):
    centre = values - jnp.mean(values, axis=-1, keepdims=True)
    spread = jnp.mean(centre * centre, axis=-1, keepdims=True)
    rstd = lax.rsqrt(spread + 1e-05)
    return centre * rstd, rstd


def normalise_back(unit, rstd, incoming):
    return rstd * (
        incoming
        - jnp.mean(incoming, axis=-1, keepdims=True)
        - unit * jnp.mean(incoming * unit, axis=-1, keepdims=True)
    )


def dot_nt(left, right):
    return lax.dot_general(left, right, (((1,), (1,)), ((), ())), preferred_element_type=F32)


def dot_nn(left, right):
    return lax.dot_general(left, right, (((1,), (0,)), ((), ())), preferred_element_type=F32)


def dot_tn(left, right):
    return lax.dot_general(left, right, (((0,), (0,)), ((), ())), preferred_element_type=F32)


def per_device(
    block_input,
    slot_spans,
    output_adjoint,
    opening_scale_factor,
    opening_offset_vector,
    intake_coefficients,
    intake_offset,
    brief_filter_coefficients,
    brief_filter_offset,
    direct_path_factor,
    filter_final_coefficients,
    mixer_output_coefficients,
    mixer_output_offset,
    closing_scale_factor,
    closing_offset_vector,
    expand_coefficients,
    expand_offset,
    contract_coefficients,
    contract_offset,
    filter_entry_coefficients,
    filter_entry_offset,
    filter_second_coefficients,
    filter_second_offset,
    filter_third_coefficients,
    filter_third_offset,
    periodic_frequency,
):
    width = block_input.shape[2]
    local = block_input.shape[1]
    seq_count = lax.axis_size("seq")
    count = lax.axis_size("dp") * seq_count
    seq_index = lax.axis_index("seq")
    me = lax.axis_index("dp") * seq_count + seq_index
    half = seq_count // 2
    group_bits = half.bit_length() - 1
    rank = seq_index % half
    side = seq_index // half
    length = local * seq_count
    channels = width // half
    chan_start = rank * channels
    up, across = orders_of(count)
    down, back = up[::-1], across[::-1]
    tables = tuple(jnp.asarray(t) for t in dft_tables(length))

    vectors = (
        opening_scale_factor,
        opening_offset_vector,
        direct_path_factor,
        mixer_output_offset,
        closing_scale_factor,
        closing_offset_vector,
        contract_offset,
        intake_offset,
        brief_filter_offset,
        brief_filter_coefficients,
        expand_offset,
    )
    middle = width // 2
    far = half.bit_length() - 1
    intake_shard = intake_coefficients.T
    front = Gather(intake_shard[:, :middle], me, count, down)
    rear = Gather(intake_shard[:, middle:], me, count, back)
    final = Gather(filter_final_coefficients.T.astype(F32), me, count, down)
    trade = Swap(
        lax.dynamic_index_in_dim(block_input, 1 - side, 0, keepdims=False), me, count, far
    )
    features = jnp.asarray(position_features(length, filter_entry_coefficients.shape[0]))
    send(front, rear, final)
    later = jnp.concatenate(
        [expand_coefficients.T]
        + [
            contract_coefficients[q * width : (q + 1) * width].T
            for q in range(contract_coefficients.shape[0] // width)
        ]
        + [mixer_output_coefficients.T],
        axis=0,
    )
    later = lax.all_gather(later, AXES, axis=0, tiled=False)
    frequency = periodic_frequency

    def angle(values, weights, offset):
        return product(values, weights) + offset

    p1 = angle(features, filter_entry_coefficients, filter_entry_offset)
    m1 = jnp.sin(frequency * p1)
    (m1,) = meet((m1,), final)
    send(final, trade)
    p2 = angle(m1, filter_second_coefficients, filter_second_offset)
    m2 = jnp.sin(frequency * p2)
    (m2,) = meet((m2,), final, front, rear)
    send(front, rear, final)
    p3 = angle(m2, filter_third_coefficients, filter_third_offset)
    hidden = jnp.sin(frequency * p3)
    (hidden,) = meet((hidden,), final)
    send(final)
    pack = jnp.concatenate([v.reshape(-1) for v in vectors])
    used = pack.size
    pad = -used % 1024
    pack = jnp.concatenate([pack, jnp.zeros((pad,), pack.dtype)]).reshape(8, -1).astype(F32)
    (pack,) = meet((pack,), final, front, rear)
    bundle = Gather(pack, me, count, down)
    send(front, rear, final, bundle)
    shaping = modulation(length, width, chan_start, channels)
    (shaping,) = meet((shaping,), final, bundle)
    drain(final)
    columns = lax.dynamic_slice_in_dim(final.held.reshape(width, -1), chan_start, channels, 0)
    send(bundle)
    filter_kernel = (
        lax.dot_general(
            hidden,
            columns,
            (((1,), (1,)), ((), ())),
            precision=lax.Precision.HIGHEST,
            preferred_element_type=F32,
        )
        * shaping
    )
    (filter_kernel,) = meet((filter_kernel,), front, rear, bundle)
    send(front, rear, bundle)
    kernel_spec = spectrum(filter_kernel, tables)
    (kernel_spec,) = meet((kernel_spec,), bundle, trade)
    send(bundle)
    own_rows = lax.dynamic_index_in_dim(block_input, side, 0, keepdims=False)
    tokens_low = jnp.concatenate([own_rows, trade.value], axis=0)
    (tokens_low,) = meet((tokens_low,), bundle, front, rear)
    send(front, rear, bundle)
    tokens = tokens_low.astype(F32)
    unit_one, rstd_one = normalise(tokens)
    unit_one, rstd_one = meet((unit_one, rstd_one), bundle, front, rear)
    drain(bundle, front, rear)
    pack_full = bundle.held.reshape(count, -1)
    fields = []
    at = 0
    for v in vectors:
        part = pack_full[:, at : at + v.size]
        at += v.size
        if v.ndim == 1:
            fields.append(part.reshape(-1))
        else:
            fields.append(
                part.reshape(count, v.shape[0], -1).transpose(1, 0, 2).reshape(v.shape[0], -1)
            )
    (
        gain_one,
        shift_one,
        skip_gain,
        mix_bias,
        gain_two,
        shift_two,
        down_bias,
        intake_bias,
        conv_bias,
        conv_taps,
        up_bias,
    ) = fields
    intake_t = jnp.concatenate(
        [front.held.reshape(-1, middle), rear.held.reshape(-1, middle)], axis=1
    )
    trade_adj = Swap(
        lax.dynamic_index_in_dim(output_adjoint, 1 - side, 0, keepdims=False), me, count, far
    )
    send(trade_adj)

    own_base = seq_index * local
    far_base = ((1 - side) * half + rank) * local
    places = jnp.concatenate(
        [own_base + jnp.arange(local), far_base + jnp.arange(local)]
    ).astype(jnp.int32)
    span = lax.dynamic_index_in_dim(slot_spans, side, 0, keepdims=False)
    row_mask = ((places >= span[0]) & (places < span[0] + span[1])).astype(F32)[:, None]
    normed_low = (unit_one * gain_one + shift_one).astype(BF)
    projected = row_mask * (dot_nt(normed_low, intake_t) + intake_bias)
    blocks = projected.reshape(2, local, -1)

    def ring(value, by):
        pairs = []
        for i in range(count):
            group, r = divmod(i, half)
            pairs.append((i, group * half + (r + by) % half))
        return lax.ppermute(value, AXES, pairs)

    ends = ring(blocks[:, local - 2 :], 1)
    wrapped = jnp.stack(
        [jnp.where(side == 1, ends[1], 0.0), jnp.where(side == 0, ends[0], 0.0)]
    )
    before = jnp.where(rank == 0, wrapped, ends)
    extended = jnp.concatenate([before, blocks], axis=1)
    rows = 2 * local

    def shifted(by):
        return extended[:, by : by + local].reshape(rows, -1)

    conv_out = (
        conv_bias
        + conv_taps[0] * shifted(0)
        + conv_taps[1] * shifted(1)
        + conv_taps[2] * shifted(2)
    )
    outer_gate = conv_out[:, :width]
    inner_gate = conv_out[:, width : 2 * width]
    values = conv_out[:, 2 * width :]
    signal = (row_mask * inner_gate * values).astype(BF)

    def traded(near, give):
        got = [near]
        for k in range(1, half):
            got.append(lax.ppermute(give(k), AXES, [(i, i ^ k) for i in range(count)]))
        if half == 2:
            return jnp.where(rank == 0, got[0], got[1]), jnp.where(rank == 0, got[1], got[0])
        stacked = jnp.take(jnp.stack(got), jnp.arange(half) ^ rank, axis=0)
        return tuple(stacked[k] for k in range(half))

    def to_channels(value):
        def give(k):
            return lax.dynamic_slice_in_dim(value, (rank ^ k) * channels, channels, 1)

        pieces = traded(give(0), give)
        first = [jnp.where(side == 0, p[:local], p[local:]) for p in pieces]
        second = [jnp.where(side == 0, p[local:], p[:local]) for p in pieces]
        return jnp.concatenate(first + second, axis=0)

    def to_rows(value):
        def give(k):
            first = lax.dynamic_slice_in_dim(value, (rank ^ k) * local, local, 0)
            second = lax.dynamic_slice_in_dim(value, (half + (rank ^ k)) * local, local, 0)
            return jnp.concatenate(
                [jnp.where(side == 0, first, second), jnp.where(side == 0, second, first)], axis=0
            )

        return jnp.concatenate(traded(give(0), give), axis=1)

    def blocks_of(value):
        return value.reshape(2, local, -1)

    projected_low_all = jnp.concatenate(
        [jnp.zeros((2, 14, before.shape[2]), BF), before.astype(BF), blocks.astype(BF)], axis=1
    )
    sig_spec, carried_cols = long_conv(to_channels(signal), kernel_spec, tables)
    carried = to_rows(carried_cols.astype(BF)).astype(F32)
    signal_wide = signal.astype(F32)
    joined = carried + skip_gain * signal_wide
    joined_low = joined.astype(BF)
    gated_mix = (joined * outer_gate).astype(BF)
    (gated_mix,) = meet((gated_mix,), trade_adj)
    own_adj = lax.dynamic_index_in_dim(output_adjoint, side, 0, keepdims=False)
    adjoint = jnp.concatenate([own_adj, trade_adj.value], axis=0)
    ff_rows = expand_coefficients.shape[1]
    mix_rows = mixer_output_coefficients.shape[1]
    up_t = later[:, :ff_rows].reshape(-1, width)
    mix_t = later[:, later.shape[1] - mix_rows :].reshape(-1, width)
    folds = contract_coefficients.shape[0] // width
    down_t = (
        later[:, ff_rows : later.shape[1] - mix_rows]
        .reshape(count, folds, -1, width)
        .transpose(1, 0, 2, 3)
        .reshape(folds, width, width)
    )
    residual = tokens + dot_nt(gated_mix, mix_t) + mix_bias
    unit_two, rstd_two = normalise(residual)
    second_low = (unit_two * gain_two + shift_two).astype(BF)
    grad_out = row_mask * adjoint.astype(F32)
    grad_low = grad_out.astype(BF)
    down_proj, grad_second, up_grad, down_grad, up_bias_grad = feed_forward(
        second_low, grad_low, up_t, down_t, up_bias
    )
    up_bias_grad = up_bias_grad.reshape(-1)
    output = (row_mask * (residual + down_proj + down_bias)).astype(BF)

    up_sum = Scatter(up_grad.reshape(count, -1, width), me, count, across, BF)
    down_sum = Scatter(down_grad.reshape(count, -1, down_grad.shape[1]), me, count, up, BF)
    send(up_sum, down_sum)
    down_bias_grad = jnp.sum(grad_out, axis=0)
    gain_two_grad = jnp.sum(grad_second * unit_two, axis=0)
    shift_two_grad = jnp.sum(grad_second, axis=0)
    grad_residual = grad_out + normalise_back(unit_two, rstd_two, grad_second * gain_two)
    mix_bias_grad = jnp.sum(grad_residual, axis=0)
    resid_low = grad_residual.astype(BF)
    mix_grad = dot_tn(resid_low, gated_mix).astype(BF)
    mix_sum = Scatter(mix_grad.reshape(count, -1, width), me, count, up, BF)
    grad_gated = dot_nn(resid_low, mix_t)
    grad_joined = grad_gated * outer_gate
    grad_joined_low = grad_joined.astype(BF)
    skip_grad = jnp.sum(grad_joined * signal_wide, axis=0)
    (grad_joined_low,) = meet((grad_joined_low,), up_sum, down_sum)
    send(mix_sum, up_sum, down_sum)
    conv_back_cols, kernel_grad = long_back(
        to_channels(grad_joined_low), kernel_spec, sig_spec, tables
    )
    conv_back_cols, kernel_grad = meet((conv_back_cols, kernel_grad), mix_sum, up_sum, down_sum)
    send(mix_sum, up_sum, down_sum)
    trade_out = Swap(output[local:], me, count, far)
    conv_back_low = to_rows(conv_back_cols.astype(BF))
    conv_back = conv_back_low.astype(F32)
    first = blocks_of(grad_gated)[:, :2]
    first_signal = blocks_of(row_mask)[:, :2] * (
        blocks_of(conv_back)[:, :2] + skip_gain * blocks_of(grad_joined_low)[:, :2].astype(F32)
    )
    starts = ring(
        jnp.concatenate(
            [
                first * blocks_of(joined_low)[:, :2].astype(F32),
                first_signal * blocks_of(values)[:, :2],
                first_signal * blocks_of(inner_gate)[:, :2],
            ],
            axis=2,
        ),
        -1,
    )
    wrapped_after = jnp.stack(
        [jnp.where(side == 0, starts[1], 0.0), jnp.where(side == 1, starts[0], 0.0)]
    )
    after = jnp.where(rank == half - 1, wrapped_after, starts)
    after = jnp.concatenate([after, jnp.zeros((2, 6, after.shape[2]), F32)], axis=1)
    grad_projected, sums = tail_back(
        projected_low_all,
        blocks_of(grad_gated),
        blocks_of(joined_low),
        blocks_of(conv_back_low),
        blocks_of(grad_joined_low),
        after,
        blocks_of(row_mask),
        conv_taps,
        conv_bias.reshape(1, -1),
        skip_gain.reshape(1, -1),
    )
    conv_bias_grad = sums[0]
    taps_grad = sums[1:4]
    intake_bias_grad = sums[4]
    projected_low = grad_projected.reshape(rows, -1)
    (projected_low,) = meet((projected_low,), mix_sum, up_sum, down_sum)
    send(mix_sum, up_sum, down_sum)
    intake_grad = dot_tn(projected_low, normed_low).astype(BF).reshape(count, -1, width)
    (intake_grad,) = meet((intake_grad,), mix_sum, up_sum, down_sum)
    front_sum = Scatter(intake_grad[:, :, :middle], me, count, up, BF)
    rear_sum = Scatter(intake_grad[:, :, middle:], me, count, across, BF)
    send(mix_sum, up_sum, down_sum, front_sum, rear_sum)
    grad_normed = dot_nn(projected_low, intake_t)
    gain_one_grad = jnp.sum(grad_normed * unit_one, axis=0)
    shift_one_grad = jnp.sum(grad_normed, axis=0)
    tokens_grad = (
        grad_residual + normalise_back(unit_one, rstd_one, grad_normed * gain_one)
    ).astype(BF)
    (tokens_grad,) = meet((tokens_grad,), mix_sum, up_sum, down_sum, front_sum, rear_sum)
    trade_tokens = Swap(tokens_grad[local:], me, count, far)
    send(mix_sum, front_sum, rear_sum, trade_out)

    shaped_grad = kernel_grad * shaping
    (shaped_grad,) = meet((shaped_grad,), front_sum, rear_sum, mix_sum)
    send(front_sum, rear_sum, trade_tokens)
    column_grad = lax.dot_general(
        shaped_grad,
        hidden,
        (((0,), (0,)), ((), ())),
        precision=lax.Precision.HIGHEST,
        preferred_element_type=F32,
    )
    hidden_grad = product(shaped_grad, columns)
    filter_full = lax.dynamic_update_slice_in_dim(
        jnp.zeros((width, hidden.shape[1]), F32), column_grad, chan_start, 0
    )

    vector_grads = (
        gain_one_grad,
        shift_one_grad,
        skip_grad,
        mix_bias_grad,
        gain_two_grad,
        shift_two_grad,
        down_bias_grad,
        intake_bias_grad,
        conv_bias_grad,
        taps_grad,
        up_bias_grad,
    )
    pieces = []
    for g in vector_grads:
        if g.ndim == 1:
            pieces.append(g.reshape(count, -1))
        else:
            pieces.append(
                g.reshape(g.shape[0], count, -1).transpose(1, 0, 2).reshape(count, -1)
            )
    packed = jnp.concatenate(pieces + [jnp.zeros((count, pad), F32)], axis=1)
    bundle_sum = Scatter(packed.reshape(count, 8, -1), me, count, up, F32)
    final_sum = Scatter(filter_full.reshape(count, -1, hidden.shape[1]), me, count, up, F32)
    send(bundle_sum, final_sum)

    def layer_back(grad, p, inputs, weights):
        turned = grad * jnp.cos(frequency * p)
        grad_p = turned * frequency
        rate = jnp.sum(turned * p, axis=0)
        return product(inputs.T, grad_p), jnp.sum(grad_p, axis=0), rate, product(grad_p, weights.T)

    third, third_bias, rate_3, grad_2 = layer_back(
        hidden_grad, p3, m2, filter_third_coefficients
    )
    (grad_2,) = meet((grad_2,), front_sum, rear_sum, bundle_sum, final_sum, trade_out)
    send(front_sum, rear_sum, bundle_sum, final_sum)
    second, second_bias, rate_2, grad_1 = layer_back(grad_2, p2, m1, filter_second_coefficients)
    (grad_1,) = meet((grad_1,), front_sum, rear_sum, bundle_sum, final_sum)
    send(front_sum, rear_sum, bundle_sum, final_sum)
    entry, entry_bias, rate_1, _ = layer_back(
        grad_1, p1, features, filter_entry_coefficients
    )
    net_grads = (
        entry,
        entry_bias,
        second,
        second_bias,
        third,
        third_bias,
        rate_1 + rate_2 + rate_3,
    )
    net_flat = jnp.concatenate([g.reshape(-1) for g in net_grads])
    net_sum = Total(net_flat, me, count)
    meet((net_flat,), front_sum, rear_sum, bundle_sum, final_sum, trade_tokens)
    drain(bundle_sum, final_sum, net_sum, front_sum, rear_sum, mix_sum, up_sum, down_sum)
    summed = bundle_sum.value.reshape(-1)
    small = []
    at = 0
    for v in vectors:
        small.append(summed[at : at + v.size].reshape(v.shape))
        at += v.size
    net_out = []
    at = 0
    for g in net_grads:
        net_out.append(net_sum.value[at : at + g.size].reshape(g.shape))
        at += g.size
    intake_shard_grad = jnp.concatenate([front_sum.value, rear_sum.value], axis=1)

    def at_home(near, far_part):
        return jnp.where(side == 0, jnp.stack([near, far_part]), jnp.stack([far_part, near]))

    output_home = at_home(output[:local], trade_out.value)
    tokens_home = at_home(tokens_grad[:local], trade_tokens.value)
    return (
        output_home,
        tokens_home,
        small[0],
        small[1],
        intake_shard_grad.T,
        small[7],
        small[9],
        small[8],
        small[2],
        final_sum.value.T,
        mix_sum.value.T,
        small[3],
        small[4],
        small[5],
        up_sum.value.T,
        small[10],
        down_sum.value.T,
        small[6],
    ) + tuple(net_out)

def solution(mesh):
    in_specs = (
        P("dp", "seq", None),
        P("dp", None),
        P("dp", "seq", None),
        P(("dp", "seq")),
        P(("dp", "seq")),
        P(None, ("dp", "seq")),
        P(("dp", "seq")),
        P(None, ("dp", "seq")),
        P(("dp", "seq")),
        P(("dp", "seq")),
        P(None, ("dp", "seq")),
        P(None, ("dp", "seq")),
        P(("dp", "seq")),
        P(("dp", "seq")),
        P(("dp", "seq")),
        P(None, ("dp", "seq")),
        P(("dp", "seq")),
        P(None, ("dp", "seq")),
        P(("dp", "seq")),
        P(),
        P(),
        P(),
        P(),
        P(),
        P(),
        P(),
    )
    out_specs = (
        P("dp", "seq", None),
        P("dp", "seq", None),
        P(("dp", "seq")),
        P(("dp", "seq")),
        P(None, ("dp", "seq")),
        P(("dp", "seq")),
        P(None, ("dp", "seq")),
        P(("dp", "seq")),
        P(("dp", "seq")),
        P(None, ("dp", "seq")),
        P(None, ("dp", "seq")),
        P(("dp", "seq")),
        P(("dp", "seq")),
        P(("dp", "seq")),
        P(None, ("dp", "seq")),
        P(("dp", "seq")),
        P(None, ("dp", "seq")),
        P(("dp", "seq")),
        P(),
        P(),
        P(),
        P(),
        P(),
        P(),
        P(),
    )
    return jax.shard_map(
        per_device, mesh=mesh, in_specs=in_specs, out_specs=out_specs, check_vma=False
    )
```

```python
import math

import jax
import jax.numpy as jnp
import ml_dtypes
import numpy as np
from jax import lax
from jax.experimental import pallas as pl
from jax.experimental.pallas import tpu as pltpu
from jax.sharding import PartitionSpec as P

AXES = ("dp", "seq")

F32=jnp.float32; BF=jnp.bfloat16
RADIX=16

def dft_tables(length):
    padded = 2*length
    inner = padded//RADIX
    pairs = RADIX//4
    half = RADIX//2
    m = np.arange(inner)
    mats=[]
    for p in range(pairs):
        for s in (p, half-1-p):
            k2 = 2*(RADIX*m+s)+1
            ang = np.pi*((k2[:,None]*m[None,:])%(2*padded))/padded
            c,sn=np.cos(ang),np.sin(ang)
            mats.append(np.block([[c,sn],[-sn,c]]))
    fwd=np.stack(mats).reshape(pairs,2,2*inner,2*inner)
    inv=np.swapaxes(fwd,-1,-2)/length
    r=np.arange(half)
    th=np.pi*(r[None,:]*(2*np.arange(pairs)[:,None]+1))/RADIX
    coef=np.concatenate([np.cos(th),np.sin(th)],axis=1).astype(np.float32)
    return fwd.astype(ml_dtypes.bfloat16),inv.astype(ml_dtypes.bfloat16),coef

def split_rows(x_ref,coef_ref,p,z_ref,inner):
    step=16
    @pl.loop(0,inner//step)
    def _(i):
        lo=pl.multiple_of(i*step,step)
        rows=pl.ds(lo,step); low=pl.ds(pl.multiple_of(inner+i*step,step),step)
        xs=[x_ref[r,rows,:].astype(F32) for r in range(8)]
        c=[coef_ref[p,r] for r in range(8)]; s=[coef_ref[p,8+r] for r in range(8)]
        ce=xs[0]+c[2]*xs[2]+c[4]*xs[4]+c[6]*xs[6]
        co=c[1]*xs[1]+c[3]*xs[3]+c[5]*xs[5]+c[7]*xs[7]
        se=s[2]*xs[2]+s[4]*xs[4]+s[6]*xs[6]
        so=s[1]*xs[1]+s[3]*xs[3]+s[5]*xs[5]+s[7]*xs[7]
        z_ref[0,rows,:]=(ce+co).astype(BF)
        z_ref[1,rows,:]=(ce-co).astype(BF)
        z_ref[0,low,:]=(-(se+so)).astype(BF)
        z_ref[1,low,:]=(se-so).astype(BF)

def join_rows(w_ref,coef_ref,p,acc_ref,inner,lanes):
    step=16
    @pl.loop(0,inner//step)
    def _(i):
        lo=pl.multiple_of(i*step,step)
        rows=pl.ds(lo,step); low=pl.ds(pl.multiple_of(inner+i*step,step),step)
        r0=w_ref[0,rows,lanes]; r1=w_ref[1,rows,lanes]
        i0=w_ref[0,low,lanes]; i1=w_ref[1,low,lanes]
        rs=(r0+r1,r0-r1); im=(i0-i1,i0+i1)
        for r in range(8):
            if r==0: term=rs[0]
            else: term=coef_ref[p,r]*rs[r%2]-coef_ref[p,8+r]*im[r%2]
            acc_ref[r,rows,:]=jnp.where(p==0,0.0,acc_ref[r,rows,:])+term

def spec_kernel(coef_ref,x_ref,f_ref,o_ref,z_ref):
    p=pl.program_id(0); inner=x_ref.shape[1]
    split_rows(x_ref,coef_ref,p,z_ref,inner)
    for j in range(2):
        o_ref[0,j]=jnp.dot(f_ref[0,j],z_ref[j],preferred_element_type=F32).astype(o_ref.dtype)

def conv_kernel(coef_ref,x_ref,k_ref,f_ref,b_ref,s_ref,y_ref,z_ref,w_ref,acc_ref):
    p=pl.program_id(0); inner=x_ref.shape[1]
    split_rows(x_ref,coef_ref,p,z_ref,inner)
    for j in range(2):
        w_ref[j]=jnp.dot(f_ref[0,j],z_ref[j],preferred_element_type=F32)
    step=16
    for j in range(2):
        @pl.loop(0,inner//step)
        def _(i):
            rows=pl.ds(pl.multiple_of(i*step,step),step); low=pl.ds(pl.multiple_of(inner+i*step,step),step)
            xr=w_ref[j,rows,:]; xi=w_ref[j,low,:]
            kr=k_ref[0,j,rows,:].astype(F32); ki=k_ref[0,j,low,:].astype(F32)
            s_ref[0,j,rows,:]=xr.astype(BF); s_ref[0,j,low,:]=xi.astype(BF)
            z_ref[j,rows,:]=(xr*kr-xi*ki).astype(BF)
            z_ref[j,low,:]=(xr*ki+xi*kr).astype(BF)
    for j in range(2):
        w_ref[j]=jnp.dot(b_ref[0,j],z_ref[j],preferred_element_type=F32)
    join_rows(w_ref,coef_ref,p,acc_ref,inner,slice(None))
    @pl.when(p==pl.num_programs(0)-1)
    def _():
        @pl.loop(0,inner//step)
        def _(i):
            rows=pl.ds(pl.multiple_of(i*step,step),step)
            for r in range(8):
                y_ref[r,rows,:]=acc_ref[r,rows,:].astype(y_ref.dtype)

def back_kernel(coef_ref,g_ref,k_ref,s_ref,f_ref,b_ref,y_ref,kg_ref,z_ref,w_ref,q_ref,v_ref,acc_ref):
    p=pl.program_id(0); inner=g_ref.shape[1]; chans=g_ref.shape[2]
    split_rows(g_ref,coef_ref,p,z_ref,inner)
    for j in range(2):
        w_ref[j]=jnp.dot(f_ref[0,j],z_ref[j],preferred_element_type=F32)
    step=16
    for j in range(2):
        @pl.loop(0,inner//step)
        def _(i):
            rows=pl.ds(pl.multiple_of(i*step,step),step); low=pl.ds(pl.multiple_of(inner+i*step,step),step)
            gr=w_ref[j,rows,:]; gi=w_ref[j,low,:]
            kr=k_ref[0,j,rows,:].astype(F32); ki=k_ref[0,j,low,:].astype(F32)
            q_ref[j,rows,0:chans]=(gr*kr+gi*ki).astype(BF)
            q_ref[j,low,0:chans]=(gi*kr-gr*ki).astype(BF)
            kr=s_ref[0,j,rows,:].astype(F32); ki=s_ref[0,j,low,:].astype(F32)
            q_ref[j,rows,chans:2*chans]=(gr*kr+gi*ki).astype(BF)
            q_ref[j,low,chans:2*chans]=(gi*kr-gr*ki).astype(BF)
    for j in range(2):
        v_ref[j]=jnp.dot(b_ref[0,j],q_ref[j],preferred_element_type=F32)
    join_rows(v_ref,coef_ref,p,acc_ref,inner,slice(0,chans))
    join_rows(v_ref,coef_ref,p,kg_ref,inner,slice(chans,2*chans))
    @pl.when(p==pl.num_programs(0)-1)
    def _():
        @pl.loop(0,inner//step)
        def _(i):
            rows=pl.ds(pl.multiple_of(i*step,step),step)
            for r in range(8):
                y_ref[r,rows,:]=acc_ref[r,rows,:].astype(y_ref.dtype)

def cost(flops,moved):
    return pl.CostEstimate(flops=flops,bytes_accessed=moved,transcendentals=0)

PAR=pltpu.CompilerParams(vmem_limit_bytes=52<<20)
SM=pl.BlockSpec(memory_space=pltpu.SMEM)
def whole(shape): return pl.BlockSpec(shape,lambda p:(0,)*len(shape))
def step_of(shape): return pl.BlockSpec((1,)+shape,lambda p:(p,)+(0,)*len(shape))

def spectrum(x,tables):
    fwd,inv,coef=tables
    length,ch=x.shape; inner=2*length//RADIX
    return pl.pallas_call(spec_kernel,grid=(RADIX//4,),
        in_specs=[SM,whole((8,inner,ch)),step_of((2,2*inner,2*inner))],
        out_specs=step_of((2,2*inner,ch)),
        out_shape=jax.ShapeDtypeStruct((RADIX//4,2,2*inner,ch),F32),
        scratch_shapes=[pltpu.VMEM((2,2*inner,ch),BF)],cost_estimate=cost(10000*length*ch,40*length*ch),compiler_params=PAR)(coef,x.reshape(8,inner,ch),fwd)

def long_conv(x,kspec,tables):
    fwd,inv,coef=tables
    length,ch=x.shape; inner=2*length//RADIX
    s,y=pl.pallas_call(conv_kernel,grid=(RADIX//4,),
        in_specs=[SM,whole((8,inner,ch)),step_of((2,2*inner,ch)),step_of((2,2*inner,2*inner)),step_of((2,2*inner,2*inner))],
        out_specs=[step_of((2,2*inner,ch)),whole((8,inner,ch))],
        out_shape=[jax.ShapeDtypeStruct((RADIX//4,2,2*inner,ch),BF),jax.ShapeDtypeStruct((8,inner,ch),BF)],
        scratch_shapes=[pltpu.VMEM((2,2*inner,ch),BF),pltpu.VMEM((2,2*inner,ch),F32),pltpu.VMEM((8,inner,ch),F32)],cost_estimate=cost(20000*length*ch,75*length*ch),compiler_params=PAR)(coef,x.reshape(8,inner,ch),kspec,fwd,inv)
    return s,y.reshape(length,ch)

def long_back(g,kspec,sspec,tables):
    fwd,inv,coef=tables
    length,ch=g.shape; inner=2*length//RADIX
    y,kg=pl.pallas_call(back_kernel,grid=(RADIX//4,),
        in_specs=[SM,whole((8,inner,ch)),step_of((2,2*inner,ch)),step_of((2,2*inner,ch)),step_of((2,2*inner,2*inner)),step_of((2,2*inner,2*inner))],
        out_specs=[whole((8,inner,ch)),whole((8,inner,ch))],
        out_shape=[jax.ShapeDtypeStruct((8,inner,ch),BF),jax.ShapeDtypeStruct((8,inner,ch),F32)],
        scratch_shapes=[pltpu.VMEM((2,2*inner,ch),BF),pltpu.VMEM((2,2*inner,ch),F32),pltpu.VMEM((2,2*inner,2*ch),BF),pltpu.VMEM((2,2*inner,2*ch),F32),pltpu.VMEM((8,inner,ch),F32)],cost_estimate=cost(27000*length*ch,100*length*ch),compiler_params=PAR)(coef,g.reshape(8,inner,ch),kspec,sspec,fwd,inv)
    return y.reshape(length,ch),kg.reshape(length,ch)

def ff_kernel(x_ref,g_ref,wu_ref,wd_ref,bu_ref,down_ref,gsec_ref,dwu_ref,dwd_ref,dbu_ref,a_ref,gu_ref):
    f=pl.program_id(0); rows=x_ref.shape[0]; step=256 if rows%256==0 else rows
    wu=wu_ref[...].reshape(-1,x_ref.shape[1]); wd=wd_ref[0]
    total=jnp.zeros(dbu_ref.shape[1:],F32)
    @pl.when(f==0)
    def _():
        down_ref[...]=jnp.zeros_like(down_ref)
        gsec_ref[...]=jnp.zeros_like(gsec_ref)
    for r in range(rows//step):
        at=pl.ds(r*step,step)
        up=lax.dot_general(x_ref[at,:],wu,(((1,),(1,)),((),())),preferred_element_type=F32)+bu_ref[0]
        ga=jnp.dot(g_ref[at,:],wd,preferred_element_type=F32)
        sq=up*up
        th=jnp.tanh(up*(GELU_A+(GELU_A*GELU_B)*sq))
        half_one=0.5+0.5*th
        a=(up*half_one).astype(BF)
        a_ref[at,:]=a
        slope=half_one+(up*half_one*(1.0-th))*(GELU_A+(3.0*GELU_A*GELU_B)*sq)
        gu=ga*slope
        total=total+jnp.sum(gu,axis=0,keepdims=True)
        gul=gu.astype(BF)
        gu_ref[at,:]=gul
        down_ref[at,:]+=lax.dot_general(a,wd,(((1,),(1,)),((),())),preferred_element_type=F32)
        gsec_ref[at,:]+=jnp.dot(gul,wu,preferred_element_type=F32)
    dbu_ref[0]=total
    dwu_ref[...]=lax.dot_general(gu_ref[...],x_ref[...],(((0,),(0,)),((),())),preferred_element_type=F32).astype(BF)
    dwd_ref[...]=lax.dot_general(g_ref[...],a_ref[...],(((0,),(0,)),((),())),preferred_element_type=F32).astype(BF)

GELU_A=0.7978845608
GELU_B=0.044715

def feed_forward(x,g,wu,wd,bu):
    rows,width=x.shape; hid=bu.size; blk=width; chunk=hid//wu.shape[0]; chunks=blk//chunk
    n=hid//blk
    return pl.pallas_call(ff_kernel,grid=(n,),
        in_specs=[whole((rows,width)),whole((rows,width)),pl.BlockSpec((chunks,chunk,width),lambda f:(f,0,0)),pl.BlockSpec((1,width,blk),lambda f:(f,0,0)),pl.BlockSpec((1,1,blk),lambda f:(f,0,0))],
        out_specs=[whole((rows,width)),whole((rows,width)),pl.BlockSpec((blk,width),lambda f:(f,0)),pl.BlockSpec((width,blk),lambda f:(0,f)),pl.BlockSpec((1,1,blk),lambda f:(f,0,0))],
        out_shape=[jax.ShapeDtypeStruct((rows,width),F32),jax.ShapeDtypeStruct((rows,width),F32),jax.ShapeDtypeStruct((hid,width),BF),jax.ShapeDtypeStruct((width,hid),BF),jax.ShapeDtypeStruct((n,1,blk),F32)],
        scratch_shapes=[pltpu.VMEM((rows,blk),BF),pltpu.VMEM((rows,blk),BF)],
        cost_estimate=cost(20*rows*width*hid,60*rows*hid),
        compiler_params=PAR)(x,g,wu,wd,bu.reshape(n,1,blk))

def tail_kernel(p_ref,gg_ref,jo_ref,cb_ref,gj_ref,af_ref,mk_ref,tap_ref,cbias_ref,skip_ref,
                gp_ref,sums_ref,pw_ref,gc_ref):
    b=pl.program_id(0); local=gg_ref.shape[1]; width=gg_ref.shape[2]; wide=3*width
    step=64 if local%64==0 else local; lanes=128
    @pl.when(b==0)
    def _():
        sums_ref[...]=jnp.zeros_like(sums_ref)
    @pl.loop(0,width//lanes)
    def _(j):
        def cols(s): return pl.ds(pl.multiple_of(s*width+j*lanes,lanes),lanes)
        c0=cols(0)
        for s in range(3):
            for r in range(-1,local//step):
                if r<0: pw_ref[s,0:16,:]=p_ref[0,0:16,cols(s)].astype(F32)
                else: pw_ref[s,16+r*step:16+(r+1)*step,:]=p_ref[0,16+r*step:16+(r+1)*step,cols(s)].astype(F32)
        tap=[[tap_ref[k:k+1,cols(s)] for k in range(3)] for s in range(3)]
        cbias=[cbias_ref[0:1,cols(s)] for s in range(3)]
        skip=skip_ref[0:1,c0]
        acc=[[jnp.zeros((8,lanes),F32) for _ in range(5)] for s in range(3)]
        def fold(v): return jnp.sum(v.reshape(-1,8,lanes),axis=0)
        for r in range(local//step):
            lo=r*step
            at=pl.ds(lo,step)
            sh=[[pw_ref[s,14+lo+k:14+lo+k+step,:] for k in range(3)] for s in range(3)]
            gate=[None]+[cbias[s]+tap[s][0]*sh[s][0]+tap[s][1]*sh[s][1]+tap[s][2]*sh[s][2] for s in (1,2)]
            gg=gg_ref[0,at,c0]
            gs=mk_ref[0,at,:]*(cb_ref[0,at,c0].astype(F32)+skip*gj_ref[0,at,c0].astype(F32))
            gc=[gg*jo_ref[0,at,c0].astype(F32),gs*gate[2],gs*gate[1]]
            for s in range(3):
                gc_ref[s,at,:]=gc[s]
                acc[s][0]=acc[s][0]+fold(gc[s])
                for k in range(3):
                    acc[s][1+k]=acc[s][1+k]+fold(gc[s]*sh[s][k])
        for s in range(3):
            gc_ref[s,local:local+8,:]=af_ref[0,:,cols(s)]
        for r in range(local//step):
            lo=r*step
            at=pl.ds(lo,step)
            mk=mk_ref[0,at,:]
            for s in range(3):
                gp=mk*(tap[s][2]*gc_ref[s,at,:]+tap[s][1]*gc_ref[s,lo+1:lo+1+step,:]+tap[s][0]*gc_ref[s,lo+2:lo+2+step,:])
                acc[s][4]=acc[s][4]+fold(gp)
                gp_ref[0,at,cols(s)]=gp.astype(BF)
        for s in range(3):
            for q in range(5):
                sums_ref[q:q+1,cols(s)]+=jnp.sum(acc[s][q],axis=0,keepdims=True)

def tail_back(p,gg,jo,cb,gj,af,mk,taps,cbias,skip):
    blocks,local,width=gg.shape; wide=3*width
    def blk(rows,cols): return pl.BlockSpec((1,rows,cols),lambda b:(b,0,0))
    return pl.pallas_call(tail_kernel,grid=(blocks,),
        in_specs=[blk(local+16,wide),blk(local,width),blk(local,width),blk(local,width),blk(local,width),blk(8,wide),blk(local,1),whole((3,wide)),whole((1,wide)),whole((1,width))],
        out_specs=[blk(local,wide),whole((8,wide))],
        out_shape=[jax.ShapeDtypeStruct((blocks,local,wide),BF),jax.ShapeDtypeStruct((8,wide),F32)],
        scratch_shapes=[pltpu.VMEM((3,local+16,128),F32),pltpu.VMEM((3,local+8,128),F32)],
        cost_estimate=cost(7000*blocks*local*wide,22*blocks*local*wide),compiler_params=PAR)(p,gg,jo,cb,gj,af,mk,taps,cbias,skip)

def front_kernel(t_ref,mk_ref,gain_ref,shift_ref,w_ref,bias_ref,tap_ref,cbias_ref,n_out,p_out,o_out,s_out,n_ref,p_ref):
    total=t_ref.shape[1]; width=t_ref.shape[2]; local=total-16
    step=48 if total%48==0 else 16
    gain=gain_ref[...]; shift=shift_ref[...]
    for r in range(total//step):
        at=pl.ds(r*step,step)
        x=t_ref[0,at,:].astype(F32)
        c=x-jnp.mean(x,axis=-1,keepdims=True)
        v=jnp.mean(c*c,axis=-1,keepdims=True)
        n_ref[at,:]=(c*lax.rsqrt(v+1e-05)*gain+shift).astype(BF)
    for s in range(3):
        cols=pl.ds(s*width,width)
        p_ref[:,cols]=mk_ref[0]*(lax.dot_general(n_ref[...],w_ref[cols,:],(((1,),(1,)),((),())),preferred_element_type=F32)+bias_ref[0:1,cols])
    n_out[0]=n_ref[16:,:]
    step=64 if local%64==0 else local; lanes=128
    @pl.loop(0,width//lanes)
    def _(j):
        def cols(s): return pl.ds(pl.multiple_of(s*width+j*lanes,lanes),lanes)
        tap=[[tap_ref[k:k+1,cols(s)] for k in range(3)] for s in range(3)]
        cbias=[cbias_ref[0:1,cols(s)] for s in range(3)]
        for s in range(3):
            p_out[0,0:16,cols(s)]=p_ref[0:16,cols(s)].astype(BF)
        for r in range(local//step):
            lo=r*step
            at=pl.ds(lo,step)
            conv=[]
            for s in range(3):
                mid=p_ref[16+lo:16+lo+step,cols(s)]
                p_out[0,16+lo:16+lo+step,cols(s)]=mid.astype(BF)
                conv.append(cbias[s]+tap[s][0]*p_ref[14+lo:14+lo+step,cols(s)]+tap[s][1]*p_ref[15+lo:15+lo+step,cols(s)]+tap[s][2]*mid)
            o_out[0,at,cols(0)]=conv[0].astype(BF)
            s_out[0,at,cols(0)]=(mk_ref[0,16+lo:16+lo+step,:]*conv[1]*conv[2]).astype(BF)

def front_part(tok,mk,gain,shift,w,bias,taps,cbias):
    blocks,total,width=tok.shape; wide=3*width; local=total-16
    def blk(rows,cols): return pl.BlockSpec((1,rows,cols),lambda b:(b,0,0))
    low=jax.ShapeDtypeStruct((blocks,local,width),BF)
    return pl.pallas_call(front_kernel,grid=(blocks,),
        in_specs=[blk(total,width),blk(total,1),whole((1,width)),whole((1,width)),whole((wide,width)),whole((1,wide)),whole((3,wide)),whole((1,wide))],
        out_specs=[blk(local,width),blk(total,wide),blk(local,width),blk(local,width)],
        out_shape=[low,jax.ShapeDtypeStruct((blocks,total,wide),BF),low,low],
        scratch_shapes=[pltpu.VMEM((total,width),BF),pltpu.VMEM((total,wide),F32)],
        cost_estimate=cost(7000*blocks*local*wide,22*blocks*local*wide),compiler_params=PAR)(tok,mk,gain,shift,w,bias,taps,cbias)

def filter_kernel_back(kg_ref,sh_ref,col_ref,hid_ref,m1_ref,m2_ref,f_ref,p1_ref,p2_ref,p3_ref,c1_ref,c2_ref,c3_ref,fr_ref,w2_ref,w3_ref,
                       colg_ref,g1_ref,g2_ref,g3_ref,vec_ref):
    i=pl.program_id(0)
    @pl.when(i==0)
    def _():
        for ref in (colg_ref,g1_ref,g2_ref,g3_ref,vec_ref):
            ref[...]=jnp.zeros_like(ref)
    def mul(a,b,da,db):
        def dot(u,v): return lax.dot_general(u,v,(((da,),(db,)),((),())),preferred_element_type=F32)
        ah,bh=a.astype(BF),b.astype(BF)
        al,bl=(a-ah.astype(F32)).astype(BF),(b-bh.astype(F32)).astype(BF)
        return dot(ah,bh)+(dot(ah,bl)+dot(al,bh))
    sg=kg_ref[...]*sh_ref[...]
    fr=fr_ref[...]
    colg_ref[...]+=mul(sg,hid_ref[...],0,0)
    grad=mul(sg,col_ref[...],1,0)
    rate=jnp.zeros((1,fr.shape[1]),F32)
    for row,p_ref,c_ref,in_ref,w_ref,g_ref in ((2,p3_ref,c3_ref,m2_ref,w3_ref,g3_ref),(1,p2_ref,c2_ref,m1_ref,w2_ref,g2_ref),(0,p1_ref,c1_ref,f_ref,None,g1_ref)):
        p=p_ref[...]
        turned=grad*c_ref[...]
        rate=rate+jnp.sum(turned*p,axis=0,keepdims=True)
        gp=turned*fr
        vec_ref[row:row+1,:]+=jnp.sum(gp,axis=0,keepdims=True)
        g_ref[...]+=mul(in_ref[...],gp,0,0)
        if w_ref is not None: grad=mul(gp,w_ref[...],1,1)
    vec_ref[3:4,:]+=rate

def filter_back(kg,sh,col,hid,m1,m2,feat,p1,p2,p3,c1,c2,c3,fr,w2,w3):
    length,ch=kg.shape; filt=hid.shape[1]; emb=feat.shape[1]; blk=512
    def rows(c): return pl.BlockSpec((blk,c),lambda i:(i,0))
    def out(a,b): return jax.ShapeDtypeStruct((a,b),F32)
    return pl.pallas_call(filter_kernel_back,grid=(length//blk,),
        in_specs=[rows(ch),rows(ch),whole((ch,filt)),rows(filt),rows(filt),rows(filt),rows(emb),rows(filt),rows(filt),rows(filt),rows(filt),rows(filt),rows(filt),whole((1,filt)),whole((filt,filt)),whole((filt,filt))],
        out_specs=[whole((ch,filt)),whole((emb,filt)),whole((filt,filt)),whole((filt,filt)),whole((8,filt))],
        out_shape=[out(ch,filt),out(emb,filt),out(filt,filt),out(filt,filt),out(8,filt)],
        cost_estimate=cost(30000*length*ch,100*length*ch),compiler_params=PAR)(kg,sh,col,hid,m1,m2,feat,p1,p2,p3,c1,c2,c3,fr.reshape(1,-1),w2,w3)

def product(left, right):
    return jnp.dot(left, right, precision=lax.Precision.HIGHEST, preferred_element_type=jnp.float32)

def gelu_tanh(values):
    return jax.nn.gelu(values, approximate=True)

def filter_hidden(
    features,
    filter_entry_coefficients,
    filter_entry_offset,
    filter_second_coefficients,
    filter_second_offset,
    filter_third_coefficients,
    filter_third_offset,
    periodic_frequency,
):
    first = jnp.sin(
        periodic_frequency * (product(features, filter_entry_coefficients) + filter_entry_offset)
    )
    middle = jnp.sin(
        periodic_frequency * (product(first, filter_second_coefficients) + filter_second_offset)
    )
    return jnp.sin(
        periodic_frequency * (product(middle, filter_third_coefficients) + filter_third_offset)
    )

def modulation(length, model_width, offset, channels):
    standardized_values = jnp.arange(length).astype(jnp.float32) / (length - 1)
    slowest = math.log(0.01) / 1.5
    fastest = math.log(0.01) / 0.3
    columns = (offset + jnp.arange(channels)).astype(jnp.float32)
    decays = slowest + (fastest - slowest) * columns / (model_width - 1)
    return jnp.exp(-standardized_values[:, None] * jnp.abs(decays)[None, :]) + 0.05

def position_features(length, emb_width):
    band_count = (emb_width - 1) // 2
    places = np.arange(length, dtype=np.float64)
    band_rates = 0.0001 + (band_count - 1 - 0.0001) * np.arange(band_count) / (band_count - 1)
    phases = (2.0 * math.pi * places / length)[:, None] * band_rates[None, :]
    return np.concatenate(
        [(places / (length - 1))[:, None], np.cos(phases), -np.sin(phases)], axis=1
    ).astype(np.float32)


def pairs_of(count, mask):
    return [(i, i ^ mask) for i in range(count)]


def bit_of(me, bit):
    return (me >> bit) & 1


def grouped(bits):
    return [tuple(bits[i : i + 2]) for i in range(0, len(bits), 2)]


class Gather:
    flight = None

    def __init__(self, value, me, count, order):
        self.held, self.me, self.count, self.order = value, me, count, list(order)
        self.at = 0

    def give(self):
        return self.held

    def ways(self, given):
        return [(given, pairs_of(self.count, 1 << self.order[self.at]))]

    def receive(self, got):
        self.at += 1
        if self.at < len(self.order):
            self.held = jnp.concatenate([self.held, got[0]], axis=0)
        else:
            self.held = place_shards(self.held, got[0], self.me, self.count, self.order)

    @property
    def open(self):
        return self.at < len(self.order)


class Scatter:
    flight = None

    def __init__(self, value, me, count, order, keep):
        self.value, self.me, self.count, self.keep = value, me, count, keep
        self.order = [g if isinstance(g, tuple) else (g,) for g in order]
        self.rows, self.columns = value.shape[1:]
        self.left = [b for g in self.order for b in g]
        self.at = 0

    def give(self):
        group = self.order[self.at]
        size = 1 << len(group)
        low = 1 << sum(1 for b in self.left if b < group[0])
        cut = self.value.reshape(-1, size, low * self.rows, self.columns)
        at = (self.me >> group[0]) & (size - 1)
        self.mine = lax.dynamic_index_in_dim(cut, at, 1, keepdims=False)
        return tuple(
            lax.dynamic_index_in_dim(cut, at ^ m, 1, keepdims=False) for m in range(1, size)
        )

    def ways(self, given):
        group = self.order[self.at]
        self.left = [b for b in self.left if b not in group]
        return [
            (g, pairs_of(self.count, m << group[0])) for m, g in enumerate(given, start=1)
        ]

    def receive(self, got):
        self.at += 1
        self.value = self.mine.astype(F32)
        for g in got:
            self.value = self.value + g.astype(F32)
        if self.open:
            self.value = self.value.astype(self.keep)
        else:
            self.value = self.value.reshape(self.rows, self.columns)

    @property
    def open(self):
        return self.at < len(self.order)


class Swap:
    flight = None

    def __init__(self, value, me, count, bit):
        self.value, self.me, self.count, self.bit = value, me, count, bit
        self.open = True

    def give(self):
        return self.value

    def ways(self, given):
        return [(given, pairs_of(self.count, 1 << self.bit))]

    def receive(self, got):
        self.value = got[0]
        self.open = False


class Ring:
    flight = None

    def __init__(self, value, count, half, by):
        self.value, self.open = value, True
        self.pairs = []
        for i in range(count):
            group, r = divmod(i, half)
            self.pairs.append((i, group * half + (r + by) % half))

    def give(self):
        return self.value

    def ways(self, given):
        return [(given, self.pairs)]

    def receive(self, got):
        self.value = got[0]
        self.open = False


class Exchange:
    flight = None

    def __init__(self, value):
        self.value, self.open = value, True

    def give(self):
        return self.value

    def ways(self, given):
        return [(given, None)]

    def receive(self, got):
        self.value = jnp.sum(got[0], axis=0)
        self.open = False


class Total:
    flight = None

    def __init__(self, value, me, count):
        self.value, self.me, self.count = value, me, count
        bits = list(range(count.bit_length() - 1))
        self.groups = grouped(bits)
        self.at = 0

    def give(self):
        return self.value

    def ways(self, given):
        group = self.groups[self.at]
        return [
            (given, pairs_of(self.count, m << group[0])) for m in range(1, 1 << len(group))
        ]

    def receive(self, got):
        self.at += 1
        for v in got:
            self.value = self.value + v

    @property
    def open(self):
        return self.at < len(self.groups)


def send(*chains, state=()):
    chains = [c for c in chains if c.open]
    given = [c.give() for c in chains]
    tied = lax.optimization_barrier(tuple(state) + tuple(given))
    for c, g in zip(chains, tied[len(state) :]):
        c.flight = [
            lax.all_to_all(v, AXES, 0, 0, tiled=True)
            if pairs is None
            else lax.ppermute(v, AXES, pairs)
            for v, pairs in c.ways(g)
        ]
    return tied[: len(state)]


def meet(state, *chains):
    chains = [c for c in chains if c.flight]
    sizes = [len(c.flight) for c in chains]
    tied = lax.optimization_barrier(tuple(state) + tuple(v for c in chains for v in c.flight))
    at = len(state)
    for c, n in zip(chains, sizes):
        c.receive(tied[at : at + n])
        c.flight = None
        at += n
    return tied[: len(state)]


def drain(*chains):
    meet((), *chains)
    while any(c.open for c in chains):
        send(*chains)
        meet((), *chains)


def place_shards(near, other, me, count, order):
    rows = near.shape[0] * 2 // count
    half = count // 2

    def spread(i):
        return sum(((i >> p) & 1) << bit for p, bit in enumerate(order[:-1]))

    def kernel(me_ref, near_ref, other_ref, out_ref):
        own = me_ref[0]
        for i in range(half):
            out_ref[jnp.bitwise_xor(own, spread(i))] = near_ref[i]
            out_ref[jnp.bitwise_xor(own, spread(i) | (1 << order[-1]))] = other_ref[i]

    vmem = pl.BlockSpec(memory_space=pltpu.VMEM)
    shape = (count, rows) + near.shape[1:]
    return pl.pallas_call(
        kernel,
        in_specs=[SM, vmem, vmem],
        out_specs=vmem,
        out_shape=jax.ShapeDtypeStruct(shape, near.dtype),
        compiler_params=PAR,
    )(
        me.reshape(1).astype(jnp.int32),
        near.reshape((half, rows) + near.shape[1:]),
        other.reshape((half, rows) + near.shape[1:]),
    )


def orders_of(count):
    bits = count.bit_length() - 1
    first = list(range(bits))
    second = list(range(bits))
    second[1], second[2] = second[2], second[1]
    return first, second


def normalise(values):
    centre = values - jnp.mean(values, axis=-1, keepdims=True)
    spread = jnp.mean(centre * centre, axis=-1, keepdims=True)
    rstd = lax.rsqrt(spread + 1e-05)
    return centre * rstd, rstd


def normalise_back(unit, rstd, incoming):
    return rstd * (
        incoming
        - jnp.mean(incoming, axis=-1, keepdims=True)
        - unit * jnp.mean(incoming * unit, axis=-1, keepdims=True)
    )


def dot_nt(left, right):
    return lax.dot_general(left, right, (((1,), (1,)), ((), ())), preferred_element_type=F32)


def dot_nn(left, right):
    return lax.dot_general(left, right, (((1,), (0,)), ((), ())), preferred_element_type=F32)


def dot_tn(left, right):
    return lax.dot_general(left, right, (((0,), (0,)), ((), ())), preferred_element_type=F32)


def per_device(
    block_input,
    slot_spans,
    output_adjoint,
    opening_scale_factor,
    opening_offset_vector,
    intake_coefficients,
    intake_offset,
    brief_filter_coefficients,
    brief_filter_offset,
    direct_path_factor,
    filter_final_coefficients,
    mixer_output_coefficients,
    mixer_output_offset,
    closing_scale_factor,
    closing_offset_vector,
    expand_coefficients,
    expand_offset,
    contract_coefficients,
    contract_offset,
    filter_entry_coefficients,
    filter_entry_offset,
    filter_second_coefficients,
    filter_second_offset,
    filter_third_coefficients,
    filter_third_offset,
    periodic_frequency,
):
    width = block_input.shape[2]
    local = block_input.shape[1]
    seq_count = lax.axis_size("seq")
    count = lax.axis_size("dp") * seq_count
    seq_index = lax.axis_index("seq")
    me = lax.axis_index("dp") * seq_count + seq_index
    half = seq_count // 2
    group_bits = half.bit_length() - 1
    rank = seq_index % half
    side = seq_index // half
    length = local * seq_count
    channels = width // half
    chan_start = rank * channels
    up, across = orders_of(count)
    down, back = up[::-1], across[::-1]
    tables = tuple(jnp.asarray(t) for t in dft_tables(length))

    vectors = (
        opening_scale_factor,
        opening_offset_vector,
        direct_path_factor,
        mixer_output_offset,
        closing_scale_factor,
        closing_offset_vector,
        contract_offset,
        intake_offset,
        brief_filter_offset,
        brief_filter_coefficients,
        expand_offset,
    )
    middle = width // 2
    far = half.bit_length() - 1
    intake_shard = intake_coefficients.T
    front = Gather(intake_shard[:, :middle], me, count, down)
    rear = Gather(intake_shard[:, middle:], me, count, back)
    bits = len(down)
    spread = list(range(1, bits)) + [0]
    final = Gather(filter_final_coefficients.T.astype(F32), me, count, spread)
    trade = Swap(
        lax.dynamic_index_in_dim(block_input, 1 - side, 0, keepdims=False), me, count, far
    )
    features = jnp.asarray(position_features(length, filter_entry_coefficients.shape[0]))
    send(final, front, rear)
    send(trade)
    later = jnp.concatenate(
        [expand_coefficients.T]
        + [
            contract_coefficients[q * width : (q + 1) * width].T
            for q in range(contract_coefficients.shape[0] // width)
        ]
        + [mixer_output_coefficients.T],
        axis=0,
    )
    frequency = periodic_frequency

    def layer(values, weights, offset):
        p = product(values, weights) + offset
        return p, jnp.sin(frequency * p), jnp.cos(frequency * p)

    p1, m1, c1 = layer(features, filter_entry_coefficients, filter_entry_offset)
    p1, m1, c1, later = meet((p1, m1, c1, later), final, front, rear)
    later = lax.all_gather(later, AXES, axis=0, tiled=False)
    (m1,) = send(final, front, rear, state=(m1,))
    p2, m2, c2 = layer(m1, filter_second_coefficients, filter_second_offset)
    p2, m2, c2 = meet((p2, m2, c2), final, front, rear)
    (m2,) = send(final, front, rear, state=(m2,))
    p3, hidden, c3 = layer(m2, filter_third_coefficients, filter_third_offset)
    pack = jnp.concatenate([v.reshape(-1) for v in vectors])
    used = pack.size
    pad = -used % 1024
    pack = jnp.concatenate([pack, jnp.zeros((pad,), pack.dtype)]).reshape(8, -1).astype(F32)
    p3, hidden, c3, pack = meet((p3, hidden, c3, pack), final)
    bundle = Gather(pack, me, count, spread)
    (hidden,) = send(final, bundle, state=(hidden,))
    shaping = modulation(length, width, chan_start, channels)
    (shaping,) = meet((shaping,), final, bundle, front, rear)
    (shaping,) = send(final, bundle, front, rear, state=(shaping,))
    own_rows = lax.dynamic_index_in_dim(block_input, side, 0, keepdims=False)
    (own_rows,) = meet((own_rows,), final, bundle, trade)
    drain(final)
    columns = lax.dynamic_slice_in_dim(final.held.reshape(width, -1), chan_start, channels, 0)
    (columns,) = send(bundle, state=(columns,))
    filter_kernel = (
        lax.dot_general(
            hidden,
            columns,
            (((1,), (1,)), ((), ())),
            precision=lax.Precision.HIGHEST,
            preferred_element_type=F32,
        )
        * shaping
    )
    (filter_kernel,) = meet((filter_kernel,), bundle)
    (filter_kernel,) = send(bundle, state=(filter_kernel,))
    kernel_spec = spectrum(filter_kernel, tables)
    tokens_low = jnp.concatenate([own_rows, trade.value], axis=0)
    kernel_spec, tokens_low = meet((kernel_spec, tokens_low), bundle, front, rear)
    blocks = tokens_low.reshape(2, local, width)
    ends = Ring(blocks[:, local - 16 :], count, half, 1)
    send(front, rear, bundle, ends)
    own_base = seq_index * local
    far_base = ((1 - side) * half + rank) * local
    span = lax.dynamic_index_in_dim(slot_spans, side, 0, keepdims=False)
    places = jnp.stack([own_base, far_base])[:, None] + jnp.arange(-16, local)
    mask_all = ((places >= span[0]) & (places < span[0] + span[1])).astype(F32)[:, :, None]
    row_mask = mask_all[:, 16:].reshape(-1, 1)
    tokens = tokens_low.astype(F32)
    (mask_all,) = meet((mask_all,), bundle, front, rear, ends)
    drain(bundle, front, rear)
    no_rows = jnp.zeros_like(ends.value[0])
    wrapped = jnp.stack(
        [
            jnp.where(side == 1, ends.value[1], no_rows),
            jnp.where(side == 0, ends.value[0], no_rows),
        ]
    )
    before = jnp.where(rank == 0, wrapped, ends.value)
    blocks = jnp.concatenate([before, blocks], axis=1)
    pack_full = bundle.held.reshape(count, -1)
    fields = []
    at = 0
    for v in vectors:
        part = pack_full[:, at : at + v.size]
        at += v.size
        if v.ndim == 1:
            fields.append(part.reshape(-1))
        else:
            fields.append(
                part.reshape(count, v.shape[0], -1).transpose(1, 0, 2).reshape(v.shape[0], -1)
            )
    (
        gain_one,
        shift_one,
        skip_gain,
        mix_bias,
        gain_two,
        shift_two,
        down_bias,
        intake_bias,
        conv_bias,
        conv_taps,
        up_bias,
    ) = fields
    intake_t = jnp.concatenate(
        [front.held.reshape(-1, middle), rear.held.reshape(-1, middle)], axis=1
    )
    trade_adj = Swap(
        lax.dynamic_index_in_dim(output_adjoint, 1 - side, 0, keepdims=False), me, count, far
    )
    send(trade_adj)

    rows = 2 * local
    normed_low, projected_all, outer_gate, signal = front_part(
        blocks,
        mask_all,
        gain_one.reshape(1, -1),
        shift_one.reshape(1, -1),
        intake_t,
        intake_bias.reshape(1, -1),
        conv_taps,
        conv_bias.reshape(1, -1),
    )
    normed_low = normed_low.reshape(rows, width)
    outer_gate = outer_gate.reshape(rows, width).astype(F32)
    signal = signal.reshape(rows, width)

    def traded(near, give):
        got = [near]
        for k in range(1, half):
            got.append(lax.ppermute(give(k), AXES, [(i, i ^ k) for i in range(count)]))
        if half == 2:
            return jnp.where(rank == 0, got[0], got[1]), jnp.where(rank == 0, got[1], got[0])
        stacked = jnp.take(jnp.stack(got), jnp.arange(half) ^ rank, axis=0)
        return tuple(stacked[k] for k in range(half))

    def to_channels(value):
        def give(k):
            return lax.dynamic_slice_in_dim(value, (rank ^ k) * channels, channels, 1)

        pieces = traded(give(0), give)
        first = [jnp.where(side == 0, p[:local], p[local:]) for p in pieces]
        second = [jnp.where(side == 0, p[local:], p[:local]) for p in pieces]
        return jnp.concatenate(first + second, axis=0)

    def to_rows(value):
        def give(k):
            first = lax.dynamic_slice_in_dim(value, (rank ^ k) * local, local, 0)
            second = lax.dynamic_slice_in_dim(value, (half + (rank ^ k)) * local, local, 0)
            return jnp.concatenate(
                [jnp.where(side == 0, first, second), jnp.where(side == 0, second, first)], axis=0
            )

        return jnp.concatenate(traded(give(0), give), axis=1)

    def blocks_of(value):
        return value.reshape(2, local, -1)

    sig_spec, carried_cols = long_conv(to_channels(signal), kernel_spec, tables)
    carried = to_rows(carried_cols.astype(BF)).astype(F32)
    signal_wide = signal.astype(F32)
    joined = carried + skip_gain * signal_wide
    joined_low = joined.astype(BF)
    gated_mix = (joined * outer_gate).astype(BF)
    (gated_mix,) = meet((gated_mix,), trade_adj)
    own_adj = lax.dynamic_index_in_dim(output_adjoint, side, 0, keepdims=False)
    adjoint = jnp.concatenate([own_adj, trade_adj.value], axis=0)
    ff_rows = expand_coefficients.shape[1]
    mix_rows = mixer_output_coefficients.shape[1]
    if ff_rows % 16 == 0:
        up_t = later
    else:
        up_t = later[:, :ff_rows]
    mix_t = later[:, later.shape[1] - mix_rows :].reshape(-1, width)
    folds = contract_coefficients.shape[0] // width
    down_t = (
        later[:, ff_rows : later.shape[1] - mix_rows]
        .reshape(count, folds, -1, width)
        .transpose(1, 0, 2, 3)
        .reshape(folds, width, width)
    )
    residual = tokens + dot_nt(gated_mix, mix_t) + mix_bias
    unit_two, rstd_two = normalise(residual)
    second_low = (unit_two * gain_two + shift_two).astype(BF)
    grad_out = row_mask * adjoint.astype(F32)
    grad_low = grad_out.astype(BF)
    down_proj, grad_second, up_grad, down_grad, up_bias_grad = feed_forward(
        second_low, grad_low, up_t, down_t, up_bias
    )
    up_bias_grad = up_bias_grad.reshape(-1)
    output = (row_mask * (residual + down_proj + down_bias)).astype(BF)

    up_sum = Scatter(up_grad.reshape(count, -1, width), me, count, across, BF)
    down_sum = Scatter(down_grad.reshape(count, -1, down_grad.shape[1]), me, count, up, BF)
    (grad_second,) = send(up_sum, down_sum, state=(grad_second,))
    down_bias_grad = jnp.sum(grad_out, axis=0)
    gain_two_grad = jnp.sum(grad_second * unit_two, axis=0)
    shift_two_grad = jnp.sum(grad_second, axis=0)
    grad_residual = grad_out + normalise_back(unit_two, rstd_two, grad_second * gain_two)
    mix_bias_grad = jnp.sum(grad_residual, axis=0)
    resid_low = grad_residual.astype(BF)
    mix_grad = dot_tn(resid_low, gated_mix).astype(BF)
    grad_gated = dot_nn(resid_low, mix_t)
    grad_joined = grad_gated * outer_gate
    grad_joined_low = grad_joined.astype(BF)
    skip_grad = jnp.sum(grad_joined * signal_wide, axis=0)
    (grad_joined_low, mix_grad) = meet((grad_joined_low, mix_grad), up_sum, down_sum)
    mix_sum = Scatter(mix_grad.reshape(count, -1, width), me, count, up, BF)
    (grad_joined_low,) = send(mix_sum, up_sum, down_sum, state=(grad_joined_low,))
    conv_back_cols, kernel_grad = long_back(
        to_channels(grad_joined_low), kernel_spec, sig_spec, tables
    )
    conv_back_cols, kernel_grad = meet((conv_back_cols, kernel_grad), mix_sum, up_sum, down_sum)
    (conv_back_cols,) = send(mix_sum, up_sum, down_sum, state=(conv_back_cols,))
    conv_back_low = to_rows(conv_back_cols.astype(BF))
    conv_back = conv_back_low.astype(F32)
    first = blocks_of(grad_gated)[:, :2]
    first_signal = blocks_of(row_mask)[:, :2] * (
        blocks_of(conv_back)[:, :2] + skip_gain * blocks_of(grad_joined_low)[:, :2].astype(F32)
    )
    near = projected_all[:, 14:18, width:].astype(F32)
    first_gates = conv_bias[width:] + sum(
        conv_taps[k, width:] * near[:, k : k + 2] for k in range(3)
    )
    starts = Ring(
        jnp.concatenate(
            [
                first * blocks_of(joined_low)[:, :2].astype(F32),
                first_signal * first_gates[:, :, width:],
                first_signal * first_gates[:, :, :width],
            ],
            axis=2,
        ),
        count,
        half,
        -1,
    )
    send(starts)
    (conv_back_low,) = meet((conv_back_low,), starts)
    starts = starts.value
    trade_out = Swap(output[local:], me, count, far)
    wrapped_after = jnp.stack(
        [jnp.where(side == 0, starts[1], 0.0), jnp.where(side == 1, starts[0], 0.0)]
    )
    after = jnp.where(rank == half - 1, wrapped_after, starts)
    after = jnp.concatenate([after, jnp.zeros((2, 6, after.shape[2]), F32)], axis=1)
    grad_projected, sums = tail_back(
        projected_all,
        blocks_of(grad_gated),
        blocks_of(joined_low),
        blocks_of(conv_back_low),
        blocks_of(grad_joined_low),
        after,
        blocks_of(row_mask),
        conv_taps,
        conv_bias.reshape(1, -1),
        skip_gain.reshape(1, -1),
    )
    conv_bias_grad = sums[0]
    taps_grad = sums[1:4]
    intake_bias_grad = sums[4]
    projected_low = grad_projected.reshape(rows, -1)
    (projected_low,) = meet((projected_low,), mix_sum, up_sum, down_sum)
    (projected_low,) = send(
        mix_sum, up_sum, down_sum, trade_out, state=(projected_low,)
    )
    intake_grad = dot_tn(projected_low, normed_low).astype(BF).reshape(count, -1, width)
    intake_grad, projected_low = meet((intake_grad, projected_low))
    front_sum = Scatter(intake_grad[:, :, :middle], me, count, up, BF)
    rear_sum = Scatter(intake_grad[:, :, middle:], me, count, across, BF)
    (projected_low,) = send(front_sum, rear_sum, state=(projected_low,))
    unit_one, rstd_one = normalise(tokens)
    grad_normed = dot_nn(projected_low, intake_t)
    gain_one_grad = jnp.sum(grad_normed * unit_one, axis=0)
    shift_one_grad = jnp.sum(grad_normed, axis=0)
    tokens_grad = (
        grad_residual + normalise_back(unit_one, rstd_one, grad_normed * gain_one)
    ).astype(BF)
    tokens_grad, kernel_grad = meet(
        (tokens_grad, kernel_grad), mix_sum, up_sum, down_sum, front_sum, rear_sum
    )
    (kernel_grad,) = send(
        mix_sum, up_sum, down_sum, front_sum, rear_sum, state=(kernel_grad,)
    )

    vector_grads = (
        gain_one_grad,
        shift_one_grad,
        skip_grad,
        mix_bias_grad,
        gain_two_grad,
        shift_two_grad,
        down_bias_grad,
        intake_bias_grad,
        conv_bias_grad,
        taps_grad,
        up_bias_grad,
    )
    pieces = []
    for g in vector_grads:
        if g.ndim == 1:
            pieces.append(g.reshape(count, -1))
        else:
            pieces.append(
                g.reshape(g.shape[0], count, -1).transpose(1, 0, 2).reshape(count, -1)
            )
    packed = jnp.concatenate(pieces + [jnp.zeros((count, pad), F32)], axis=1)
    bundle_sum = Exchange(packed.reshape(count, 8, -1))
    trade_tokens = Swap(tokens_grad[local:], me, count, far)
    (kernel_grad,) = send(bundle_sum, state=(kernel_grad,))
    column_grad, entry, second, third, vecs = filter_back(
        kernel_grad,
        shaping,
        columns,
        hidden,
        m1,
        m2,
        features,
        p1,
        p2,
        p3,
        c1,
        c2,
        c3,
        frequency,
        filter_second_coefficients,
        filter_third_coefficients,
    )
    column_grad, entry = meet(
        (column_grad, entry), front_sum, rear_sum, mix_sum, up_sum, down_sum, trade_out
    )
    filter_full = lax.dynamic_update_slice_in_dim(
        jnp.zeros((width, hidden.shape[1]), F32), column_grad, chan_start, 0
    )
    net_sum = Total(
        jnp.concatenate([entry, second, third, vecs], axis=0), me, count
    )
    final_sum = Exchange(filter_full.reshape(count, -1, hidden.shape[1]))
    send(front_sum, rear_sum, mix_sum, net_sum, final_sum, trade_tokens)
    meet((), front_sum, rear_sum, mix_sum, net_sum)
    send(front_sum, rear_sum, net_sum)
    meet((), front_sum, rear_sum, net_sum, bundle_sum, trade_tokens)
    send(front_sum, rear_sum, net_sum)
    meet((), front_sum, rear_sum, net_sum, final_sum)
    drain(
        bundle_sum,
        final_sum,
        net_sum,
        front_sum,
        rear_sum,
        mix_sum,
        up_sum,
        down_sum,
        trade_tokens,
    )
    summed = bundle_sum.value.reshape(-1)
    small = []
    at = 0
    for v in vectors:
        small.append(summed[at : at + v.size].reshape(v.shape))
        at += v.size
    emb, filt = entry.shape
    total = net_sum.value
    vec_at = emb + 2 * filt
    net_out = (
        total[:emb],
        total[vec_at],
        total[emb : emb + filt],
        total[vec_at + 1],
        total[emb + filt : vec_at],
        total[vec_at + 2],
        total[vec_at + 3],
    )
    intake_shard_grad = jnp.concatenate([front_sum.value, rear_sum.value], axis=1)

    def at_home(near, far_part):
        return jnp.where(side == 0, jnp.stack([near, far_part]), jnp.stack([far_part, near]))

    output_home = at_home(output[:local], trade_out.value)
    tokens_home = at_home(tokens_grad[:local], trade_tokens.value)
    return (
        output_home,
        tokens_home,
        small[0],
        small[1],
        intake_shard_grad.T,
        small[7],
        small[9],
        small[8],
        small[2],
        final_sum.value.T,
        mix_sum.value.T,
        small[3],
        small[4],
        small[5],
        up_sum.value.T,
        small[10],
        down_sum.value.T,
        small[6],
    ) + net_out

def solution(mesh):
    in_specs = (
        P("dp", "seq", None),
        P("dp", None),
        P("dp", "seq", None),
        P(("dp", "seq")),
        P(("dp", "seq")),
        P(None, ("dp", "seq")),
        P(("dp", "seq")),
        P(None, ("dp", "seq")),
        P(("dp", "seq")),
        P(("dp", "seq")),
        P(None, ("dp", "seq")),
        P(None, ("dp", "seq")),
        P(("dp", "seq")),
        P(("dp", "seq")),
        P(("dp", "seq")),
        P(None, ("dp", "seq")),
        P(("dp", "seq")),
        P(None, ("dp", "seq")),
        P(("dp", "seq")),
        P(),
        P(),
        P(),
        P(),
        P(),
        P(),
        P(),
    )
    out_specs = (
        P("dp", "seq", None),
        P("dp", "seq", None),
        P(("dp", "seq")),
        P(("dp", "seq")),
        P(None, ("dp", "seq")),
        P(("dp", "seq")),
        P(None, ("dp", "seq")),
        P(("dp", "seq")),
        P(("dp", "seq")),
        P(None, ("dp", "seq")),
        P(None, ("dp", "seq")),
        P(("dp", "seq")),
        P(("dp", "seq")),
        P(("dp", "seq")),
        P(None, ("dp", "seq")),
        P(("dp", "seq")),
        P(None, ("dp", "seq")),
        P(("dp", "seq")),
        P(),
        P(),
        P(),
        P(),
        P(),
        P(),
        P(),
    )
    return jax.shard_map(
        per_device, mesh=mesh, in_specs=in_specs, out_specs=out_specs, check_vma=False
    )
```

```python
import math

import jax
import jax.numpy as jnp
import ml_dtypes
import numpy as np
from jax import lax
from jax.experimental import pallas as pl
from jax.experimental.pallas import tpu as pltpu
from jax.sharding import PartitionSpec as P

AXES = ("dp", "seq")

F32=jnp.float32; BF=jnp.bfloat16
RADIX=16

def dft_tables(length):
    padded = 2*length
    inner = padded//RADIX
    pairs = RADIX//4
    half = RADIX//2
    m = np.arange(inner)
    mats=[]
    for p in range(pairs):
        for s in (p, half-1-p):
            k2 = 2*(RADIX*m+s)+1
            ang = np.pi*((k2[:,None]*m[None,:])%(2*padded))/padded
            c,sn=np.cos(ang),np.sin(ang)
            mats.append(np.block([[c,sn],[-sn,c]]))
    fwd=np.stack(mats).reshape(pairs,2,2*inner,2*inner)
    inv=np.swapaxes(fwd,-1,-2)/length
    r=np.arange(half)
    th=np.pi*(r[None,:]*(2*np.arange(pairs)[:,None]+1))/RADIX
    coef=np.concatenate([np.cos(th),np.sin(th)],axis=1).astype(np.float32)
    return fwd.astype(ml_dtypes.bfloat16),inv.astype(ml_dtypes.bfloat16),coef

def split_rows(x_ref,coef_ref,p,z_ref,inner):
    step=16
    @pl.loop(0,inner//step,unroll=True)
    def _(i):
        lo=pl.multiple_of(i*step,step)
        rows=pl.ds(lo,step); low=pl.ds(pl.multiple_of(inner+i*step,step),step)
        xs=[x_ref[r,rows,:].astype(F32) for r in range(8)]
        c=[coef_ref[p,r] for r in range(8)]; s=[coef_ref[p,8+r] for r in range(8)]
        ce=xs[0]+c[2]*xs[2]+c[4]*xs[4]+c[6]*xs[6]
        co=c[1]*xs[1]+c[3]*xs[3]+c[5]*xs[5]+c[7]*xs[7]
        se=s[2]*xs[2]+s[4]*xs[4]+s[6]*xs[6]
        so=s[1]*xs[1]+s[3]*xs[3]+s[5]*xs[5]+s[7]*xs[7]
        z_ref[0,rows,:]=(ce+co).astype(BF)
        z_ref[1,rows,:]=(ce-co).astype(BF)
        z_ref[0,low,:]=(-(se+so)).astype(BF)
        z_ref[1,low,:]=(se-so).astype(BF)

def join_rows(w_ref,coef_ref,p,acc_ref,inner,lanes):
    step=16
    @pl.loop(0,inner//step,unroll=True)
    def _(i):
        lo=pl.multiple_of(i*step,step)
        rows=pl.ds(lo,step); low=pl.ds(pl.multiple_of(inner+i*step,step),step)
        r0=w_ref[0,rows,lanes]; r1=w_ref[1,rows,lanes]
        i0=w_ref[0,low,lanes]; i1=w_ref[1,low,lanes]
        rs=(r0+r1,r0-r1); im=(i0-i1,i0+i1)
        for r in range(8):
            if r==0: term=rs[0]
            else: term=coef_ref[p,r]*rs[r%2]-coef_ref[p,8+r]*im[r%2]
            acc_ref[r,rows,:]=jnp.where(p==0,0.0,acc_ref[r,rows,:])+term

def spec_kernel(coef_ref,x_ref,f_ref,o_ref,z_ref):
    p=pl.program_id(0); inner=x_ref.shape[1]
    split_rows(x_ref,coef_ref,p,z_ref,inner)
    for j in range(2):
        o_ref[0,j]=jnp.dot(f_ref[0,j],z_ref[j],preferred_element_type=F32).astype(o_ref.dtype)

def conv_kernel(coef_ref,x_ref,k_ref,f_ref,b_ref,s_ref,y_ref,z_ref,w_ref,acc_ref):
    p=pl.program_id(0); inner=x_ref.shape[1]
    split_rows(x_ref,coef_ref,p,z_ref,inner)
    for j in range(2):
        w_ref[j]=jnp.dot(f_ref[0,j],z_ref[j],preferred_element_type=F32)
    step=16
    for j in range(2):
        @pl.loop(0,inner//step,unroll=True)
        def _(i):
            rows=pl.ds(pl.multiple_of(i*step,step),step); low=pl.ds(pl.multiple_of(inner+i*step,step),step)
            xr=w_ref[j,rows,:]; xi=w_ref[j,low,:]
            kr=k_ref[0,j,rows,:].astype(F32); ki=k_ref[0,j,low,:].astype(F32)
            s_ref[0,j,rows,:]=xr.astype(BF); s_ref[0,j,low,:]=xi.astype(BF)
            z_ref[j,rows,:]=(xr*kr-xi*ki).astype(BF)
            z_ref[j,low,:]=(xr*ki+xi*kr).astype(BF)
    for j in range(2):
        w_ref[j]=jnp.dot(b_ref[0,j],z_ref[j],preferred_element_type=F32)
    join_rows(w_ref,coef_ref,p,acc_ref,inner,slice(None))
    @pl.when(p==pl.num_programs(0)-1)
    def _():
        @pl.loop(0,inner//step,unroll=True)
        def _(i):
            rows=pl.ds(pl.multiple_of(i*step,step),step)
            for r in range(8):
                y_ref[r,rows,:]=acc_ref[r,rows,:].astype(y_ref.dtype)

def back_kernel(coef_ref,g_ref,k_ref,s_ref,f_ref,b_ref,y_ref,kg_ref,z_ref,w_ref,q_ref,v_ref,acc_ref):
    p=pl.program_id(0); inner=g_ref.shape[1]; chans=g_ref.shape[2]
    split_rows(g_ref,coef_ref,p,z_ref,inner)
    for j in range(2):
        w_ref[j]=jnp.dot(f_ref[0,j],z_ref[j],preferred_element_type=F32)
    step=16
    for j in range(2):
        @pl.loop(0,inner//step,unroll=True)
        def _(i):
            rows=pl.ds(pl.multiple_of(i*step,step),step); low=pl.ds(pl.multiple_of(inner+i*step,step),step)
            gr=w_ref[j,rows,:]; gi=w_ref[j,low,:]
            kr=k_ref[0,j,rows,:].astype(F32); ki=k_ref[0,j,low,:].astype(F32)
            q_ref[j,rows,0:chans]=(gr*kr+gi*ki).astype(BF)
            q_ref[j,low,0:chans]=(gi*kr-gr*ki).astype(BF)
            kr=s_ref[0,j,rows,:].astype(F32); ki=s_ref[0,j,low,:].astype(F32)
            q_ref[j,rows,chans:2*chans]=(gr*kr+gi*ki).astype(BF)
            q_ref[j,low,chans:2*chans]=(gi*kr-gr*ki).astype(BF)
    for j in range(2):
        v_ref[j]=jnp.dot(b_ref[0,j],q_ref[j],preferred_element_type=F32)
    join_rows(v_ref,coef_ref,p,acc_ref,inner,slice(0,chans))
    join_rows(v_ref,coef_ref,p,kg_ref,inner,slice(chans,2*chans))
    @pl.when(p==pl.num_programs(0)-1)
    def _():
        @pl.loop(0,inner//step,unroll=True)
        def _(i):
            rows=pl.ds(pl.multiple_of(i*step,step),step)
            for r in range(8):
                y_ref[r,rows,:]=acc_ref[r,rows,:].astype(y_ref.dtype)

def cost(flops,moved):
    return pl.CostEstimate(flops=flops,bytes_accessed=moved,transcendentals=0)

PAR=pltpu.CompilerParams(vmem_limit_bytes=52<<20)
SM=pl.BlockSpec(memory_space=pltpu.SMEM)
def whole(shape): return pl.BlockSpec(shape,lambda p:(0,)*len(shape))
def step_of(shape): return pl.BlockSpec((1,)+shape,lambda p:(p,)+(0,)*len(shape))

def spectrum(x,tables):
    fwd,inv,coef=tables
    length,ch=x.shape; inner=2*length//RADIX
    return pl.pallas_call(spec_kernel,grid=(RADIX//4,),
        in_specs=[SM,whole((8,inner,ch)),step_of((2,2*inner,2*inner))],
        out_specs=step_of((2,2*inner,ch)),
        out_shape=jax.ShapeDtypeStruct((RADIX//4,2,2*inner,ch),F32),
        scratch_shapes=[pltpu.VMEM((2,2*inner,ch),BF)],cost_estimate=cost(10000*length*ch,40*length*ch),compiler_params=PAR)(coef,x.reshape(8,inner,ch),fwd)

def long_conv(x,kspec,tables):
    fwd,inv,coef=tables
    length,ch=x.shape; inner=2*length//RADIX
    s,y=pl.pallas_call(conv_kernel,grid=(RADIX//4,),
        in_specs=[SM,whole((8,inner,ch)),step_of((2,2*inner,ch)),step_of((2,2*inner,2*inner)),step_of((2,2*inner,2*inner))],
        out_specs=[step_of((2,2*inner,ch)),whole((8,inner,ch))],
        out_shape=[jax.ShapeDtypeStruct((RADIX//4,2,2*inner,ch),BF),jax.ShapeDtypeStruct((8,inner,ch),BF)],
        scratch_shapes=[pltpu.VMEM((2,2*inner,ch),BF),pltpu.VMEM((2,2*inner,ch),F32),pltpu.VMEM((8,inner,ch),F32)],cost_estimate=cost(20000*length*ch,75*length*ch),compiler_params=PAR)(coef,x.reshape(8,inner,ch),kspec,fwd,inv)
    return s,y.reshape(length,ch)

def long_back(g,kspec,sspec,tables):
    fwd,inv,coef=tables
    length,ch=g.shape; inner=2*length//RADIX
    y,kg=pl.pallas_call(back_kernel,grid=(RADIX//4,),
        in_specs=[SM,whole((8,inner,ch)),step_of((2,2*inner,ch)),step_of((2,2*inner,ch)),step_of((2,2*inner,2*inner)),step_of((2,2*inner,2*inner))],
        out_specs=[whole((8,inner,ch)),whole((8,inner,ch))],
        out_shape=[jax.ShapeDtypeStruct((8,inner,ch),BF),jax.ShapeDtypeStruct((8,inner,ch),F32)],
        scratch_shapes=[pltpu.VMEM((2,2*inner,ch),BF),pltpu.VMEM((2,2*inner,ch),F32),pltpu.VMEM((2,2*inner,2*ch),BF),pltpu.VMEM((2,2*inner,2*ch),F32),pltpu.VMEM((8,inner,ch),F32)],cost_estimate=cost(27000*length*ch,100*length*ch),compiler_params=PAR)(coef,g.reshape(8,inner,ch),kspec,sspec,fwd,inv)
    return y.reshape(length,ch),kg.reshape(length,ch)

def ff_kernel(x_ref,g_ref,wu_ref,wd_ref,bu_ref,down_ref,gsec_ref,dwu_ref,dwd_ref,dbu_ref,a_ref,gu_ref):
    f=pl.program_id(0); rows=x_ref.shape[0]; step=256 if rows%256==0 else rows
    wu=wu_ref[...].reshape(-1,x_ref.shape[1]); wd=wd_ref[0]
    total=jnp.zeros(dbu_ref.shape[1:],F32)
    @pl.when(f==0)
    def _():
        down_ref[...]=jnp.zeros_like(down_ref)
        gsec_ref[...]=jnp.zeros_like(gsec_ref)
    for r in range(rows//step):
        at=pl.ds(r*step,step)
        up=lax.dot_general(x_ref[at,:],wu,(((1,),(1,)),((),())),preferred_element_type=F32)+bu_ref[0]
        ga=jnp.dot(g_ref[at,:],wd,preferred_element_type=F32)
        sq=up*up
        th=jnp.tanh(up*(GELU_A+(GELU_A*GELU_B)*sq))
        half_one=0.5+0.5*th
        a=(up*half_one).astype(BF)
        a_ref[at,:]=a
        slope=half_one+(up*half_one*(1.0-th))*(GELU_A+(3.0*GELU_A*GELU_B)*sq)
        gu=ga*slope
        total=total+jnp.sum(gu,axis=0,keepdims=True)
        gul=gu.astype(BF)
        gu_ref[at,:]=gul
        down_ref[at,:]+=lax.dot_general(a,wd,(((1,),(1,)),((),())),preferred_element_type=F32)
        gsec_ref[at,:]+=jnp.dot(gul,wu,preferred_element_type=F32)
    dbu_ref[0]=total
    dwu_ref[...]=lax.dot_general(gu_ref[...],x_ref[...],(((0,),(0,)),((),())),preferred_element_type=F32).astype(BF)
    dwd_ref[...]=lax.dot_general(g_ref[...],a_ref[...],(((0,),(0,)),((),())),preferred_element_type=F32).astype(BF)

GELU_A=0.7978845608
GELU_B=0.044715

def feed_forward(x,g,wu,wd,bu):
    rows,width=x.shape; hid=bu.size; blk=width; chunk=hid//wu.shape[0]; chunks=blk//chunk
    n=hid//blk
    return pl.pallas_call(ff_kernel,grid=(n,),
        in_specs=[whole((rows,width)),whole((rows,width)),pl.BlockSpec((chunks,chunk,width),lambda f:(f,0,0)),pl.BlockSpec((1,width,blk),lambda f:(f,0,0)),pl.BlockSpec((1,1,blk),lambda f:(f,0,0))],
        out_specs=[whole((rows,width)),whole((rows,width)),pl.BlockSpec((blk,width),lambda f:(f,0)),pl.BlockSpec((width,blk),lambda f:(0,f)),pl.BlockSpec((1,1,blk),lambda f:(f,0,0))],
        out_shape=[jax.ShapeDtypeStruct((rows,width),F32),jax.ShapeDtypeStruct((rows,width),F32),jax.ShapeDtypeStruct((hid,width),BF),jax.ShapeDtypeStruct((width,hid),BF),jax.ShapeDtypeStruct((n,1,blk),F32)],
        scratch_shapes=[pltpu.VMEM((rows,blk),BF),pltpu.VMEM((rows,blk),BF)],
        cost_estimate=cost(20*rows*width*hid,60*rows*hid),
        compiler_params=PAR)(x,g,wu,wd,bu.reshape(n,1,blk))

def tail_kernel(p_ref,gg_ref,jo_ref,cb_ref,gj_ref,af_ref,mk_ref,tap_ref,cbias_ref,skip_ref,
                gp_ref,sums_ref,pw_ref,gc_ref):
    b=pl.program_id(0); local=gg_ref.shape[1]; width=gg_ref.shape[2]; wide=3*width
    step=64 if local%64==0 else local; lanes=128
    @pl.when(b==0)
    def _():
        sums_ref[...]=jnp.zeros_like(sums_ref)
    @pl.loop(0,width//lanes)
    def _(j):
        def cols(s): return pl.ds(pl.multiple_of(s*width+j*lanes,lanes),lanes)
        c0=cols(0)
        for s in range(3):
            for r in range(-1,local//step):
                if r<0: pw_ref[s,0:16,:]=p_ref[0,0:16,cols(s)].astype(F32)
                else: pw_ref[s,16+r*step:16+(r+1)*step,:]=p_ref[0,16+r*step:16+(r+1)*step,cols(s)].astype(F32)
        tap=[[tap_ref[k:k+1,cols(s)] for k in range(3)] for s in range(3)]
        cbias=[cbias_ref[0:1,cols(s)] for s in range(3)]
        skip=skip_ref[0:1,c0]
        acc=[[jnp.zeros((8,lanes),F32) for _ in range(5)] for s in range(3)]
        def fold(v): return jnp.sum(v.reshape(-1,8,lanes),axis=0)
        for r in range(local//step):
            lo=r*step
            at=pl.ds(lo,step)
            sh=[[pw_ref[s,14+lo+k:14+lo+k+step,:] for k in range(3)] for s in range(3)]
            gate=[None]+[cbias[s]+tap[s][0]*sh[s][0]+tap[s][1]*sh[s][1]+tap[s][2]*sh[s][2] for s in (1,2)]
            gg=gg_ref[0,at,c0]
            gs=mk_ref[0,at,:]*(cb_ref[0,at,c0].astype(F32)+skip*gj_ref[0,at,c0].astype(F32))
            gc=[gg*jo_ref[0,at,c0].astype(F32),gs*gate[2],gs*gate[1]]
            for s in range(3):
                gc_ref[s,at,:]=gc[s]
                acc[s][0]=acc[s][0]+fold(gc[s])
                for k in range(3):
                    acc[s][1+k]=acc[s][1+k]+fold(gc[s]*sh[s][k])
        for s in range(3):
            gc_ref[s,local:local+8,:]=af_ref[0,:,cols(s)]
        for r in range(local//step):
            lo=r*step
            at=pl.ds(lo,step)
            mk=mk_ref[0,at,:]
            for s in range(3):
                gp=mk*(tap[s][2]*gc_ref[s,at,:]+tap[s][1]*gc_ref[s,lo+1:lo+1+step,:]+tap[s][0]*gc_ref[s,lo+2:lo+2+step,:])
                acc[s][4]=acc[s][4]+fold(gp)
                gp_ref[0,at,cols(s)]=gp.astype(BF)
        for s in range(3):
            for q in range(5):
                sums_ref[q:q+1,cols(s)]+=jnp.sum(acc[s][q],axis=0,keepdims=True)

def tail_back(p,gg,jo,cb,gj,af,mk,taps,cbias,skip):
    blocks,local,width=gg.shape; wide=3*width
    def blk(rows,cols): return pl.BlockSpec((1,rows,cols),lambda b:(b,0,0))
    return pl.pallas_call(tail_kernel,grid=(blocks,),
        in_specs=[blk(local+16,wide),blk(local,width),blk(local,width),blk(local,width),blk(local,width),blk(8,wide),blk(local,1),whole((3,wide)),whole((1,wide)),whole((1,width))],
        out_specs=[blk(local,wide),whole((8,wide))],
        out_shape=[jax.ShapeDtypeStruct((blocks,local,wide),BF),jax.ShapeDtypeStruct((8,wide),F32)],
        scratch_shapes=[pltpu.VMEM((3,local+16,128),F32),pltpu.VMEM((3,local+8,128),F32)],
        cost_estimate=cost(7000*blocks*local*wide,22*blocks*local*wide),compiler_params=PAR)(p,gg,jo,cb,gj,af,mk,taps,cbias,skip)

def front_kernel(t_ref,mk_ref,gain_ref,shift_ref,w_ref,bias_ref,tap_ref,cbias_ref,n_out,p_out,o_out,s_out,n_ref,p_ref):
    total=t_ref.shape[1]; width=t_ref.shape[2]; local=total-16
    step=48 if total%48==0 else 16
    gain=gain_ref[...]; shift=shift_ref[...]
    for r in range(total//step):
        at=pl.ds(r*step,step)
        x=t_ref[0,at,:].astype(F32)
        c=x-jnp.mean(x,axis=-1,keepdims=True)
        v=jnp.mean(c*c,axis=-1,keepdims=True)
        n_ref[at,:]=(c*lax.rsqrt(v+1e-05)*gain+shift).astype(BF)
    for s in range(3):
        cols=pl.ds(s*width,width)
        p_ref[:,cols]=mk_ref[0]*(lax.dot_general(n_ref[...],w_ref[cols,:],(((1,),(1,)),((),())),preferred_element_type=F32)+bias_ref[0:1,cols])
    n_out[0]=n_ref[16:,:]
    step=64 if local%64==0 else local; lanes=128
    @pl.loop(0,width//lanes)
    def _(j):
        def cols(s): return pl.ds(pl.multiple_of(s*width+j*lanes,lanes),lanes)
        tap=[[tap_ref[k:k+1,cols(s)] for k in range(3)] for s in range(3)]
        cbias=[cbias_ref[0:1,cols(s)] for s in range(3)]
        for s in range(3):
            p_out[0,0:16,cols(s)]=p_ref[0:16,cols(s)].astype(BF)
        for r in range(local//step):
            lo=r*step
            at=pl.ds(lo,step)
            conv=[]
            for s in range(3):
                mid=p_ref[16+lo:16+lo+step,cols(s)]
                p_out[0,16+lo:16+lo+step,cols(s)]=mid.astype(BF)
                conv.append(cbias[s]+tap[s][0]*p_ref[14+lo:14+lo+step,cols(s)]+tap[s][1]*p_ref[15+lo:15+lo+step,cols(s)]+tap[s][2]*mid)
            o_out[0,at,cols(0)]=conv[0].astype(BF)
            s_out[0,at,cols(0)]=(mk_ref[0,16+lo:16+lo+step,:]*conv[1]*conv[2]).astype(BF)

def front_part(tok,mk,gain,shift,w,bias,taps,cbias):
    blocks,total,width=tok.shape; wide=3*width; local=total-16
    def blk(rows,cols): return pl.BlockSpec((1,rows,cols),lambda b:(b,0,0))
    low=jax.ShapeDtypeStruct((blocks,local,width),BF)
    return pl.pallas_call(front_kernel,grid=(blocks,),
        in_specs=[blk(total,width),blk(total,1),whole((1,width)),whole((1,width)),whole((wide,width)),whole((1,wide)),whole((3,wide)),whole((1,wide))],
        out_specs=[blk(local,width),blk(total,wide),blk(local,width),blk(local,width)],
        out_shape=[low,jax.ShapeDtypeStruct((blocks,total,wide),BF),low,low],
        scratch_shapes=[pltpu.VMEM((total,width),BF),pltpu.VMEM((total,wide),F32)],
        cost_estimate=cost(7000*blocks*local*wide,22*blocks*local*wide),compiler_params=PAR)(tok,mk,gain,shift,w,bias,taps,cbias)

def net_places(emb,filt):
    second=-(-emb//8)*8
    return second,second+filt,second+2*filt

def filter_kernel_back(kg_ref,sh_ref,col_ref,hid_ref,m1_ref,m2_ref,f_ref,p1_ref,p2_ref,p3_ref,c1_ref,c2_ref,c3_ref,fr_ref,w2_ref,w3_ref,
                       colg_ref,net_ref):
    i=pl.program_id(0)
    fr=fr_ref[...]
    @pl.when(i==0)
    def _():
        colg_ref[...]=jnp.zeros_like(colg_ref)
        net_ref[...]=jnp.zeros_like(net_ref)
    emb=f_ref.shape[1]; filt=fr.shape[1]
    second_at,third_at,vec_at=net_places(emb,filt)
    def mul(a,b,da,db):
        def dot(u,v): return lax.dot_general(u,v,(((da,),(db,)),((),())),preferred_element_type=F32)
        ah,bh=a.astype(BF),b.astype(BF)
        al,bl=(a-ah.astype(F32)).astype(BF),(b-bh.astype(F32)).astype(BF)
        return dot(ah,bh)+(dot(ah,bl)+dot(al,bh))
    sg=kg_ref[...]*sh_ref[...]
    colg_ref[...]+=mul(sg,hid_ref[...],0,0)
    grad=mul(sg,col_ref[...],1,0)
    rate=jnp.zeros((1,fr.shape[1]),F32)
    for row,p_ref,c_ref,in_ref,w_ref,at in ((2,p3_ref,c3_ref,m2_ref,w3_ref,third_at),(1,p2_ref,c2_ref,m1_ref,w2_ref,second_at),(0,p1_ref,c1_ref,f_ref,None,0)):
        p=p_ref[...]
        turned=grad*c_ref[...]
        rate=rate+jnp.sum(turned*p,axis=0,keepdims=True)
        gp=turned*fr
        net_ref[vec_at+row:vec_at+row+1,:]+=jnp.sum(gp,axis=0,keepdims=True)
        net_ref[at:at+in_ref.shape[1],:]+=mul(in_ref[...],gp,0,0)
        if w_ref is not None: grad=mul(gp,w_ref[...],1,1)
    net_ref[vec_at+3:vec_at+4,:]+=rate

def filter_back(kg,sh,col,hid,m1,m2,feat,p1,p2,p3,c1,c2,c3,fr,w2,w3,multiple):
    length,ch=kg.shape; filt=hid.shape[1]; emb=feat.shape[1]; blk=512
    net=-(-(net_places(emb,filt)[2]+8)//multiple)*multiple
    def rows(c): return pl.BlockSpec((blk,c),lambda i:(i,0))
    def out(a,b): return jax.ShapeDtypeStruct((a,b),F32)
    return pl.pallas_call(filter_kernel_back,grid=(length//blk,),
        in_specs=[rows(ch),rows(ch),whole((ch,filt)),rows(filt),rows(filt),rows(filt),rows(emb),rows(filt),rows(filt),rows(filt),rows(filt),rows(filt),rows(filt),whole((1,filt)),whole((filt,filt)),whole((filt,filt))],
        out_specs=[whole((ch,filt)),whole((net,filt))],
        out_shape=[out(ch,filt),out(net,filt)],
        cost_estimate=cost(30000*length*ch,100*length*ch),compiler_params=PAR)(kg,sh,col,hid,m1,m2,feat,p1,p2,p3,c1,c2,c3,fr.reshape(1,-1),w2,w3)

def product(left, right):
    return jnp.dot(left, right, precision=lax.Precision.HIGHEST, preferred_element_type=jnp.float32)

def gelu_tanh(values):
    return jax.nn.gelu(values, approximate=True)

def filter_hidden(
    features,
    filter_entry_coefficients,
    filter_entry_offset,
    filter_second_coefficients,
    filter_second_offset,
    filter_third_coefficients,
    filter_third_offset,
    periodic_frequency,
):
    first = jnp.sin(
        periodic_frequency * (product(features, filter_entry_coefficients) + filter_entry_offset)
    )
    middle = jnp.sin(
        periodic_frequency * (product(first, filter_second_coefficients) + filter_second_offset)
    )
    return jnp.sin(
        periodic_frequency * (product(middle, filter_third_coefficients) + filter_third_offset)
    )

def modulation(length, model_width, offset, channels):
    standardized_values = jnp.arange(length).astype(jnp.float32) / (length - 1)
    slowest = math.log(0.01) / 1.5
    fastest = math.log(0.01) / 0.3
    columns = (offset + jnp.arange(channels)).astype(jnp.float32)
    decays = slowest + (fastest - slowest) * columns / (model_width - 1)
    return jnp.exp(-standardized_values[:, None] * jnp.abs(decays)[None, :]) + 0.05

def position_features(length, emb_width):
    band_count = (emb_width - 1) // 2
    places = np.arange(length, dtype=np.float64)
    band_rates = 0.0001 + (band_count - 1 - 0.0001) * np.arange(band_count) / (band_count - 1)
    phases = (2.0 * math.pi * places / length)[:, None] * band_rates[None, :]
    return np.concatenate(
        [(places / (length - 1))[:, None], np.cos(phases), -np.sin(phases)], axis=1
    ).astype(np.float32)


def pairs_of(count, mask):
    return [(i, i ^ mask) for i in range(count)]


def bit_of(me, bit):
    return (me >> bit) & 1


def grouped(bits):
    return [tuple(bits[i : i + 2]) for i in range(0, len(bits), 2)]


class Gather:
    flight = None

    def __init__(self, value, me, count, order, placed=True):
        self.placed = placed
        self.held, self.me, self.count, self.order = value, me, count, list(order)
        self.at = 0

    def give(self):
        return self.held

    def ways(self, given):
        return [(given, pairs_of(self.count, 1 << self.order[self.at]))]

    def receive(self, got):
        self.at += 1
        if self.at < len(self.order):
            self.held = jnp.concatenate([self.held, got[0]], axis=0)
        else:
            self.last = got[0]
            if self.placed:
                self.held = place_shards([self], self.me, self.count)

    @property
    def open(self):
        return self.at < len(self.order)


class Scatter:
    flight = None

    def __init__(self, value, me, count, order, keep):
        self.value, self.me, self.count, self.keep = value, me, count, keep
        self.order = [g if isinstance(g, tuple) else (g,) for g in order]
        self.rows, self.columns = value.shape[1:]
        self.left = [b for g in self.order for b in g]
        self.at = 0

    def give(self):
        group = self.order[self.at]
        size = 1 << len(group)
        low = 1 << sum(1 for b in self.left if b < group[0])
        cut = self.value.reshape(-1, size, low * self.rows, self.columns)
        at = (self.me >> group[0]) & (size - 1)
        self.mine = lax.dynamic_index_in_dim(cut, at, 1, keepdims=False)
        return tuple(
            lax.dynamic_index_in_dim(cut, at ^ m, 1, keepdims=False) for m in range(1, size)
        )

    def ways(self, given):
        group = self.order[self.at]
        self.left = [b for b in self.left if b not in group]
        return [
            (g, pairs_of(self.count, m << group[0])) for m, g in enumerate(given, start=1)
        ]

    def receive(self, got):
        self.at += 1
        self.value = self.mine.astype(F32)
        for g in got:
            self.value = self.value + g.astype(F32)
        if self.open:
            self.value = self.value.astype(self.keep)
        else:
            self.value = self.value.reshape(self.rows, self.columns)

    @property
    def open(self):
        return self.at < len(self.order)


class Swap:
    flight = None

    def __init__(self, value, me, count, bit):
        self.value, self.me, self.count, self.bit = value, me, count, bit
        self.open = True

    def give(self):
        return self.value

    def ways(self, given):
        return [(given, pairs_of(self.count, 1 << self.bit))]

    def receive(self, got):
        self.value = got[0]
        self.open = False


class Ring:
    flight = None

    def __init__(self, value, count, half, by):
        self.value, self.open = value, True
        self.pairs = []
        for i in range(count):
            group, r = divmod(i, half)
            self.pairs.append((i, group * half + (r + by) % half))

    def give(self):
        return self.value

    def ways(self, given):
        return [(given, self.pairs)]

    def receive(self, got):
        self.value = got[0]
        self.open = False


class Exchange:
    flight = None

    def __init__(self, value, add=True):
        self.value, self.open, self.add = value, True, add

    def give(self):
        return self.value

    def ways(self, given):
        return [(given, None)]

    def receive(self, got):
        self.value = jnp.sum(got[0], axis=0) if self.add else got[0]
        self.open = False


def send(*chains, state=()):
    chains = [c for c in chains if c.open]
    given = [c.give() for c in chains]
    tied = lax.optimization_barrier(tuple(state) + tuple(given))
    for c, g in zip(chains, tied[len(state) :]):
        c.flight = [
            lax.all_to_all(v, AXES, 0, 0, tiled=True)
            if pairs is None
            else lax.ppermute(v, AXES, pairs)
            for v, pairs in c.ways(g)
        ]
    return tied[: len(state)]


def meet(state, *chains):
    chains = [c for c in chains if c.flight]
    sizes = [len(c.flight) for c in chains]
    tied = lax.optimization_barrier(tuple(state) + tuple(v for c in chains for v in c.flight))
    at = len(state)
    for c, n in zip(chains, sizes):
        c.receive(tied[at : at + n])
        c.flight = None
        at += n
    return tied[: len(state)]


def drain(*chains):
    meet((), *chains)
    while any(c.open for c in chains):
        send(*chains)
        meet((), *chains)


def place_shards(chains, me, count):
    half = count // 2
    rows = chains[0].held.shape[0] // half
    widths = [c.held.shape[1] for c in chains]

    def from_device(order, i):
        return sum(((i >> p) & 1) << bit for p, bit in enumerate(order[:-1]))

    def kernel(me_ref, *refs):
        own = me_ref[0]
        out_ref = refs[-1]
        left = 0
        for n, c in enumerate(chains):
            columns = slice(left, left + widths[n])
            left += widths[n]
            for i in range(half):
                near = from_device(c.order, i)
                out_ref[jnp.bitwise_xor(own, near), :, columns] = refs[2 * n][i]
                other = near | (1 << c.order[-1])
                out_ref[jnp.bitwise_xor(own, other), :, columns] = refs[2 * n + 1][i]

    vmem = pl.BlockSpec(memory_space=pltpu.VMEM)
    operands = [v.reshape(half, rows, -1) for c in chains for v in (c.held, c.last)]
    return pl.pallas_call(
        kernel,
        in_specs=[SM] + [vmem] * len(operands),
        out_specs=vmem,
        out_shape=jax.ShapeDtypeStruct((count, rows, sum(widths)), chains[0].held.dtype),
        compiler_params=PAR,
    )(me.reshape(1).astype(jnp.int32), *operands)


def orders_of(count):
    bits = count.bit_length() - 1
    first = list(range(bits))
    second = list(range(bits))
    second[1], second[2] = second[2], second[1]
    return first, second


def normalise(values):
    centre = values - jnp.mean(values, axis=-1, keepdims=True)
    spread = jnp.mean(centre * centre, axis=-1, keepdims=True)
    rstd = lax.rsqrt(spread + 1e-05)
    return centre * rstd, rstd


def normalise_back(unit, rstd, incoming):
    return rstd * (
        incoming
        - jnp.mean(incoming, axis=-1, keepdims=True)
        - unit * jnp.mean(incoming * unit, axis=-1, keepdims=True)
    )


def dot_nt(left, right):
    return lax.dot_general(left, right, (((1,), (1,)), ((), ())), preferred_element_type=F32)


def dot_nn(left, right):
    return lax.dot_general(left, right, (((1,), (0,)), ((), ())), preferred_element_type=F32)


def dot_tn(left, right):
    return lax.dot_general(left, right, (((0,), (0,)), ((), ())), preferred_element_type=F32)


def per_device(
    block_input,
    slot_spans,
    output_adjoint,
    opening_scale_factor,
    opening_offset_vector,
    intake_coefficients,
    intake_offset,
    brief_filter_coefficients,
    brief_filter_offset,
    direct_path_factor,
    filter_final_coefficients,
    mixer_output_coefficients,
    mixer_output_offset,
    closing_scale_factor,
    closing_offset_vector,
    expand_coefficients,
    expand_offset,
    contract_coefficients,
    contract_offset,
    filter_entry_coefficients,
    filter_entry_offset,
    filter_second_coefficients,
    filter_second_offset,
    filter_third_coefficients,
    filter_third_offset,
    periodic_frequency,
):
    width = block_input.shape[2]
    local = block_input.shape[1]
    seq_count = lax.axis_size("seq")
    count = lax.axis_size("dp") * seq_count
    seq_index = lax.axis_index("seq")
    me = lax.axis_index("dp") * seq_count + seq_index
    half = seq_count // 2
    group_bits = half.bit_length() - 1
    rank = seq_index % half
    side = seq_index // half
    length = local * seq_count
    channels = width // half
    chan_start = rank * channels
    up, across = orders_of(count)
    down, back = up[::-1], across[::-1]
    tables = tuple(jnp.asarray(t) for t in dft_tables(length))

    vectors = (
        opening_scale_factor,
        opening_offset_vector,
        direct_path_factor,
        mixer_output_offset,
        closing_scale_factor,
        closing_offset_vector,
        contract_offset,
        intake_offset,
        brief_filter_offset,
        brief_filter_coefficients,
        expand_offset,
    )
    middle = width // 2
    far = half.bit_length() - 1
    intake_shard = intake_coefficients.T
    front = Gather(intake_shard[:, :middle], me, count, down, placed=False)
    rear = Gather(intake_shard[:, middle:], me, count, back, placed=False)
    bits = len(down)
    spread = list(range(1, bits)) + [0]
    final = Gather(filter_final_coefficients.T.astype(F32), me, count, spread)
    trade = Swap(
        lax.dynamic_index_in_dim(block_input, 1 - side, 0, keepdims=False), me, count, far
    )
    features = jnp.asarray(position_features(length, filter_entry_coefficients.shape[0]))
    send(final, front, rear)
    send(trade)
    later = jnp.concatenate(
        [expand_coefficients.T]
        + [
            contract_coefficients[q * width : (q + 1) * width].T
            for q in range(contract_coefficients.shape[0] // width)
        ]
        + [mixer_output_coefficients.T],
        axis=0,
    )
    frequency = periodic_frequency

    def layer(values, weights, offset):
        p = product(values, weights) + offset
        return p, jnp.sin(frequency * p), jnp.cos(frequency * p)

    p1, m1, c1 = layer(features, filter_entry_coefficients, filter_entry_offset)
    p1, m1, c1, later = meet((p1, m1, c1, later), final, front, rear)
    later = lax.all_gather(later, AXES, axis=0, tiled=False)
    (m1,) = send(final, front, rear, state=(m1,))
    p2, m2, c2 = layer(m1, filter_second_coefficients, filter_second_offset)
    p2, m2, c2 = meet((p2, m2, c2), final, front, rear)
    (m2,) = send(final, front, rear, state=(m2,))
    p3, hidden, c3 = layer(m2, filter_third_coefficients, filter_third_offset)
    pack = jnp.concatenate([v.astype(F32).reshape(-1) for v in vectors])
    used = pack.size
    pad = -used % 1024
    pack = jnp.concatenate([pack, jnp.zeros((pad,), F32)]).reshape(8, -1)
    p3, hidden, c3, pack = meet((p3, hidden, c3, pack), final)
    bundle = Gather(pack, me, count, spread)
    (hidden,) = send(final, bundle, state=(hidden,))
    shaping = modulation(length, width, chan_start, channels)
    (shaping,) = meet((shaping,), final, bundle, front, rear)
    (shaping,) = send(final, bundle, front, rear, state=(shaping,))
    own_rows = lax.dynamic_index_in_dim(block_input, side, 0, keepdims=False)
    (own_rows,) = meet((own_rows,), final, bundle, trade)
    drain(final)
    columns = lax.dynamic_slice_in_dim(final.held.reshape(width, -1), chan_start, channels, 0)
    (columns,) = send(bundle, state=(columns,))
    filter_kernel = (
        lax.dot_general(
            hidden,
            columns,
            (((1,), (1,)), ((), ())),
            precision=lax.Precision.HIGHEST,
            preferred_element_type=F32,
        )
        * shaping
    )
    (filter_kernel,) = meet((filter_kernel,), bundle)
    (filter_kernel,) = send(bundle, state=(filter_kernel,))
    kernel_spec = spectrum(filter_kernel, tables)
    tokens_low = jnp.concatenate([own_rows, trade.value], axis=0)
    kernel_spec, tokens_low = meet((kernel_spec, tokens_low), bundle, front, rear)
    blocks = tokens_low.reshape(2, local, width)
    ends = Ring(blocks[:, local - 16 :], count, half, 1)
    send(front, rear, bundle, ends)
    own_base = seq_index * local
    far_base = ((1 - side) * half + rank) * local
    span = lax.dynamic_index_in_dim(slot_spans, side, 0, keepdims=False)
    places = jnp.stack([own_base, far_base])[:, None] + jnp.arange(-16, local)
    mask_all = ((places >= span[0]) & (places < span[0] + span[1])).astype(F32)[:, :, None]
    row_mask = mask_all[:, 16:].reshape(-1, 1)
    tokens = tokens_low.astype(F32)
    (mask_all,) = meet((mask_all,), bundle, front, rear, ends)
    drain(bundle, front, rear)
    no_rows = jnp.zeros_like(ends.value[0])
    wrapped = jnp.stack(
        [
            jnp.where(side == 1, ends.value[1], no_rows),
            jnp.where(side == 0, ends.value[0], no_rows),
        ]
    )
    before = jnp.where(rank == 0, wrapped, ends.value)
    blocks = jnp.concatenate([before, blocks], axis=1)
    pack_full = bundle.held.reshape(count, -1)
    fields = []
    at = 0
    for v in vectors:
        part = pack_full[:, at : at + v.size]
        at += v.size
        if v.ndim == 1:
            fields.append(part.reshape(-1))
        else:
            fields.append(
                part.reshape(count, v.shape[0], -1).transpose(1, 0, 2).reshape(v.shape[0], -1)
            )
    (
        gain_one,
        shift_one,
        skip_gain,
        mix_bias,
        gain_two,
        shift_two,
        down_bias,
        intake_bias,
        conv_bias,
        conv_taps,
        up_bias,
    ) = fields
    intake_t = place_shards([front, rear], me, count).reshape(-1, width)
    trade_adj = Swap(
        lax.dynamic_index_in_dim(output_adjoint, 1 - side, 0, keepdims=False), me, count, far
    )
    send(trade_adj)

    rows = 2 * local
    normed_low, projected_all, outer_gate, signal = front_part(
        blocks,
        mask_all,
        gain_one.reshape(1, -1),
        shift_one.reshape(1, -1),
        intake_t,
        intake_bias.reshape(1, -1),
        conv_taps,
        conv_bias.reshape(1, -1),
    )
    normed_low = normed_low.reshape(rows, width)
    outer_gate = outer_gate.reshape(rows, width).astype(F32)
    signal = signal.reshape(rows, width)

    def traded(near, give):
        got = [near]
        for k in range(1, half):
            got.append(lax.ppermute(give(k), AXES, [(i, i ^ k) for i in range(count)]))
        if half == 2:
            return jnp.where(rank == 0, got[0], got[1]), jnp.where(rank == 0, got[1], got[0])
        stacked = jnp.take(jnp.stack(got), jnp.arange(half) ^ rank, axis=0)
        return tuple(stacked[k] for k in range(half))

    def to_channels(value):
        def give(k):
            return lax.dynamic_slice_in_dim(value, (rank ^ k) * channels, channels, 1)

        pieces = traded(give(0), give)
        first = [jnp.where(side == 0, p[:local], p[local:]) for p in pieces]
        second = [jnp.where(side == 0, p[local:], p[:local]) for p in pieces]
        return jnp.concatenate(first + second, axis=0)

    def to_rows(value):
        def give(k):
            first = lax.dynamic_slice_in_dim(value, (rank ^ k) * local, local, 0)
            second = lax.dynamic_slice_in_dim(value, (half + (rank ^ k)) * local, local, 0)
            return jnp.concatenate(
                [jnp.where(side == 0, first, second), jnp.where(side == 0, second, first)], axis=0
            )

        return jnp.concatenate(traded(give(0), give), axis=1)

    def blocks_of(value):
        return value.reshape(2, local, -1)

    sig_spec, carried_cols = long_conv(to_channels(signal), kernel_spec, tables)
    carried = to_rows(carried_cols.astype(BF)).astype(F32)
    signal_wide = signal.astype(F32)
    joined = carried + skip_gain * signal_wide
    joined_low = joined.astype(BF)
    gated_mix = (joined * outer_gate).astype(BF)
    (gated_mix,) = meet((gated_mix,), trade_adj)
    own_adj = lax.dynamic_index_in_dim(output_adjoint, side, 0, keepdims=False)
    adjoint = jnp.concatenate([own_adj, trade_adj.value], axis=0)
    ff_rows = expand_coefficients.shape[1]
    mix_rows = mixer_output_coefficients.shape[1]
    if ff_rows % 16 == 0:
        up_t = later
    else:
        up_t = later[:, :ff_rows]
    mix_t = later[:, later.shape[1] - mix_rows :].reshape(-1, width)
    folds = contract_coefficients.shape[0] // width
    down_t = (
        later[:, ff_rows : later.shape[1] - mix_rows]
        .reshape(count, folds, -1, width)
        .transpose(1, 0, 2, 3)
        .reshape(folds, width, width)
    )
    residual = tokens + dot_nt(gated_mix, mix_t) + mix_bias
    unit_two, rstd_two = normalise(residual)
    second_low = (unit_two * gain_two + shift_two).astype(BF)
    grad_out = row_mask * adjoint.astype(F32)
    grad_low = grad_out.astype(BF)
    down_proj, grad_second, up_grad, down_grad, up_bias_grad = feed_forward(
        second_low, grad_low, up_t, down_t, up_bias
    )
    up_bias_grad = up_bias_grad.reshape(-1)
    output = (row_mask * (residual + down_proj + down_bias)).astype(BF)

    up_sum = Scatter(up_grad.reshape(count, -1, width), me, count, across, BF)
    down_sum = Scatter(down_grad.reshape(count, -1, down_grad.shape[1]), me, count, up, BF)
    (grad_second,) = send(up_sum, down_sum, state=(grad_second,))
    down_bias_grad = jnp.sum(grad_out, axis=0)
    gain_two_grad = jnp.sum(grad_second * unit_two, axis=0)
    shift_two_grad = jnp.sum(grad_second, axis=0)
    grad_residual = grad_out + normalise_back(unit_two, rstd_two, grad_second * gain_two)
    mix_bias_grad = jnp.sum(grad_residual, axis=0)
    resid_low = grad_residual.astype(BF)
    mix_grad = dot_tn(resid_low, gated_mix).astype(BF)
    grad_gated = dot_nn(resid_low, mix_t)
    grad_joined = grad_gated * outer_gate
    grad_joined_low = grad_joined.astype(BF)
    skip_grad = jnp.sum(grad_joined * signal_wide, axis=0)
    (grad_joined_low, mix_grad) = meet((grad_joined_low, mix_grad), up_sum, down_sum)
    (grad_joined_low,) = send(up_sum, down_sum, state=(grad_joined_low,))
    conv_back_cols, kernel_grad = long_back(
        to_channels(grad_joined_low), kernel_spec, sig_spec, tables
    )
    conv_back_cols, kernel_grad = meet((conv_back_cols, kernel_grad), up_sum, down_sum)
    (conv_back_cols,) = send(up_sum, down_sum, state=(conv_back_cols,))
    conv_back_low = to_rows(conv_back_cols.astype(BF))
    conv_back = conv_back_low.astype(F32)
    first = blocks_of(grad_gated)[:, :2]
    first_signal = blocks_of(row_mask)[:, :2] * (
        blocks_of(conv_back)[:, :2] + skip_gain * blocks_of(grad_joined_low)[:, :2].astype(F32)
    )
    near = projected_all[:, 14:18, width:].astype(F32)
    first_gates = conv_bias[width:] + sum(
        conv_taps[k, width:] * near[:, k : k + 2] for k in range(3)
    )
    starts = Ring(
        jnp.concatenate(
            [
                first * blocks_of(joined_low)[:, :2].astype(F32),
                first_signal * first_gates[:, :, width:],
                first_signal * first_gates[:, :, :width],
            ],
            axis=2,
        ),
        count,
        half,
        -1,
    )
    send(starts)
    (conv_back_low,) = meet((conv_back_low,), starts)
    starts = starts.value
    trade_out = Swap(output[local:], me, count, far)
    wrapped_after = jnp.stack(
        [jnp.where(side == 0, starts[1], 0.0), jnp.where(side == 1, starts[0], 0.0)]
    )
    after = jnp.where(rank == half - 1, wrapped_after, starts)
    after = jnp.concatenate([after, jnp.zeros((2, 6, after.shape[2]), F32)], axis=1)
    grad_projected, sums = tail_back(
        projected_all,
        blocks_of(grad_gated),
        blocks_of(joined_low),
        blocks_of(conv_back_low),
        blocks_of(grad_joined_low),
        after,
        blocks_of(row_mask),
        conv_taps,
        conv_bias.reshape(1, -1),
        skip_gain.reshape(1, -1),
    )
    conv_bias_grad = sums[0]
    taps_grad = sums[1:4]
    intake_bias_grad = sums[4]
    projected_low = grad_projected.reshape(rows, -1)
    (projected_low,) = meet((projected_low,), up_sum, down_sum)
    (projected_low,) = send(
        up_sum, down_sum, trade_out, state=(projected_low,)
    )
    intake_grad = dot_tn(projected_low, normed_low).astype(BF).reshape(count, -1, width)
    intake_grad, projected_low = meet((intake_grad, projected_low))
    both_grad = jnp.concatenate([intake_grad, mix_grad.reshape(count, -1, width)], axis=1)
    front_sum = Scatter(both_grad[:, :, :middle], me, count, up, BF)
    rear_sum = Scatter(both_grad[:, :, middle:], me, count, across, BF)
    (projected_low,) = send(front_sum, rear_sum, state=(projected_low,))
    unit_one, rstd_one = normalise(tokens)
    grad_normed = dot_nn(projected_low, intake_t)
    gain_one_grad = jnp.sum(grad_normed * unit_one, axis=0)
    shift_one_grad = jnp.sum(grad_normed, axis=0)
    tokens_grad = (
        grad_residual + normalise_back(unit_one, rstd_one, grad_normed * gain_one)
    ).astype(BF)
    tokens_grad, kernel_grad = meet(
        (tokens_grad, kernel_grad), up_sum, down_sum, front_sum, rear_sum
    )
    (kernel_grad,) = send(
        up_sum, down_sum, front_sum, rear_sum, state=(kernel_grad,)
    )

    vector_grads = (
        gain_one_grad,
        shift_one_grad,
        skip_grad,
        mix_bias_grad,
        gain_two_grad,
        shift_two_grad,
        down_bias_grad,
        intake_bias_grad,
        conv_bias_grad,
        taps_grad,
        up_bias_grad,
    )
    pieces = []
    for g in vector_grads:
        if g.ndim == 1:
            pieces.append(g.reshape(count, -1))
        else:
            pieces.append(
                g.reshape(g.shape[0], count, -1).transpose(1, 0, 2).reshape(count, -1)
            )
    packed = jnp.concatenate(pieces + [jnp.zeros((count, pad), F32)], axis=1)
    bundle_sum = Exchange(packed.reshape(count, 8, -1))
    trade_tokens = Swap(tokens_grad[local:], me, count, far)
    (kernel_grad,) = send(bundle_sum, trade_tokens, state=(kernel_grad,))
    column_grad, net = filter_back(
        kernel_grad,
        shaping,
        columns,
        hidden,
        m1,
        m2,
        features,
        p1,
        p2,
        p3,
        c1,
        c2,
        c3,
        frequency,
        filter_second_coefficients,
        filter_third_coefficients,
        8 * count,
    )
    column_grad, net = meet(
        (column_grad, net), bundle_sum, front_sum, rear_sum, up_sum, down_sum, trade_out
    )
    filter_full = lax.dynamic_update_slice_in_dim(
        jnp.zeros((width, hidden.shape[1]), F32), column_grad, chan_start, 0
    )
    emb, filt = filter_entry_coefficients.shape
    share = filter_full.shape[0] // count
    final_sum = Exchange(
        jnp.concatenate(
            [filter_full.reshape(count, share, filt), net.reshape(count, -1, filt)], axis=1
        )
    )
    (filter_full,) = send(final_sum, state=(filter_full,))
    send(front_sum, rear_sum)
    meet((), front_sum, rear_sum, trade_tokens)
    send(front_sum, rear_sum)
    meet((), front_sum, rear_sum, final_sum)
    final_grad = final_sum.value[:share]
    net_part = final_sum.value[share:]
    net_all = Exchange(jnp.broadcast_to(net_part, (count,) + net_part.shape), add=False)
    send(net_all)
    send(front_sum, rear_sum)
    drain(net_all, bundle_sum, final_sum, front_sum, rear_sum, up_sum, down_sum, trade_tokens)
    summed = bundle_sum.value.reshape(-1)
    small = []
    at = 0
    for v in vectors:
        small.append(summed[at : at + v.size].reshape(v.shape))
        at += v.size
    total = net_all.value.reshape(-1, filt)
    second_at, third_at, vec_at = net_places(emb, filt)
    net_out = (
        total[:emb],
        total[vec_at],
        total[second_at : second_at + filt],
        total[vec_at + 1],
        total[third_at : third_at + filt],
        total[vec_at + 2],
        total[vec_at + 3],
    )
    both_shard = jnp.concatenate([front_sum.value, rear_sum.value], axis=1)
    intake_rows = intake_grad.shape[1]
    intake_shard_grad = both_shard[:intake_rows]

    def at_home(near, far_part):
        return jnp.where(side == 0, jnp.stack([near, far_part]), jnp.stack([far_part, near]))

    output_home = at_home(output[:local], trade_out.value)
    tokens_home = at_home(tokens_grad[:local], trade_tokens.value)
    return (
        output_home,
        tokens_home,
        small[0],
        small[1],
        intake_shard_grad.T,
        small[7],
        small[9],
        small[8],
        small[2],
        final_grad.T,
        both_shard[intake_rows:].T,
        small[3],
        small[4],
        small[5],
        up_sum.value.T,
        small[10],
        down_sum.value.T,
        small[6],
    ) + net_out

def solution(mesh):
    in_specs = (
        P("dp", "seq", None),
        P("dp", None),
        P("dp", "seq", None),
        P(("dp", "seq")),
        P(("dp", "seq")),
        P(None, ("dp", "seq")),
        P(("dp", "seq")),
        P(None, ("dp", "seq")),
        P(("dp", "seq")),
        P(("dp", "seq")),
        P(None, ("dp", "seq")),
        P(None, ("dp", "seq")),
        P(("dp", "seq")),
        P(("dp", "seq")),
        P(("dp", "seq")),
        P(None, ("dp", "seq")),
        P(("dp", "seq")),
        P(None, ("dp", "seq")),
        P(("dp", "seq")),
        P(),
        P(),
        P(),
        P(),
        P(),
        P(),
        P(),
    )
    out_specs = (
        P("dp", "seq", None),
        P("dp", "seq", None),
        P(("dp", "seq")),
        P(("dp", "seq")),
        P(None, ("dp", "seq")),
        P(("dp", "seq")),
        P(None, ("dp", "seq")),
        P(("dp", "seq")),
        P(("dp", "seq")),
        P(None, ("dp", "seq")),
        P(None, ("dp", "seq")),
        P(("dp", "seq")),
        P(("dp", "seq")),
        P(("dp", "seq")),
        P(None, ("dp", "seq")),
        P(("dp", "seq")),
        P(None, ("dp", "seq")),
        P(("dp", "seq")),
        P(),
        P(),
        P(),
        P(),
        P(),
        P(),
        P(),
    )
    return jax.shard_map(
        per_device, mesh=mesh, in_specs=in_specs, out_specs=out_specs, check_vma=False
    )
```

```python
import math

import jax
import jax.numpy as jnp
import ml_dtypes
import numpy as np
from jax import lax
from jax.experimental import pallas as pl
from jax.experimental.pallas import tpu as pltpu
from jax.sharding import PartitionSpec as P

AXES = ("dp", "seq")

F32=jnp.float32; BF=jnp.bfloat16
RADIX=16

def dft_tables(length):
    padded = 2*length
    inner = padded//RADIX
    pairs = RADIX//4
    half = RADIX//2
    m = np.arange(inner)
    mats=[]
    for p in range(pairs):
        for s in (p, half-1-p):
            k2 = 2*(RADIX*m+s)+1
            ang = np.pi*((k2[:,None]*m[None,:])%(2*padded))/padded
            c,sn=np.cos(ang),np.sin(ang)
            mats.append(np.block([[c,sn],[-sn,c]]))
    fwd=np.stack(mats).reshape(pairs,2,2*inner,2*inner)
    inv=np.swapaxes(fwd,-1,-2)/length
    r=np.arange(half)
    th=np.pi*(r[None,:]*(2*np.arange(pairs)[:,None]+1))/RADIX
    coef=np.concatenate([np.cos(th),np.sin(th)],axis=1).astype(np.float32)
    return fwd.astype(ml_dtypes.bfloat16),inv.astype(ml_dtypes.bfloat16),coef

def split_rows(x_ref,coef_ref,p,z_ref,inner):
    step=16
    @pl.loop(0,inner//step,unroll=True)
    def _(i):
        lo=pl.multiple_of(i*step,step)
        rows=pl.ds(lo,step); low=pl.ds(pl.multiple_of(inner+i*step,step),step)
        xs=[x_ref[r,rows,:].astype(F32) for r in range(8)]
        c=[coef_ref[p,r] for r in range(8)]; s=[coef_ref[p,8+r] for r in range(8)]
        ce=xs[0]+c[2]*xs[2]+c[4]*xs[4]+c[6]*xs[6]
        co=c[1]*xs[1]+c[3]*xs[3]+c[5]*xs[5]+c[7]*xs[7]
        se=s[2]*xs[2]+s[4]*xs[4]+s[6]*xs[6]
        so=s[1]*xs[1]+s[3]*xs[3]+s[5]*xs[5]+s[7]*xs[7]
        z_ref[0,rows,:]=(ce+co).astype(BF)
        z_ref[1,rows,:]=(ce-co).astype(BF)
        z_ref[0,low,:]=(-(se+so)).astype(BF)
        z_ref[1,low,:]=(se-so).astype(BF)

def join_rows(w_ref,coef_ref,p,acc_ref,inner,lanes):
    step=16
    @pl.loop(0,inner//step,unroll=True)
    def _(i):
        lo=pl.multiple_of(i*step,step)
        rows=pl.ds(lo,step); low=pl.ds(pl.multiple_of(inner+i*step,step),step)
        r0=w_ref[0,rows,lanes]; r1=w_ref[1,rows,lanes]
        i0=w_ref[0,low,lanes]; i1=w_ref[1,low,lanes]
        rs=(r0+r1,r0-r1); im=(i0-i1,i0+i1)
        for r in range(8):
            if r==0: term=rs[0]
            else: term=coef_ref[p,r]*rs[r%2]-coef_ref[p,8+r]*im[r%2]
            acc_ref[r,rows,:]=jnp.where(p==0,0.0,acc_ref[r,rows,:])+term

def spec_kernel(coef_ref,x_ref,f_ref,o_ref,z_ref):
    p=pl.program_id(0); inner=x_ref.shape[1]
    split_rows(x_ref,coef_ref,p,z_ref,inner)
    for j in range(2):
        o_ref[0,j]=jnp.dot(f_ref[0,j],z_ref[j],preferred_element_type=F32).astype(o_ref.dtype)

def conv_kernel(coef_ref,x_ref,k_ref,f_ref,b_ref,s_ref,y_ref,z_ref,w_ref,acc_ref):
    p=pl.program_id(0); inner=x_ref.shape[1]
    split_rows(x_ref,coef_ref,p,z_ref,inner)
    for j in range(2):
        w_ref[j]=jnp.dot(f_ref[0,j],z_ref[j],preferred_element_type=F32)
    step=16
    for j in range(2):
        @pl.loop(0,inner//step,unroll=True)
        def _(i):
            rows=pl.ds(pl.multiple_of(i*step,step),step); low=pl.ds(pl.multiple_of(inner+i*step,step),step)
            xr=w_ref[j,rows,:]; xi=w_ref[j,low,:]
            kr=k_ref[0,j,rows,:].astype(F32); ki=k_ref[0,j,low,:].astype(F32)
            s_ref[0,j,rows,:]=xr.astype(BF); s_ref[0,j,low,:]=xi.astype(BF)
            z_ref[j,rows,:]=(xr*kr-xi*ki).astype(BF)
            z_ref[j,low,:]=(xr*ki+xi*kr).astype(BF)
    for j in range(2):
        w_ref[j]=jnp.dot(b_ref[0,j],z_ref[j],preferred_element_type=F32)
    join_rows(w_ref,coef_ref,p,acc_ref,inner,slice(None))
    if y_ref is None: return
    @pl.when(p==pl.num_programs(0)-1)
    def _():
        @pl.loop(0,inner//step,unroll=True)
        def _(i):
            rows=pl.ds(pl.multiple_of(i*step,step),step)
            for r in range(8):
                y_ref[r,rows,:]=acc_ref[r,rows,:].astype(y_ref.dtype)

def back_kernel(coef_ref,g_ref,k_ref,s_ref,f_ref,b_ref,y_ref,kg_ref,z_ref,w_ref,q_ref,v_ref,acc_ref):
    p=pl.program_id(0); inner=g_ref.shape[1]; chans=g_ref.shape[2]
    split_rows(g_ref,coef_ref,p,z_ref,inner)
    for j in range(2):
        w_ref[j]=jnp.dot(f_ref[0,j],z_ref[j],preferred_element_type=F32)
    step=16
    for j in range(2):
        @pl.loop(0,inner//step,unroll=True)
        def _(i):
            rows=pl.ds(pl.multiple_of(i*step,step),step); low=pl.ds(pl.multiple_of(inner+i*step,step),step)
            gr=w_ref[j,rows,:]; gi=w_ref[j,low,:]
            kr=k_ref[0,j,rows,:].astype(F32); ki=k_ref[0,j,low,:].astype(F32)
            q_ref[j,rows,0:chans]=(gr*kr+gi*ki).astype(BF)
            q_ref[j,low,0:chans]=(gi*kr-gr*ki).astype(BF)
            kr=s_ref[0,j,rows,:].astype(F32); ki=s_ref[0,j,low,:].astype(F32)
            q_ref[j,rows,chans:2*chans]=(gr*kr+gi*ki).astype(BF)
            q_ref[j,low,chans:2*chans]=(gi*kr-gr*ki).astype(BF)
    for j in range(2):
        v_ref[j]=jnp.dot(b_ref[0,j],q_ref[j],preferred_element_type=F32)
    join_rows(v_ref,coef_ref,p,acc_ref,inner,slice(0,chans))
    join_rows(v_ref,coef_ref,p,kg_ref,inner,slice(chans,2*chans))
    if y_ref is None: return
    @pl.when(p==pl.num_programs(0)-1)
    def _():
        @pl.loop(0,inner//step,unroll=True)
        def _(i):
            rows=pl.ds(pl.multiple_of(i*step,step),step)
            for r in range(8):
                y_ref[r,rows,:]=acc_ref[r,rows,:].astype(y_ref.dtype)

def fill(place_ref,a_ref,b_ref,xs_ref):
    local=a_ref.shape[0]//2; inner=xs_ref.shape[1]; per=local//inner
    for rank in (0,1):
        for side in (0,1):
            @pl.when((place_ref[0]==rank)&(place_ref[1]==side))
            def _():
                for r in range(8):
                    j=r//per
                    src=a_ref if j%2==rank else b_ref
                    lo=(0 if j//2==side else local)+(r%per)*inner
                    xs_ref[r]=src[lo:lo+inner,:]

def spill(place_ref,acc_ref,keep_ref,give_ref):
    local=keep_ref.shape[0]//2; inner=acc_ref.shape[1]; per=local//inner
    for rank in (0,1):
        for side in (0,1):
            @pl.when((place_ref[0]==rank)&(place_ref[1]==side))
            def _():
                for r in range(8):
                    j=r//per
                    dst=keep_ref if j%2==rank else give_ref
                    lo=(0 if j//2==side else local)+(r%per)*inner
                    dst[lo:lo+inner,:]=acc_ref[r].astype(BF)

def paired_conv_kernel(place_ref,coef_ref,a_ref,o_ref,k_ref,f_ref,b_ref,s_ref,keep_ref,give_ref,xs_ref,z_ref,w_ref,acc_ref):
    @pl.when(pl.program_id(0)==0)
    def _(): fill(place_ref,a_ref,o_ref,xs_ref)
    conv_kernel(coef_ref,xs_ref,k_ref,f_ref,b_ref,s_ref,None,z_ref,w_ref,acc_ref)
    @pl.when(pl.program_id(0)==pl.num_programs(0)-1)
    def _(): spill(place_ref,acc_ref,keep_ref,give_ref)

def paired_back_kernel(place_ref,coef_ref,a_ref,o_ref,k_ref,s_ref,f_ref,b_ref,keep_ref,give_ref,kg_ref,xs_ref,z_ref,w_ref,q_ref,v_ref,acc_ref):
    @pl.when(pl.program_id(0)==0)
    def _(): fill(place_ref,a_ref,o_ref,xs_ref)
    back_kernel(coef_ref,xs_ref,k_ref,s_ref,f_ref,b_ref,None,kg_ref,z_ref,w_ref,q_ref,v_ref,acc_ref)
    @pl.when(pl.program_id(0)==pl.num_programs(0)-1)
    def _(): spill(place_ref,acc_ref,keep_ref,give_ref)

def cost(flops,moved):
    return pl.CostEstimate(flops=flops,bytes_accessed=moved,transcendentals=0)

PAR=pltpu.CompilerParams(vmem_limit_bytes=52<<20)
SM=pl.BlockSpec(memory_space=pltpu.SMEM)
def whole(shape): return pl.BlockSpec(shape,lambda p:(0,)*len(shape))
def step_of(shape): return pl.BlockSpec((1,)+shape,lambda p:(p,)+(0,)*len(shape))

def spectrum(x,tables):
    fwd,inv,coef=tables
    length,ch=x.shape; inner=2*length//RADIX
    return pl.pallas_call(spec_kernel,grid=(RADIX//4,),
        in_specs=[SM,whole((8,inner,ch)),step_of((2,2*inner,2*inner))],
        out_specs=step_of((2,2*inner,ch)),
        out_shape=jax.ShapeDtypeStruct((RADIX//4,2,2*inner,ch),F32),
        scratch_shapes=[pltpu.VMEM((2,2*inner,ch),BF)],cost_estimate=cost(10000*length*ch,40*length*ch),compiler_params=PAR)(coef,x.reshape(8,inner,ch),fwd)

def long_conv(x,kspec,tables):
    fwd,inv,coef=tables
    length,ch=x.shape; inner=2*length//RADIX
    s,y=pl.pallas_call(conv_kernel,grid=(RADIX//4,),
        in_specs=[SM,whole((8,inner,ch)),step_of((2,2*inner,ch)),step_of((2,2*inner,2*inner)),step_of((2,2*inner,2*inner))],
        out_specs=[step_of((2,2*inner,ch)),whole((8,inner,ch))],
        out_shape=[jax.ShapeDtypeStruct((RADIX//4,2,2*inner,ch),BF),jax.ShapeDtypeStruct((8,inner,ch),BF)],
        scratch_shapes=[pltpu.VMEM((2,2*inner,ch),BF),pltpu.VMEM((2,2*inner,ch),F32),pltpu.VMEM((8,inner,ch),F32)],cost_estimate=cost(20000*length*ch,75*length*ch),compiler_params=PAR)(coef,x.reshape(8,inner,ch),kspec,fwd,inv)
    return s,y.reshape(length,ch)

def long_back(g,kspec,sspec,tables):
    fwd,inv,coef=tables
    length,ch=g.shape; inner=2*length//RADIX
    y,kg=pl.pallas_call(back_kernel,grid=(RADIX//4,),
        in_specs=[SM,whole((8,inner,ch)),step_of((2,2*inner,ch)),step_of((2,2*inner,ch)),step_of((2,2*inner,2*inner)),step_of((2,2*inner,2*inner))],
        out_specs=[whole((8,inner,ch)),whole((8,inner,ch))],
        out_shape=[jax.ShapeDtypeStruct((8,inner,ch),BF),jax.ShapeDtypeStruct((8,inner,ch),F32)],
        scratch_shapes=[pltpu.VMEM((2,2*inner,ch),BF),pltpu.VMEM((2,2*inner,ch),F32),pltpu.VMEM((2,2*inner,2*ch),BF),pltpu.VMEM((2,2*inner,2*ch),F32),pltpu.VMEM((8,inner,ch),F32)],cost_estimate=cost(27000*length*ch,100*length*ch),compiler_params=PAR)(coef,g.reshape(8,inner,ch),kspec,sspec,fwd,inv)
    return y.reshape(length,ch),kg.reshape(length,ch)


def paired_conv(place,near,other,kspec,tables):
    fwd,inv,coef=tables
    rows,ch=near.shape; inner=fwd.shape[-1]//2; length=8*inner
    low=jax.ShapeDtypeStruct((rows,ch),BF)
    return pl.pallas_call(paired_conv_kernel,grid=(RADIX//4,),
        in_specs=[SM,SM,whole((rows,ch)),whole((rows,ch)),step_of((2,2*inner,ch)),step_of((2,2*inner,2*inner)),step_of((2,2*inner,2*inner))],
        out_specs=[step_of((2,2*inner,ch)),whole((rows,ch)),whole((rows,ch))],
        out_shape=[jax.ShapeDtypeStruct((RADIX//4,2,2*inner,ch),BF),low,low],
        scratch_shapes=[pltpu.VMEM((8,inner,ch),BF),pltpu.VMEM((2,2*inner,ch),BF),pltpu.VMEM((2,2*inner,ch),F32),pltpu.VMEM((8,inner,ch),F32)],
        cost_estimate=cost(20000*length*ch,75*length*ch),compiler_params=PAR)(place,coef,near,other,kspec,fwd,inv)

def paired_back(place,near,other,kspec,sspec,tables):
    fwd,inv,coef=tables
    rows,ch=near.shape; inner=fwd.shape[-1]//2; length=8*inner
    low=jax.ShapeDtypeStruct((rows,ch),BF)
    keep,give,kg=pl.pallas_call(paired_back_kernel,grid=(RADIX//4,),
        in_specs=[SM,SM,whole((rows,ch)),whole((rows,ch)),step_of((2,2*inner,ch)),step_of((2,2*inner,ch)),step_of((2,2*inner,2*inner)),step_of((2,2*inner,2*inner))],
        out_specs=[whole((rows,ch)),whole((rows,ch)),whole((8,inner,ch))],
        out_shape=[low,low,jax.ShapeDtypeStruct((8,inner,ch),F32)],
        scratch_shapes=[pltpu.VMEM((8,inner,ch),BF),pltpu.VMEM((2,2*inner,ch),BF),pltpu.VMEM((2,2*inner,ch),F32),pltpu.VMEM((2,2*inner,2*ch),BF),pltpu.VMEM((2,2*inner,2*ch),F32),pltpu.VMEM((8,inner,ch),F32)],
        cost_estimate=cost(27000*length*ch,100*length*ch),compiler_params=PAR)(place,coef,near,other,kspec,sspec,fwd,inv)
    return keep,give,kg.reshape(length,ch)

def ff_kernel(x_ref,g_ref,wu_ref,wd_ref,bu_ref,down_ref,gsec_ref,dwu_ref,dwd_ref,dbu_ref,a_ref,gu_ref):
    f=pl.program_id(0); rows=x_ref.shape[0]; step=256 if rows%256==0 else rows
    wu=wu_ref[...].reshape(-1,x_ref.shape[1]); wd=wd_ref[0]
    total=jnp.zeros(dbu_ref.shape[1:],F32)
    @pl.when(f==0)
    def _():
        down_ref[...]=jnp.zeros_like(down_ref)
        gsec_ref[...]=jnp.zeros_like(gsec_ref)
    for r in range(rows//step):
        at=pl.ds(r*step,step)
        up=lax.dot_general(x_ref[at,:],wu,(((1,),(1,)),((),())),preferred_element_type=F32)+bu_ref[0]
        ga=jnp.dot(g_ref[at,:],wd,preferred_element_type=F32)
        sq=up*up
        th=jnp.tanh(up*(GELU_A+(GELU_A*GELU_B)*sq))
        half_one=0.5+0.5*th
        a=(up*half_one).astype(BF)
        a_ref[at,:]=a
        slope=half_one+(up*half_one*(1.0-th))*(GELU_A+(3.0*GELU_A*GELU_B)*sq)
        gu=ga*slope
        total=total+jnp.sum(gu,axis=0,keepdims=True)
        gul=gu.astype(BF)
        gu_ref[at,:]=gul
        down_ref[at,:]+=lax.dot_general(a,wd,(((1,),(1,)),((),())),preferred_element_type=F32)
        gsec_ref[at,:]+=jnp.dot(gul,wu,preferred_element_type=F32)
    dbu_ref[0]=total
    dwu_ref[...]=lax.dot_general(gu_ref[...],x_ref[...],(((0,),(0,)),((),())),preferred_element_type=F32).astype(BF)
    dwd_ref[...]=lax.dot_general(g_ref[...],a_ref[...],(((0,),(0,)),((),())),preferred_element_type=F32).astype(BF)

GELU_A=0.7978845608
GELU_B=0.044715

def feed_forward(x,g,wu,wd,bu):
    rows,width=x.shape; hid=bu.size; blk=width; chunk=hid//wu.shape[0]; chunks=blk//chunk
    n=hid//blk
    return pl.pallas_call(ff_kernel,grid=(n,),
        in_specs=[whole((rows,width)),whole((rows,width)),pl.BlockSpec((chunks,chunk,width),lambda f:(f,0,0)),pl.BlockSpec((1,width,blk),lambda f:(f,0,0)),pl.BlockSpec((1,1,blk),lambda f:(f,0,0))],
        out_specs=[whole((rows,width)),whole((rows,width)),pl.BlockSpec((blk,width),lambda f:(f,0)),pl.BlockSpec((width,blk),lambda f:(0,f)),pl.BlockSpec((1,1,blk),lambda f:(f,0,0))],
        out_shape=[jax.ShapeDtypeStruct((rows,width),F32),jax.ShapeDtypeStruct((rows,width),F32),jax.ShapeDtypeStruct((hid,width),BF),jax.ShapeDtypeStruct((width,hid),BF),jax.ShapeDtypeStruct((n,1,blk),F32)],
        scratch_shapes=[pltpu.VMEM((rows,blk),BF),pltpu.VMEM((rows,blk),BF)],
        cost_estimate=cost(20*rows*width*hid,60*rows*hid),
        compiler_params=PAR)(x,g,wu,wd,bu.reshape(n,1,blk))

def tail_kernel(p_ref,gg_ref,jo_ref,cb_ref,gj_ref,af_ref,mk_ref,tap_ref,cbias_ref,skip_ref,
                gp_ref,sums_ref,pw_ref,gc_ref):
    b=pl.program_id(0); local=gg_ref.shape[1]; width=gg_ref.shape[2]; wide=3*width
    step=64 if local%64==0 else local; lanes=128
    @pl.when(b==0)
    def _():
        sums_ref[...]=jnp.zeros_like(sums_ref)
    @pl.loop(0,width//lanes)
    def _(j):
        def cols(s): return pl.ds(pl.multiple_of(s*width+j*lanes,lanes),lanes)
        c0=cols(0)
        for s in range(3):
            for r in range(-1,local//step):
                if r<0: pw_ref[s,0:16,:]=p_ref[0,0:16,cols(s)].astype(F32)
                else: pw_ref[s,16+r*step:16+(r+1)*step,:]=p_ref[0,16+r*step:16+(r+1)*step,cols(s)].astype(F32)
        tap=[[tap_ref[k:k+1,cols(s)] for k in range(3)] for s in range(3)]
        cbias=[cbias_ref[0:1,cols(s)] for s in range(3)]
        skip=skip_ref[0:1,c0]
        acc=[[jnp.zeros((8,lanes),F32) for _ in range(5)] for s in range(3)]
        def fold(v): return jnp.sum(v.reshape(-1,8,lanes),axis=0)
        for r in range(local//step):
            lo=r*step
            at=pl.ds(lo,step)
            sh=[[pw_ref[s,14+lo+k:14+lo+k+step,:] for k in range(3)] for s in range(3)]
            gate=[None]+[cbias[s]+tap[s][0]*sh[s][0]+tap[s][1]*sh[s][1]+tap[s][2]*sh[s][2] for s in (1,2)]
            gg=gg_ref[0,at,c0]
            gs=mk_ref[0,at,:]*(cb_ref[0,at,c0].astype(F32)+skip*gj_ref[0,at,c0].astype(F32))
            gc=[gg*jo_ref[0,at,c0].astype(F32),gs*gate[2],gs*gate[1]]
            for s in range(3):
                gc_ref[s,at,:]=gc[s]
                acc[s][0]=acc[s][0]+fold(gc[s])
                for k in range(3):
                    acc[s][1+k]=acc[s][1+k]+fold(gc[s]*sh[s][k])
        for s in range(3):
            gc_ref[s,local:local+8,:]=af_ref[0,:,cols(s)]
        for r in range(local//step):
            lo=r*step
            at=pl.ds(lo,step)
            mk=mk_ref[0,at,:]
            for s in range(3):
                gp=mk*(tap[s][2]*gc_ref[s,at,:]+tap[s][1]*gc_ref[s,lo+1:lo+1+step,:]+tap[s][0]*gc_ref[s,lo+2:lo+2+step,:])
                acc[s][4]=acc[s][4]+fold(gp)
                gp_ref[0,at,cols(s)]=gp.astype(BF)
        for s in range(3):
            for q in range(5):
                sums_ref[q:q+1,cols(s)]+=jnp.sum(acc[s][q],axis=0,keepdims=True)

def tail_back(p,gg,jo,cb,gj,af,mk,taps,cbias,skip):
    blocks,local,width=gg.shape; wide=3*width
    def blk(rows,cols): return pl.BlockSpec((1,rows,cols),lambda b:(b,0,0))
    return pl.pallas_call(tail_kernel,grid=(blocks,),
        in_specs=[blk(local+16,wide),blk(local,width),blk(local,width),blk(local,width),blk(local,width),blk(8,wide),blk(local,1),whole((3,wide)),whole((1,wide)),whole((1,width))],
        out_specs=[blk(local,wide),whole((8,wide))],
        out_shape=[jax.ShapeDtypeStruct((blocks,local,wide),BF),jax.ShapeDtypeStruct((8,wide),F32)],
        scratch_shapes=[pltpu.VMEM((3,local+16,128),F32),pltpu.VMEM((3,local+8,128),F32)],
        cost_estimate=cost(7000*blocks*local*wide,22*blocks*local*wide),compiler_params=PAR)(p,gg,jo,cb,gj,af,mk,taps,cbias,skip)

def front_kernel(t_ref,mk_ref,gain_ref,shift_ref,w_ref,bias_ref,tap_ref,cbias_ref,n_out,p_out,o_out,s_out,n_ref,p_ref):
    total=t_ref.shape[1]; width=t_ref.shape[2]; local=total-16
    step=48 if total%48==0 else 16
    gain=gain_ref[...]; shift=shift_ref[...]
    for r in range(total//step):
        at=pl.ds(r*step,step)
        x=t_ref[0,at,:].astype(F32)
        c=x-jnp.mean(x,axis=-1,keepdims=True)
        v=jnp.mean(c*c,axis=-1,keepdims=True)
        n_ref[at,:]=(c*lax.rsqrt(v+1e-05)*gain+shift).astype(BF)
    for s in range(3):
        cols=pl.ds(s*width,width)
        p_ref[:,cols]=mk_ref[0]*(lax.dot_general(n_ref[...],w_ref[cols,:],(((1,),(1,)),((),())),preferred_element_type=F32)+bias_ref[0:1,cols])
    n_out[0]=n_ref[16:,:]
    step=64 if local%64==0 else local; lanes=128
    @pl.loop(0,width//lanes)
    def _(j):
        def cols(s): return pl.ds(pl.multiple_of(s*width+j*lanes,lanes),lanes)
        tap=[[tap_ref[k:k+1,cols(s)] for k in range(3)] for s in range(3)]
        cbias=[cbias_ref[0:1,cols(s)] for s in range(3)]
        for s in range(3):
            p_out[0,0:16,cols(s)]=p_ref[0:16,cols(s)].astype(BF)
        for r in range(local//step):
            lo=r*step
            at=pl.ds(lo,step)
            conv=[]
            for s in range(3):
                mid=p_ref[16+lo:16+lo+step,cols(s)]
                p_out[0,16+lo:16+lo+step,cols(s)]=mid.astype(BF)
                conv.append(cbias[s]+tap[s][0]*p_ref[14+lo:14+lo+step,cols(s)]+tap[s][1]*p_ref[15+lo:15+lo+step,cols(s)]+tap[s][2]*mid)
            o_out[0,at,cols(0)]=conv[0].astype(BF)
            s_out[0,at,cols(0)]=(mk_ref[0,16+lo:16+lo+step,:]*conv[1]*conv[2]).astype(BF)

def front_part(tok,mk,gain,shift,w,bias,taps,cbias):
    blocks,total,width=tok.shape; wide=3*width; local=total-16
    def blk(rows,cols): return pl.BlockSpec((1,rows,cols),lambda b:(b,0,0))
    low=jax.ShapeDtypeStruct((blocks,local,width),BF)
    return pl.pallas_call(front_kernel,grid=(blocks,),
        in_specs=[blk(total,width),blk(total,1),whole((1,width)),whole((1,width)),whole((wide,width)),whole((1,wide)),whole((3,wide)),whole((1,wide))],
        out_specs=[blk(local,width),blk(total,wide),blk(local,width),blk(local,width)],
        out_shape=[low,jax.ShapeDtypeStruct((blocks,total,wide),BF),low,low],
        scratch_shapes=[pltpu.VMEM((total,width),BF),pltpu.VMEM((total,wide),F32)],
        cost_estimate=cost(7000*blocks*local*wide,22*blocks*local*wide),compiler_params=PAR)(tok,mk,gain,shift,w,bias,taps,cbias)

def net_places(emb,filt):
    second=-(-emb//8)*8
    return second,second+filt,second+2*filt

def filter_kernel_back(kg_ref,sh_ref,col_ref,hid_ref,m1_ref,m2_ref,f_ref,p1_ref,p2_ref,p3_ref,c1_ref,c2_ref,c3_ref,fr_ref,w2_ref,w3_ref,
                       colg_ref,net_ref):
    i=pl.program_id(0)
    fr=fr_ref[...]
    @pl.when(i==0)
    def _():
        colg_ref[...]=jnp.zeros_like(colg_ref)
        net_ref[...]=jnp.zeros_like(net_ref)
    emb=f_ref.shape[1]; filt=fr.shape[1]
    second_at,third_at,vec_at=net_places(emb,filt)
    def mul(a,b,da,db):
        def dot(u,v): return lax.dot_general(u,v,(((da,),(db,)),((),())),preferred_element_type=F32)
        ah,bh=a.astype(BF),b.astype(BF)
        al,bl=(a-ah.astype(F32)).astype(BF),(b-bh.astype(F32)).astype(BF)
        return dot(ah,bh)+(dot(ah,bl)+dot(al,bh))
    sg=kg_ref[...]*sh_ref[...]
    colg_ref[...]+=mul(sg,hid_ref[...],0,0)
    grad=mul(sg,col_ref[...],1,0)
    rate=jnp.zeros((1,fr.shape[1]),F32)
    for row,p_ref,c_ref,in_ref,w_ref,at in ((2,p3_ref,c3_ref,m2_ref,w3_ref,third_at),(1,p2_ref,c2_ref,m1_ref,w2_ref,second_at),(0,p1_ref,c1_ref,f_ref,None,0)):
        p=p_ref[...]
        turned=grad*c_ref[...]
        rate=rate+jnp.sum(turned*p,axis=0,keepdims=True)
        gp=turned*fr
        net_ref[vec_at+row:vec_at+row+1,:]+=jnp.sum(gp,axis=0,keepdims=True)
        net_ref[at:at+in_ref.shape[1],:]+=mul(in_ref[...],gp,0,0)
        if w_ref is not None: grad=mul(gp,w_ref[...],1,1)
    net_ref[vec_at+3:vec_at+4,:]+=rate

def filter_back(kg,sh,col,hid,m1,m2,feat,p1,p2,p3,c1,c2,c3,fr,w2,w3,multiple):
    length,ch=kg.shape; filt=hid.shape[1]; emb=feat.shape[1]; blk=512
    net=-(-(net_places(emb,filt)[2]+8)//multiple)*multiple
    def rows(c): return pl.BlockSpec((blk,c),lambda i:(i,0))
    def out(a,b): return jax.ShapeDtypeStruct((a,b),F32)
    return pl.pallas_call(filter_kernel_back,grid=(length//blk,),
        in_specs=[rows(ch),rows(ch),whole((ch,filt)),rows(filt),rows(filt),rows(filt),rows(emb),rows(filt),rows(filt),rows(filt),rows(filt),rows(filt),rows(filt),whole((1,filt)),whole((filt,filt)),whole((filt,filt))],
        out_specs=[whole((ch,filt)),whole((net,filt))],
        out_shape=[out(ch,filt),out(net,filt)],
        cost_estimate=cost(30000*length*ch,100*length*ch),compiler_params=PAR)(kg,sh,col,hid,m1,m2,feat,p1,p2,p3,c1,c2,c3,fr.reshape(1,-1),w2,w3)

def product(left, right):
    return jnp.dot(left, right, precision=lax.Precision.HIGHEST, preferred_element_type=jnp.float32)

def gelu_tanh(values):
    return jax.nn.gelu(values, approximate=True)

def filter_hidden(
    features,
    filter_entry_coefficients,
    filter_entry_offset,
    filter_second_coefficients,
    filter_second_offset,
    filter_third_coefficients,
    filter_third_offset,
    periodic_frequency,
):
    first = jnp.sin(
        periodic_frequency * (product(features, filter_entry_coefficients) + filter_entry_offset)
    )
    middle = jnp.sin(
        periodic_frequency * (product(first, filter_second_coefficients) + filter_second_offset)
    )
    return jnp.sin(
        periodic_frequency * (product(middle, filter_third_coefficients) + filter_third_offset)
    )

def modulation(length, model_width, offset, channels):
    standardized_values = jnp.arange(length).astype(jnp.float32) / (length - 1)
    slowest = math.log(0.01) / 1.5
    fastest = math.log(0.01) / 0.3
    columns = (offset + jnp.arange(channels)).astype(jnp.float32)
    decays = slowest + (fastest - slowest) * columns / (model_width - 1)
    return jnp.exp(-standardized_values[:, None] * jnp.abs(decays)[None, :]) + 0.05

def position_features(length, emb_width):
    band_count = (emb_width - 1) // 2
    places = np.arange(length, dtype=np.float64)
    band_rates = 0.0001 + (band_count - 1 - 0.0001) * np.arange(band_count) / (band_count - 1)
    phases = (2.0 * math.pi * places / length)[:, None] * band_rates[None, :]
    return np.concatenate(
        [(places / (length - 1))[:, None], np.cos(phases), -np.sin(phases)], axis=1
    ).astype(np.float32)


def pairs_of(count, mask):
    return [(i, i ^ mask) for i in range(count)]


def bit_of(me, bit):
    return (me >> bit) & 1


def grouped(bits):
    return [tuple(bits[i : i + 2]) for i in range(0, len(bits), 2)]


class Gather:
    flight = None

    def __init__(self, value, me, count, order, placed=True):
        self.placed = placed
        self.held, self.me, self.count, self.order = value, me, count, list(order)
        self.at = 0

    def give(self):
        return self.held

    def ways(self, given):
        return [(given, pairs_of(self.count, 1 << self.order[self.at]))]

    def receive(self, got):
        self.at += 1
        if self.at < len(self.order):
            self.held = jnp.concatenate([self.held, got[0]], axis=0)
        else:
            self.last = got[0]
            if self.placed:
                self.held = place_shards([self], self.me, self.count)

    @property
    def open(self):
        return self.at < len(self.order)


class Scatter:
    flight = None

    def __init__(self, value, me, count, order, keep):
        self.value, self.me, self.count, self.keep = value, me, count, keep
        self.order = [g if isinstance(g, tuple) else (g,) for g in order]
        self.rows, self.columns = value.shape[1:]
        self.left = [b for g in self.order for b in g]
        self.at = 0

    def give(self):
        group = self.order[self.at]
        size = 1 << len(group)
        low = 1 << sum(1 for b in self.left if b < group[0])
        cut = self.value.reshape(-1, size, low * self.rows, self.columns)
        at = (self.me >> group[0]) & (size - 1)
        self.mine = lax.dynamic_index_in_dim(cut, at, 1, keepdims=False)
        return tuple(
            lax.dynamic_index_in_dim(cut, at ^ m, 1, keepdims=False) for m in range(1, size)
        )

    def ways(self, given):
        group = self.order[self.at]
        self.left = [b for b in self.left if b not in group]
        return [
            (g, pairs_of(self.count, m << group[0])) for m, g in enumerate(given, start=1)
        ]

    def receive(self, got):
        self.at += 1
        self.value = self.mine.astype(F32)
        for g in got:
            self.value = self.value + g.astype(F32)
        if self.open:
            self.value = self.value.astype(self.keep)
        else:
            self.value = self.value.reshape(self.rows, self.columns)

    @property
    def open(self):
        return self.at < len(self.order)


class Swap:
    flight = None

    def __init__(self, value, me, count, bit):
        self.value, self.me, self.count, self.bit = value, me, count, bit
        self.open = True

    def give(self):
        return self.value

    def ways(self, given):
        return [(given, pairs_of(self.count, 1 << self.bit))]

    def receive(self, got):
        self.value = got[0]
        self.open = False


class Ring:
    flight = None

    def __init__(self, value, count, half, by):
        self.value, self.open = value, True
        self.pairs = []
        for i in range(count):
            group, r = divmod(i, half)
            self.pairs.append((i, group * half + (r + by) % half))

    def give(self):
        return self.value

    def ways(self, given):
        return [(given, self.pairs)]

    def receive(self, got):
        self.value = got[0]
        self.open = False


class Exchange:
    flight = None

    def __init__(self, value, add=True):
        self.value, self.open, self.add = value, True, add

    def give(self):
        return self.value

    def ways(self, given):
        return [(given, None)]

    def receive(self, got):
        self.value = jnp.sum(got[0], axis=0) if self.add else got[0]
        self.open = False


def send(*chains, state=()):
    chains = [c for c in chains if c.open]
    given = [c.give() for c in chains]
    tied = lax.optimization_barrier(tuple(state) + tuple(given))
    for c, g in zip(chains, tied[len(state) :]):
        c.flight = [
            lax.all_to_all(v, AXES, 0, 0, tiled=True)
            if pairs is None
            else lax.ppermute(v, AXES, pairs)
            for v, pairs in c.ways(g)
        ]
    return tied[: len(state)]


def meet(state, *chains):
    chains = [c for c in chains if c.flight]
    sizes = [len(c.flight) for c in chains]
    tied = lax.optimization_barrier(tuple(state) + tuple(v for c in chains for v in c.flight))
    at = len(state)
    for c, n in zip(chains, sizes):
        c.receive(tied[at : at + n])
        c.flight = None
        at += n
    return tied[: len(state)]


def drain(*chains):
    meet((), *chains)
    while any(c.open for c in chains):
        send(*chains)
        meet((), *chains)


def place_shards(chains, me, count):
    half = count // 2
    rows = chains[0].held.shape[0] // half
    widths = [c.held.shape[1] for c in chains]

    def from_device(order, i):
        return sum(((i >> p) & 1) << bit for p, bit in enumerate(order[:-1]))

    def kernel(me_ref, *refs):
        own = me_ref[0]
        out_ref = refs[-1]
        left = 0
        for n, c in enumerate(chains):
            columns = slice(left, left + widths[n])
            left += widths[n]
            for i in range(half):
                near = from_device(c.order, i)
                out_ref[jnp.bitwise_xor(own, near), :, columns] = refs[2 * n][i]
                other = near | (1 << c.order[-1])
                out_ref[jnp.bitwise_xor(own, other), :, columns] = refs[2 * n + 1][i]

    vmem = pl.BlockSpec(memory_space=pltpu.VMEM)
    operands = [v.reshape(half, rows, -1) for c in chains for v in (c.held, c.last)]
    return pl.pallas_call(
        kernel,
        in_specs=[SM] + [vmem] * len(operands),
        out_specs=vmem,
        out_shape=jax.ShapeDtypeStruct((count, rows, sum(widths)), chains[0].held.dtype),
        compiler_params=PAR,
    )(me.reshape(1).astype(jnp.int32), *operands)


def orders_of(count):
    bits = count.bit_length() - 1
    first = list(range(bits))
    second = list(range(bits))
    second[1], second[2] = second[2], second[1]
    return first, second


def normalise(values):
    centre = values - jnp.mean(values, axis=-1, keepdims=True)
    spread = jnp.mean(centre * centre, axis=-1, keepdims=True)
    rstd = lax.rsqrt(spread + 1e-05)
    return centre * rstd, rstd


def normalise_back(unit, rstd, incoming):
    return rstd * (
        incoming
        - jnp.mean(incoming, axis=-1, keepdims=True)
        - unit * jnp.mean(incoming * unit, axis=-1, keepdims=True)
    )


def dot_nt(left, right):
    return lax.dot_general(left, right, (((1,), (1,)), ((), ())), preferred_element_type=F32)


def dot_nn(left, right):
    return lax.dot_general(left, right, (((1,), (0,)), ((), ())), preferred_element_type=F32)


def dot_tn(left, right):
    return lax.dot_general(left, right, (((0,), (0,)), ((), ())), preferred_element_type=F32)


def per_device(
    block_input,
    slot_spans,
    output_adjoint,
    opening_scale_factor,
    opening_offset_vector,
    intake_coefficients,
    intake_offset,
    brief_filter_coefficients,
    brief_filter_offset,
    direct_path_factor,
    filter_final_coefficients,
    mixer_output_coefficients,
    mixer_output_offset,
    closing_scale_factor,
    closing_offset_vector,
    expand_coefficients,
    expand_offset,
    contract_coefficients,
    contract_offset,
    filter_entry_coefficients,
    filter_entry_offset,
    filter_second_coefficients,
    filter_second_offset,
    filter_third_coefficients,
    filter_third_offset,
    periodic_frequency,
):
    width = block_input.shape[2]
    local = block_input.shape[1]
    seq_count = lax.axis_size("seq")
    count = lax.axis_size("dp") * seq_count
    seq_index = lax.axis_index("seq")
    me = lax.axis_index("dp") * seq_count + seq_index
    half = seq_count // 2
    group_bits = half.bit_length() - 1
    rank = seq_index % half
    side = seq_index // half
    length = local * seq_count
    channels = width // half
    chan_start = rank * channels
    up, across = orders_of(count)
    down, back = up[::-1], across[::-1]
    tables = tuple(jnp.asarray(t) for t in dft_tables(length))

    vectors = (
        opening_scale_factor,
        opening_offset_vector,
        direct_path_factor,
        mixer_output_offset,
        closing_scale_factor,
        closing_offset_vector,
        contract_offset,
        intake_offset,
        brief_filter_offset,
        brief_filter_coefficients,
        expand_offset,
    )
    middle = width // 2
    far = half.bit_length() - 1
    intake_shard = intake_coefficients.T
    front = Gather(intake_shard[:, :middle], me, count, down, placed=False)
    rear = Gather(intake_shard[:, middle:], me, count, back, placed=False)
    bits = len(down)
    spread = list(range(1, bits)) + [0]
    final = Gather(filter_final_coefficients.T.astype(F32), me, count, spread)
    trade = Swap(
        lax.dynamic_index_in_dim(block_input, 1 - side, 0, keepdims=False), me, count, far
    )
    features = jnp.asarray(position_features(length, filter_entry_coefficients.shape[0]))
    send(final, front, rear)
    send(trade)
    later = jnp.concatenate(
        [expand_coefficients.T]
        + [
            contract_coefficients[q * width : (q + 1) * width].T
            for q in range(contract_coefficients.shape[0] // width)
        ]
        + [mixer_output_coefficients.T],
        axis=0,
    )
    frequency = periodic_frequency

    def layer(values, weights, offset):
        p = product(values, weights) + offset
        return p, jnp.sin(frequency * p), jnp.cos(frequency * p)

    p1, m1, c1 = layer(features, filter_entry_coefficients, filter_entry_offset)
    p1, m1, c1, later = meet((p1, m1, c1, later), final, front, rear)
    later = lax.all_gather(later, AXES, axis=0, tiled=False)
    (m1,) = send(final, front, rear, state=(m1,))
    p2, m2, c2 = layer(m1, filter_second_coefficients, filter_second_offset)
    p2, m2, c2 = meet((p2, m2, c2), final, front, rear)
    (m2,) = send(final, front, rear, state=(m2,))
    p3, hidden, c3 = layer(m2, filter_third_coefficients, filter_third_offset)
    pack = jnp.concatenate([v.astype(F32).reshape(-1) for v in vectors])
    used = pack.size
    pad = -used % 1024
    pack = jnp.concatenate([pack, jnp.zeros((pad,), F32)]).reshape(8, -1)
    p3, hidden, c3, pack = meet((p3, hidden, c3, pack), final)
    bundle = Gather(pack, me, count, spread)
    (hidden,) = send(final, bundle, state=(hidden,))
    shaping = modulation(length, width, chan_start, channels)
    (shaping,) = meet((shaping,), final, bundle, front, rear)
    (shaping,) = send(final, bundle, front, rear, state=(shaping,))
    own_rows = lax.dynamic_index_in_dim(block_input, side, 0, keepdims=False)
    (own_rows,) = meet((own_rows,), final, bundle, trade)
    drain(final)
    columns = lax.dynamic_slice_in_dim(final.held.reshape(width, -1), chan_start, channels, 0)
    (columns,) = send(bundle, state=(columns,))
    filter_kernel = (
        lax.dot_general(
            hidden,
            columns,
            (((1,), (1,)), ((), ())),
            precision=lax.Precision.HIGHEST,
            preferred_element_type=F32,
        )
        * shaping
    )
    (filter_kernel,) = meet((filter_kernel,), bundle)
    (filter_kernel,) = send(bundle, state=(filter_kernel,))
    kernel_spec = spectrum(filter_kernel, tables)
    tokens_low = jnp.concatenate([own_rows, trade.value], axis=0)
    kernel_spec, tokens_low = meet((kernel_spec, tokens_low), bundle, front, rear)
    blocks = tokens_low.reshape(2, local, width)
    ends = Ring(blocks[:, local - 16 :], count, half, 1)
    send(front, rear, bundle, ends)
    own_base = seq_index * local
    far_base = ((1 - side) * half + rank) * local
    span = lax.dynamic_index_in_dim(slot_spans, side, 0, keepdims=False)
    places = jnp.stack([own_base, far_base])[:, None] + jnp.arange(-16, local)
    mask_all = ((places >= span[0]) & (places < span[0] + span[1])).astype(F32)[:, :, None]
    row_mask = mask_all[:, 16:].reshape(-1, 1)
    tokens = tokens_low.astype(F32)
    (mask_all,) = meet((mask_all,), bundle, front, rear, ends)
    drain(bundle, front, rear)
    no_rows = jnp.zeros_like(ends.value[0])
    wrapped = jnp.stack(
        [
            jnp.where(side == 1, ends.value[1], no_rows),
            jnp.where(side == 0, ends.value[0], no_rows),
        ]
    )
    before = jnp.where(rank == 0, wrapped, ends.value)
    blocks = jnp.concatenate([before, blocks], axis=1)
    pack_full = bundle.held.reshape(count, -1)
    fields = []
    at = 0
    for v in vectors:
        part = pack_full[:, at : at + v.size]
        at += v.size
        if v.ndim == 1:
            fields.append(part.reshape(-1))
        else:
            fields.append(
                part.reshape(count, v.shape[0], -1).transpose(1, 0, 2).reshape(v.shape[0], -1)
            )
    (
        gain_one,
        shift_one,
        skip_gain,
        mix_bias,
        gain_two,
        shift_two,
        down_bias,
        intake_bias,
        conv_bias,
        conv_taps,
        up_bias,
    ) = fields
    intake_t = place_shards([front, rear], me, count).reshape(-1, width)
    trade_adj = Swap(
        lax.dynamic_index_in_dim(output_adjoint, 1 - side, 0, keepdims=False), me, count, far
    )
    send(trade_adj)

    rows = 2 * local
    normed_low, projected_all, outer_gate, signal = front_part(
        blocks,
        mask_all,
        gain_one.reshape(1, -1),
        shift_one.reshape(1, -1),
        intake_t,
        intake_bias.reshape(1, -1),
        conv_taps,
        conv_bias.reshape(1, -1),
    )
    normed_low = normed_low.reshape(rows, width)
    outer_gate = outer_gate.reshape(rows, width).astype(F32)
    signal = signal.reshape(rows, width)

    def traded(near, give):
        got = [near]
        for k in range(1, half):
            got.append(lax.ppermute(give(k), AXES, [(i, i ^ k) for i in range(count)]))
        if half == 2:
            return jnp.where(rank == 0, got[0], got[1]), jnp.where(rank == 0, got[1], got[0])
        stacked = jnp.take(jnp.stack(got), jnp.arange(half) ^ rank, axis=0)
        return tuple(stacked[k] for k in range(half))

    def to_channels(value):
        def give(k):
            return lax.dynamic_slice_in_dim(value, (rank ^ k) * channels, channels, 1)

        pieces = traded(give(0), give)
        first = [jnp.where(side == 0, p[:local], p[local:]) for p in pieces]
        second = [jnp.where(side == 0, p[local:], p[:local]) for p in pieces]
        return jnp.concatenate(first + second, axis=0)

    def to_rows(value):
        def give(k):
            first = lax.dynamic_slice_in_dim(value, (rank ^ k) * local, local, 0)
            second = lax.dynamic_slice_in_dim(value, (half + (rank ^ k)) * local, local, 0)
            return jnp.concatenate(
                [jnp.where(side == 0, first, second), jnp.where(side == 0, second, first)], axis=0
            )

        return jnp.concatenate(traded(give(0), give), axis=1)

    def blocks_of(value):
        return value.reshape(2, local, -1)

    paired = half == 2 and local % (2 * length // RADIX) == 0
    place = jnp.stack([rank, side]).astype(jnp.int32)

    def halves(value):
        near = lax.dynamic_slice_in_dim(value, rank * channels, channels, 1)
        given = lax.dynamic_slice_in_dim(value, (1 - rank) * channels, channels, 1)
        return near, lax.ppermute(given, AXES, pairs_of(count, 1))

    def joined_halves(keep, give):
        got = lax.ppermute(give, AXES, pairs_of(count, 1))
        return jnp.where(
            rank == 0,
            jnp.concatenate([keep, got], axis=1),
            jnp.concatenate([got, keep], axis=1),
        )

    if paired:
        sig_spec, keep, give = paired_conv(place, *halves(signal), kernel_spec, tables)
        carried = joined_halves(keep, give).astype(F32)
    else:
        sig_spec, carried_cols = long_conv(to_channels(signal), kernel_spec, tables)
        carried = to_rows(carried_cols.astype(BF)).astype(F32)
    signal_wide = signal.astype(F32)
    joined = carried + skip_gain * signal_wide
    joined_low = joined.astype(BF)
    gated_mix = (joined * outer_gate).astype(BF)
    (gated_mix,) = meet((gated_mix,), trade_adj)
    own_adj = lax.dynamic_index_in_dim(output_adjoint, side, 0, keepdims=False)
    adjoint = jnp.concatenate([own_adj, trade_adj.value], axis=0)
    ff_rows = expand_coefficients.shape[1]
    mix_rows = mixer_output_coefficients.shape[1]
    if ff_rows % 16 == 0:
        up_t = later
    else:
        up_t = later[:, :ff_rows]
    mix_t = later[:, later.shape[1] - mix_rows :].reshape(-1, width)
    folds = contract_coefficients.shape[0] // width
    down_t = (
        later[:, ff_rows : later.shape[1] - mix_rows]
        .reshape(count, folds, -1, width)
        .transpose(1, 0, 2, 3)
        .reshape(folds, width, width)
    )
    residual = tokens + dot_nt(gated_mix, mix_t) + mix_bias
    unit_two, rstd_two = normalise(residual)
    second_low = (unit_two * gain_two + shift_two).astype(BF)
    grad_out = row_mask * adjoint.astype(F32)
    grad_low = grad_out.astype(BF)
    down_proj, grad_second, up_grad, down_grad, up_bias_grad = feed_forward(
        second_low, grad_low, up_t, down_t, up_bias
    )
    up_bias_grad = up_bias_grad.reshape(-1)
    output = (row_mask * (residual + down_proj + down_bias)).astype(BF)

    up_sum = Scatter(up_grad.reshape(count, -1, width), me, count, across, BF)
    down_sum = Scatter(down_grad.reshape(count, -1, down_grad.shape[1]), me, count, up, BF)
    (grad_second,) = send(up_sum, down_sum, state=(grad_second,))
    down_bias_grad = jnp.sum(grad_out, axis=0)
    gain_two_grad = jnp.sum(grad_second * unit_two, axis=0)
    shift_two_grad = jnp.sum(grad_second, axis=0)
    grad_residual = grad_out + normalise_back(unit_two, rstd_two, grad_second * gain_two)
    mix_bias_grad = jnp.sum(grad_residual, axis=0)
    resid_low = grad_residual.astype(BF)
    mix_grad = dot_tn(resid_low, gated_mix).astype(BF)
    grad_gated = dot_nn(resid_low, mix_t)
    grad_joined = grad_gated * outer_gate
    grad_joined_low = grad_joined.astype(BF)
    skip_grad = jnp.sum(grad_joined * signal_wide, axis=0)
    (grad_joined_low, mix_grad) = meet((grad_joined_low, mix_grad), up_sum, down_sum)
    (grad_joined_low,) = send(up_sum, down_sum, state=(grad_joined_low,))
    if paired:
        keep, give, kernel_grad = paired_back(
            place, *halves(grad_joined_low), kernel_spec, sig_spec, tables
        )
        keep, give, kernel_grad = meet((keep, give, kernel_grad), up_sum, down_sum)
        keep, give = send(up_sum, down_sum, state=(keep, give))
        conv_back_low = joined_halves(keep, give)
    else:
        conv_back_cols, kernel_grad = long_back(
            to_channels(grad_joined_low), kernel_spec, sig_spec, tables
        )
        conv_back_cols, kernel_grad = meet((conv_back_cols, kernel_grad), up_sum, down_sum)
        (conv_back_cols,) = send(up_sum, down_sum, state=(conv_back_cols,))
        conv_back_low = to_rows(conv_back_cols.astype(BF))
    conv_back = conv_back_low.astype(F32)
    first = blocks_of(grad_gated)[:, :2]
    first_signal = blocks_of(row_mask)[:, :2] * (
        blocks_of(conv_back)[:, :2] + skip_gain * blocks_of(grad_joined_low)[:, :2].astype(F32)
    )
    near = projected_all[:, 14:18, width:].astype(F32)
    first_gates = conv_bias[width:] + sum(
        conv_taps[k, width:] * near[:, k : k + 2] for k in range(3)
    )
    starts = Ring(
        jnp.concatenate(
            [
                first * blocks_of(joined_low)[:, :2].astype(F32),
                first_signal * first_gates[:, :, width:],
                first_signal * first_gates[:, :, :width],
            ],
            axis=2,
        ),
        count,
        half,
        -1,
    )
    send(starts)
    (conv_back_low,) = meet((conv_back_low,), starts)
    starts = starts.value
    trade_out = Swap(output[local:], me, count, far)
    wrapped_after = jnp.stack(
        [jnp.where(side == 0, starts[1], 0.0), jnp.where(side == 1, starts[0], 0.0)]
    )
    after = jnp.where(rank == half - 1, wrapped_after, starts)
    after = jnp.concatenate([after, jnp.zeros((2, 6, after.shape[2]), F32)], axis=1)
    grad_projected, sums = tail_back(
        projected_all,
        blocks_of(grad_gated),
        blocks_of(joined_low),
        blocks_of(conv_back_low),
        blocks_of(grad_joined_low),
        after,
        blocks_of(row_mask),
        conv_taps,
        conv_bias.reshape(1, -1),
        skip_gain.reshape(1, -1),
    )
    conv_bias_grad = sums[0]
    taps_grad = sums[1:4]
    intake_bias_grad = sums[4]
    projected_low = grad_projected.reshape(rows, -1)
    (projected_low,) = meet((projected_low,), up_sum, down_sum)
    (projected_low,) = send(
        up_sum, down_sum, trade_out, state=(projected_low,)
    )
    intake_grad = dot_tn(projected_low, normed_low).astype(BF).reshape(count, -1, width)
    intake_grad, projected_low = meet((intake_grad, projected_low))
    both_grad = jnp.concatenate([intake_grad, mix_grad.reshape(count, -1, width)], axis=1)
    front_sum = Scatter(both_grad[:, :, :middle], me, count, up, BF)
    rear_sum = Scatter(both_grad[:, :, middle:], me, count, across, BF)
    (projected_low,) = send(front_sum, rear_sum, state=(projected_low,))
    unit_one, rstd_one = normalise(tokens)
    grad_normed = dot_nn(projected_low, intake_t)
    gain_one_grad = jnp.sum(grad_normed * unit_one, axis=0)
    shift_one_grad = jnp.sum(grad_normed, axis=0)
    tokens_grad = (
        grad_residual + normalise_back(unit_one, rstd_one, grad_normed * gain_one)
    ).astype(BF)
    tokens_grad, kernel_grad = meet(
        (tokens_grad, kernel_grad), up_sum, down_sum, front_sum, rear_sum
    )
    (kernel_grad,) = send(
        up_sum, down_sum, front_sum, rear_sum, state=(kernel_grad,)
    )

    vector_grads = (
        gain_one_grad,
        shift_one_grad,
        skip_grad,
        mix_bias_grad,
        gain_two_grad,
        shift_two_grad,
        down_bias_grad,
        intake_bias_grad,
        conv_bias_grad,
        taps_grad,
        up_bias_grad,
    )
    pieces = []
    for g in vector_grads:
        if g.ndim == 1:
            pieces.append(g.reshape(count, -1))
        else:
            pieces.append(
                g.reshape(g.shape[0], count, -1).transpose(1, 0, 2).reshape(count, -1)
            )
    packed = jnp.concatenate(pieces + [jnp.zeros((count, pad), F32)], axis=1)
    bundle_sum = Exchange(packed.reshape(count, 8, -1))
    trade_tokens = Swap(tokens_grad[local:], me, count, far)
    (kernel_grad,) = send(bundle_sum, trade_tokens, state=(kernel_grad,))
    column_grad, net = filter_back(
        kernel_grad,
        shaping,
        columns,
        hidden,
        m1,
        m2,
        features,
        p1,
        p2,
        p3,
        c1,
        c2,
        c3,
        frequency,
        filter_second_coefficients,
        filter_third_coefficients,
        8 * count,
    )
    column_grad, net = meet(
        (column_grad, net), bundle_sum, front_sum, rear_sum, up_sum, down_sum, trade_out
    )
    filter_full = lax.dynamic_update_slice_in_dim(
        jnp.zeros((width, hidden.shape[1]), F32), column_grad, chan_start, 0
    )
    emb, filt = filter_entry_coefficients.shape
    share = filter_full.shape[0] // count
    final_sum = Exchange(
        jnp.concatenate(
            [filter_full.reshape(count, share, filt), net.reshape(count, -1, filt)], axis=1
        )
    )
    (filter_full,) = send(final_sum, state=(filter_full,))
    send(front_sum, rear_sum)
    meet((), front_sum, rear_sum, trade_tokens)
    send(front_sum, rear_sum)
    meet((), front_sum, rear_sum, final_sum)
    final_grad = final_sum.value[:share]
    net_part = final_sum.value[share:]
    net_all = Exchange(jnp.broadcast_to(net_part, (count,) + net_part.shape), add=False)
    send(net_all)
    send(front_sum, rear_sum)
    drain(net_all, bundle_sum, final_sum, front_sum, rear_sum, up_sum, down_sum, trade_tokens)
    summed = bundle_sum.value.reshape(-1)
    small = []
    at = 0
    for v in vectors:
        small.append(summed[at : at + v.size].reshape(v.shape))
        at += v.size
    total = net_all.value.reshape(-1, filt)
    second_at, third_at, vec_at = net_places(emb, filt)
    net_out = (
        total[:emb],
        total[vec_at],
        total[second_at : second_at + filt],
        total[vec_at + 1],
        total[third_at : third_at + filt],
        total[vec_at + 2],
        total[vec_at + 3],
    )
    both_shard = jnp.concatenate([front_sum.value, rear_sum.value], axis=1)
    intake_rows = intake_grad.shape[1]
    intake_shard_grad = both_shard[:intake_rows]

    def at_home(near, far_part):
        held = jnp.zeros((2,) + near.shape, near.dtype)
        held = lax.dynamic_update_slice_in_dim(held, near[None], side, 0)
        return lax.dynamic_update_slice_in_dim(held, far_part[None], 1 - side, 0)

    output_home = at_home(output[:local], trade_out.value)
    tokens_home = at_home(tokens_grad[:local], trade_tokens.value)
    return (
        output_home,
        tokens_home,
        small[0],
        small[1],
        intake_shard_grad.T,
        small[7],
        small[9],
        small[8],
        small[2],
        final_grad.T,
        both_shard[intake_rows:].T,
        small[3],
        small[4],
        small[5],
        up_sum.value.T,
        small[10],
        down_sum.value.T,
        small[6],
    ) + net_out

def solution(mesh):
    in_specs = (
        P("dp", "seq", None),
        P("dp", None),
        P("dp", "seq", None),
        P(("dp", "seq")),
        P(("dp", "seq")),
        P(None, ("dp", "seq")),
        P(("dp", "seq")),
        P(None, ("dp", "seq")),
        P(("dp", "seq")),
        P(("dp", "seq")),
        P(None, ("dp", "seq")),
        P(None, ("dp", "seq")),
        P(("dp", "seq")),
        P(("dp", "seq")),
        P(("dp", "seq")),
        P(None, ("dp", "seq")),
        P(("dp", "seq")),
        P(None, ("dp", "seq")),
        P(("dp", "seq")),
        P(),
        P(),
        P(),
        P(),
        P(),
        P(),
        P(),
    )
    out_specs = (
        P("dp", "seq", None),
        P("dp", "seq", None),
        P(("dp", "seq")),
        P(("dp", "seq")),
        P(None, ("dp", "seq")),
        P(("dp", "seq")),
        P(None, ("dp", "seq")),
        P(("dp", "seq")),
        P(("dp", "seq")),
        P(None, ("dp", "seq")),
        P(None, ("dp", "seq")),
        P(("dp", "seq")),
        P(("dp", "seq")),
        P(("dp", "seq")),
        P(None, ("dp", "seq")),
        P(("dp", "seq")),
        P(None, ("dp", "seq")),
        P(("dp", "seq")),
        P(),
        P(),
        P(),
        P(),
        P(),
        P(),
        P(),
    )
    return jax.shard_map(
        per_device, mesh=mesh, in_specs=in_specs, out_specs=out_specs, check_vma=False
    )
```

```python
import math

import jax
import jax.numpy as jnp
import ml_dtypes
import numpy as np
from jax import lax
from jax.experimental import pallas as pl
from jax.experimental.pallas import tpu as pltpu
from jax.sharding import PartitionSpec as P

AXES = ("dp", "seq")

F32=jnp.float32; BF=jnp.bfloat16
RADIX=16

def dft_tables(length):
    padded = 2*length
    inner = padded//RADIX
    pairs = RADIX//4
    half = RADIX//2
    m = np.arange(inner)
    mats=[]
    for p in range(pairs):
        for s in (p, half-1-p):
            k2 = 2*(RADIX*m+s)+1
            ang = np.pi*((k2[:,None]*m[None,:])%(2*padded))/padded
            c,sn=np.cos(ang),np.sin(ang)
            mats.append(np.block([[c,sn],[-sn,c]]))
    fwd=np.stack(mats).reshape(pairs,2,2*inner,2*inner)
    inv=np.swapaxes(fwd,-1,-2)/length
    r=np.arange(half)
    th=np.pi*(r[None,:]*(2*np.arange(pairs)[:,None]+1))/RADIX
    coef=np.concatenate([np.cos(th),np.sin(th)],axis=1).astype(np.float32)
    return fwd.astype(ml_dtypes.bfloat16),inv.astype(ml_dtypes.bfloat16),coef

def split_rows(x_ref,coef_ref,p,z_ref,inner):
    step=16
    @pl.loop(0,inner//step,unroll=True)
    def _(i):
        lo=pl.multiple_of(i*step,step)
        rows=pl.ds(lo,step); low=pl.ds(pl.multiple_of(inner+i*step,step),step)
        xs=[x_ref[r,rows,:].astype(F32) for r in range(8)]
        c=[coef_ref[p,r] for r in range(8)]; s=[coef_ref[p,8+r] for r in range(8)]
        ce=xs[0]+c[2]*xs[2]+c[4]*xs[4]+c[6]*xs[6]
        co=c[1]*xs[1]+c[3]*xs[3]+c[5]*xs[5]+c[7]*xs[7]
        se=s[2]*xs[2]+s[4]*xs[4]+s[6]*xs[6]
        so=s[1]*xs[1]+s[3]*xs[3]+s[5]*xs[5]+s[7]*xs[7]
        z_ref[0,rows,:]=(ce+co).astype(BF)
        z_ref[1,rows,:]=(ce-co).astype(BF)
        z_ref[0,low,:]=(-(se+so)).astype(BF)
        z_ref[1,low,:]=(se-so).astype(BF)

def join_rows(w_ref,coef_ref,p,acc_ref,inner,lanes):
    step=16
    @pl.loop(0,inner//step,unroll=True)
    def _(i):
        lo=pl.multiple_of(i*step,step)
        rows=pl.ds(lo,step); low=pl.ds(pl.multiple_of(inner+i*step,step),step)
        r0=w_ref[0,rows,lanes]; r1=w_ref[1,rows,lanes]
        i0=w_ref[0,low,lanes]; i1=w_ref[1,low,lanes]
        rs=(r0+r1,r0-r1); im=(i0-i1,i0+i1)
        for r in range(8):
            if r==0: term=rs[0]
            else: term=coef_ref[p,r]*rs[r%2]-coef_ref[p,8+r]*im[r%2]
            acc_ref[r,rows,:]=jnp.where(p==0,0.0,acc_ref[r,rows,:])+term

def spec_kernel(coef_ref,x_ref,f_ref,o_ref,z_ref):
    p=pl.program_id(0); inner=x_ref.shape[1]
    split_rows(x_ref,coef_ref,p,z_ref,inner)
    for j in range(2):
        o_ref[0,j]=jnp.dot(f_ref[0,j],z_ref[j],preferred_element_type=F32).astype(o_ref.dtype)

def conv_kernel(coef_ref,x_ref,k_ref,f_ref,b_ref,s_ref,y_ref,z_ref,w_ref,acc_ref):
    p=pl.program_id(0); inner=x_ref.shape[1]
    split_rows(x_ref,coef_ref,p,z_ref,inner)
    for j in range(2):
        w_ref[j]=jnp.dot(f_ref[0,j],z_ref[j],preferred_element_type=F32)
    step=16
    for j in range(2):
        @pl.loop(0,inner//step,unroll=True)
        def _(i):
            rows=pl.ds(pl.multiple_of(i*step,step),step); low=pl.ds(pl.multiple_of(inner+i*step,step),step)
            xr=w_ref[j,rows,:]; xi=w_ref[j,low,:]
            kr=k_ref[0,j,rows,:].astype(F32); ki=k_ref[0,j,low,:].astype(F32)
            s_ref[0,j,rows,:]=xr.astype(BF); s_ref[0,j,low,:]=xi.astype(BF)
            z_ref[j,rows,:]=(xr*kr-xi*ki).astype(BF)
            z_ref[j,low,:]=(xr*ki+xi*kr).astype(BF)
    for j in range(2):
        w_ref[j]=jnp.dot(b_ref[0,j],z_ref[j],preferred_element_type=F32)
    join_rows(w_ref,coef_ref,p,acc_ref,inner,slice(None))
    if y_ref is None: return
    @pl.when(p==pl.num_programs(0)-1)
    def _():
        @pl.loop(0,inner//step,unroll=True)
        def _(i):
            rows=pl.ds(pl.multiple_of(i*step,step),step)
            for r in range(8):
                y_ref[r,rows,:]=acc_ref[r,rows,:].astype(y_ref.dtype)

def back_kernel(coef_ref,g_ref,k_ref,s_ref,f_ref,b_ref,y_ref,kg_ref,z_ref,w_ref,q_ref,v_ref,acc_ref):
    p=pl.program_id(0); inner=g_ref.shape[1]; chans=g_ref.shape[2]
    split_rows(g_ref,coef_ref,p,z_ref,inner)
    for j in range(2):
        w_ref[j]=jnp.dot(f_ref[0,j],z_ref[j],preferred_element_type=F32)
    step=16
    for j in range(2):
        @pl.loop(0,inner//step,unroll=True)
        def _(i):
            rows=pl.ds(pl.multiple_of(i*step,step),step); low=pl.ds(pl.multiple_of(inner+i*step,step),step)
            gr=w_ref[j,rows,:]; gi=w_ref[j,low,:]
            kr=k_ref[0,j,rows,:].astype(F32); ki=k_ref[0,j,low,:].astype(F32)
            q_ref[j,rows,0:chans]=(gr*kr+gi*ki).astype(BF)
            q_ref[j,low,0:chans]=(gi*kr-gr*ki).astype(BF)
            kr=s_ref[0,j,rows,:].astype(F32); ki=s_ref[0,j,low,:].astype(F32)
            q_ref[j,rows,chans:2*chans]=(gr*kr+gi*ki).astype(BF)
            q_ref[j,low,chans:2*chans]=(gi*kr-gr*ki).astype(BF)
    for j in range(2):
        v_ref[j]=jnp.dot(b_ref[0,j],q_ref[j],preferred_element_type=F32)
    join_rows(v_ref,coef_ref,p,acc_ref,inner,slice(0,chans))
    join_rows(v_ref,coef_ref,p,kg_ref,inner,slice(chans,2*chans))
    if y_ref is None: return
    @pl.when(p==pl.num_programs(0)-1)
    def _():
        @pl.loop(0,inner//step,unroll=True)
        def _(i):
            rows=pl.ds(pl.multiple_of(i*step,step),step)
            for r in range(8):
                y_ref[r,rows,:]=acc_ref[r,rows,:].astype(y_ref.dtype)

def fill(place_ref,a_ref,b_ref,xs_ref):
    local=a_ref.shape[0]//2; inner=xs_ref.shape[1]; per=local//inner
    for rank in (0,1):
        for side in (0,1):
            @pl.when((place_ref[0]==rank)&(place_ref[1]==side))
            def _():
                for r in range(8):
                    j=r//per
                    src=a_ref if j%2==rank else b_ref
                    lo=(0 if j//2==side else local)+(r%per)*inner
                    xs_ref[r]=src[lo:lo+inner,:]

def spill(place_ref,acc_ref,keep_ref,give_ref):
    local=keep_ref.shape[0]//2; inner=acc_ref.shape[1]; per=local//inner
    for rank in (0,1):
        for side in (0,1):
            @pl.when((place_ref[0]==rank)&(place_ref[1]==side))
            def _():
                for r in range(8):
                    j=r//per
                    dst=keep_ref if j%2==rank else give_ref
                    lo=(0 if j//2==side else local)+(r%per)*inner
                    dst[lo:lo+inner,:]=acc_ref[r].astype(BF)

def paired_conv_kernel(place_ref,coef_ref,a_ref,o_ref,k_ref,f_ref,b_ref,s_ref,keep_ref,give_ref,xs_ref,z_ref,w_ref,acc_ref):
    @pl.when(pl.program_id(0)==0)
    def _(): fill(place_ref,a_ref,o_ref,xs_ref)
    conv_kernel(coef_ref,xs_ref,k_ref,f_ref,b_ref,s_ref,None,z_ref,w_ref,acc_ref)
    @pl.when(pl.program_id(0)==pl.num_programs(0)-1)
    def _(): spill(place_ref,acc_ref,keep_ref,give_ref)

def paired_back_kernel(place_ref,coef_ref,a_ref,o_ref,k_ref,s_ref,f_ref,b_ref,keep_ref,give_ref,kg_ref,xs_ref,z_ref,w_ref,q_ref,v_ref,acc_ref):
    @pl.when(pl.program_id(0)==0)
    def _(): fill(place_ref,a_ref,o_ref,xs_ref)
    back_kernel(coef_ref,xs_ref,k_ref,s_ref,f_ref,b_ref,None,kg_ref,z_ref,w_ref,q_ref,v_ref,acc_ref)
    @pl.when(pl.program_id(0)==pl.num_programs(0)-1)
    def _(): spill(place_ref,acc_ref,keep_ref,give_ref)

def cost(flops,moved):
    return pl.CostEstimate(flops=flops,bytes_accessed=moved,transcendentals=0)

PAR=pltpu.CompilerParams(vmem_limit_bytes=52<<20)
SM=pl.BlockSpec(memory_space=pltpu.SMEM)
def whole(shape): return pl.BlockSpec(shape,lambda p:(0,)*len(shape))
def step_of(shape): return pl.BlockSpec((1,)+shape,lambda p:(p,)+(0,)*len(shape))

def spectrum(x,tables):
    fwd,inv,coef=tables
    length,ch=x.shape; inner=2*length//RADIX
    return pl.pallas_call(spec_kernel,grid=(RADIX//4,),
        in_specs=[SM,whole((8,inner,ch)),step_of((2,2*inner,2*inner))],
        out_specs=step_of((2,2*inner,ch)),
        out_shape=jax.ShapeDtypeStruct((RADIX//4,2,2*inner,ch),BF),
        scratch_shapes=[pltpu.VMEM((2,2*inner,ch),BF)],cost_estimate=cost(10000*length*ch,40*length*ch),compiler_params=PAR)(coef,x.reshape(8,inner,ch),fwd)

def long_conv(x,kspec,tables):
    fwd,inv,coef=tables
    length,ch=x.shape; inner=2*length//RADIX
    s,y=pl.pallas_call(conv_kernel,grid=(RADIX//4,),
        in_specs=[SM,whole((8,inner,ch)),step_of((2,2*inner,ch)),step_of((2,2*inner,2*inner)),step_of((2,2*inner,2*inner))],
        out_specs=[step_of((2,2*inner,ch)),whole((8,inner,ch))],
        out_shape=[jax.ShapeDtypeStruct((RADIX//4,2,2*inner,ch),BF),jax.ShapeDtypeStruct((8,inner,ch),BF)],
        scratch_shapes=[pltpu.VMEM((2,2*inner,ch),BF),pltpu.VMEM((2,2*inner,ch),F32),pltpu.VMEM((8,inner,ch),F32)],cost_estimate=cost(20000*length*ch,75*length*ch),compiler_params=PAR)(coef,x.reshape(8,inner,ch),kspec,fwd,inv)
    return s,y.reshape(length,ch)

def long_back(g,kspec,sspec,tables):
    fwd,inv,coef=tables
    length,ch=g.shape; inner=2*length//RADIX
    y,kg=pl.pallas_call(back_kernel,grid=(RADIX//4,),
        in_specs=[SM,whole((8,inner,ch)),step_of((2,2*inner,ch)),step_of((2,2*inner,ch)),step_of((2,2*inner,2*inner)),step_of((2,2*inner,2*inner))],
        out_specs=[whole((8,inner,ch)),whole((8,inner,ch))],
        out_shape=[jax.ShapeDtypeStruct((8,inner,ch),BF),jax.ShapeDtypeStruct((8,inner,ch),F32)],
        scratch_shapes=[pltpu.VMEM((2,2*inner,ch),BF),pltpu.VMEM((2,2*inner,ch),F32),pltpu.VMEM((2,2*inner,2*ch),BF),pltpu.VMEM((2,2*inner,2*ch),F32),pltpu.VMEM((8,inner,ch),F32)],cost_estimate=cost(27000*length*ch,100*length*ch),compiler_params=PAR)(coef,g.reshape(8,inner,ch),kspec,sspec,fwd,inv)
    return y.reshape(length,ch),kg.reshape(length,ch)


def paired_conv(place,near,other,kspec,tables):
    fwd,inv,coef=tables
    rows,ch=near.shape; inner=fwd.shape[-1]//2; length=8*inner
    low=jax.ShapeDtypeStruct((rows,ch),BF)
    return pl.pallas_call(paired_conv_kernel,grid=(RADIX//4,),
        in_specs=[SM,SM,whole((rows,ch)),whole((rows,ch)),step_of((2,2*inner,ch)),step_of((2,2*inner,2*inner)),step_of((2,2*inner,2*inner))],
        out_specs=[step_of((2,2*inner,ch)),whole((rows,ch)),whole((rows,ch))],
        out_shape=[jax.ShapeDtypeStruct((RADIX//4,2,2*inner,ch),BF),low,low],
        scratch_shapes=[pltpu.VMEM((8,inner,ch),BF),pltpu.VMEM((2,2*inner,ch),BF),pltpu.VMEM((2,2*inner,ch),F32),pltpu.VMEM((8,inner,ch),F32)],
        cost_estimate=cost(20000*length*ch,75*length*ch),compiler_params=PAR)(place,coef,near,other,kspec,fwd,inv)

def paired_back(place,near,other,kspec,sspec,tables):
    fwd,inv,coef=tables
    rows,ch=near.shape; inner=fwd.shape[-1]//2; length=8*inner
    low=jax.ShapeDtypeStruct((rows,ch),BF)
    keep,give,kg=pl.pallas_call(paired_back_kernel,grid=(RADIX//4,),
        in_specs=[SM,SM,whole((rows,ch)),whole((rows,ch)),step_of((2,2*inner,ch)),step_of((2,2*inner,ch)),step_of((2,2*inner,2*inner)),step_of((2,2*inner,2*inner))],
        out_specs=[whole((rows,ch)),whole((rows,ch)),whole((8,inner,ch))],
        out_shape=[low,low,jax.ShapeDtypeStruct((8,inner,ch),F32)],
        scratch_shapes=[pltpu.VMEM((8,inner,ch),BF),pltpu.VMEM((2,2*inner,ch),BF),pltpu.VMEM((2,2*inner,ch),F32),pltpu.VMEM((2,2*inner,2*ch),BF),pltpu.VMEM((2,2*inner,2*ch),F32),pltpu.VMEM((8,inner,ch),F32)],
        cost_estimate=cost(27000*length*ch,100*length*ch),compiler_params=PAR)(place,coef,near,other,kspec,sspec,fwd,inv)
    return keep,give,kg.reshape(length,ch)

def ff_kernel(x_ref,g_ref,wu_ref,wd_ref,bu_ref,down_ref,gsec_ref,dwu_ref,dwd_ref,dbu_ref,a_ref,gu_ref):
    f=pl.program_id(0); rows=x_ref.shape[0]; step=256 if rows%256==0 else rows
    wu=wu_ref[...].reshape(-1,x_ref.shape[1]); wd=wd_ref[0]
    total=jnp.zeros(dbu_ref.shape[1:],F32)
    @pl.when(f==0)
    def _():
        down_ref[...]=jnp.zeros_like(down_ref)
        gsec_ref[...]=jnp.zeros_like(gsec_ref)
    for r in range(rows//step):
        at=pl.ds(r*step,step)
        up=lax.dot_general(x_ref[at,:],wu,(((1,),(1,)),((),())),preferred_element_type=F32)+bu_ref[0]
        ga=jnp.dot(g_ref[at,:],wd,preferred_element_type=F32)
        sq=up*up
        th=jnp.tanh(up*(GELU_A+(GELU_A*GELU_B)*sq))
        half_one=0.5+0.5*th
        a=(up*half_one).astype(BF)
        a_ref[at,:]=a
        slope=half_one+(up*half_one*(1.0-th))*(GELU_A+(3.0*GELU_A*GELU_B)*sq)
        gu=ga*slope
        total=total+jnp.sum(gu,axis=0,keepdims=True)
        gul=gu.astype(BF)
        gu_ref[at,:]=gul
        down_ref[at,:]+=lax.dot_general(a,wd,(((1,),(1,)),((),())),preferred_element_type=F32)
        gsec_ref[at,:]+=jnp.dot(gul,wu,preferred_element_type=F32)
    dbu_ref[0]=total
    dwu_ref[...]=lax.dot_general(gu_ref[...],x_ref[...],(((0,),(0,)),((),())),preferred_element_type=F32).astype(BF)
    dwd_ref[...]=lax.dot_general(g_ref[...],a_ref[...],(((0,),(0,)),((),())),preferred_element_type=F32).astype(BF)

GELU_A=0.7978845608
GELU_B=0.044715

def feed_forward(x,g,wu,wd,bu):
    rows,width=x.shape; hid=bu.size; blk=width; chunk=hid//wu.shape[0]; chunks=blk//chunk
    n=hid//blk
    return pl.pallas_call(ff_kernel,grid=(n,),
        in_specs=[whole((rows,width)),whole((rows,width)),pl.BlockSpec((chunks,chunk,width),lambda f:(f,0,0)),pl.BlockSpec((1,width,blk),lambda f:(f,0,0)),pl.BlockSpec((1,1,blk),lambda f:(f,0,0))],
        out_specs=[whole((rows,width)),whole((rows,width)),pl.BlockSpec((blk,width),lambda f:(f,0)),pl.BlockSpec((width,blk),lambda f:(0,f)),pl.BlockSpec((1,1,blk),lambda f:(f,0,0))],
        out_shape=[jax.ShapeDtypeStruct((rows,width),F32),jax.ShapeDtypeStruct((rows,width),F32),jax.ShapeDtypeStruct((hid,width),BF),jax.ShapeDtypeStruct((width,hid),BF),jax.ShapeDtypeStruct((n,1,blk),F32)],
        scratch_shapes=[pltpu.VMEM((rows,blk),BF),pltpu.VMEM((rows,blk),BF)],
        cost_estimate=cost(20*rows*width*hid,60*rows*hid),
        compiler_params=PAR)(x,g,wu,wd,bu.reshape(n,1,blk))

def tail_kernel(p_ref,gg_ref,jo_ref,cb_ref,gj_ref,af_ref,mk_ref,tap_ref,cbias_ref,skip_ref,
                gp_ref,sums_ref,pw_ref,gc_ref):
    b=pl.program_id(0); local=gg_ref.shape[1]; width=gg_ref.shape[2]; wide=3*width
    step=64 if local%64==0 else local; lanes=128
    @pl.when(b==0)
    def _():
        sums_ref[...]=jnp.zeros_like(sums_ref)
    @pl.loop(0,width//lanes)
    def _(j):
        def cols(s): return pl.ds(pl.multiple_of(s*width+j*lanes,lanes),lanes)
        c0=cols(0)
        for s in range(3):
            for r in range(-1,local//step):
                if r<0: pw_ref[s,0:16,:]=p_ref[0,0:16,cols(s)].astype(F32)
                else: pw_ref[s,16+r*step:16+(r+1)*step,:]=p_ref[0,16+r*step:16+(r+1)*step,cols(s)].astype(F32)
        tap=[[tap_ref[k:k+1,cols(s)] for k in range(3)] for s in range(3)]
        cbias=[cbias_ref[0:1,cols(s)] for s in range(3)]
        skip=skip_ref[0:1,c0]
        acc=[[jnp.zeros((8,lanes),F32) for _ in range(5)] for s in range(3)]
        def fold(v): return jnp.sum(v.reshape(-1,8,lanes),axis=0)
        for r in range(local//step):
            lo=r*step
            at=pl.ds(lo,step)
            sh=[[pw_ref[s,14+lo+k:14+lo+k+step,:] for k in range(3)] for s in range(3)]
            gate=[None]+[cbias[s]+tap[s][0]*sh[s][0]+tap[s][1]*sh[s][1]+tap[s][2]*sh[s][2] for s in (1,2)]
            gg=gg_ref[0,at,c0]
            gs=mk_ref[0,at,:]*(cb_ref[0,at,c0].astype(F32)+skip*gj_ref[0,at,c0].astype(F32))
            gc=[gg*jo_ref[0,at,c0].astype(F32),gs*gate[2],gs*gate[1]]
            for s in range(3):
                gc_ref[s,at,:]=gc[s]
                acc[s][0]=acc[s][0]+fold(gc[s])
                for k in range(3):
                    acc[s][1+k]=acc[s][1+k]+fold(gc[s]*sh[s][k])
        for s in range(3):
            gc_ref[s,local:local+8,:]=af_ref[0,:,cols(s)]
        for r in range(local//step):
            lo=r*step
            at=pl.ds(lo,step)
            mk=mk_ref[0,at,:]
            for s in range(3):
                gp=mk*(tap[s][2]*gc_ref[s,at,:]+tap[s][1]*gc_ref[s,lo+1:lo+1+step,:]+tap[s][0]*gc_ref[s,lo+2:lo+2+step,:])
                acc[s][4]=acc[s][4]+fold(gp)
                gp_ref[0,at,cols(s)]=gp.astype(BF)
        for s in range(3):
            for q in range(5):
                sums_ref[q:q+1,cols(s)]+=jnp.sum(acc[s][q],axis=0,keepdims=True)

def tail_back(p,gg,jo,cb,gj,af,mk,taps,cbias,skip):
    blocks,local,width=gg.shape; wide=3*width
    def blk(rows,cols): return pl.BlockSpec((1,rows,cols),lambda b:(b,0,0))
    return pl.pallas_call(tail_kernel,grid=(blocks,),
        in_specs=[blk(local+16,wide),blk(local,width),blk(local,width),blk(local,width),blk(local,width),blk(8,wide),blk(local,1),whole((3,wide)),whole((1,wide)),whole((1,width))],
        out_specs=[blk(local,wide),whole((8,wide))],
        out_shape=[jax.ShapeDtypeStruct((blocks,local,wide),BF),jax.ShapeDtypeStruct((8,wide),F32)],
        scratch_shapes=[pltpu.VMEM((3,local+16,128),F32),pltpu.VMEM((3,local+8,128),F32)],
        cost_estimate=cost(7000*blocks*local*wide,22*blocks*local*wide),compiler_params=PAR)(p,gg,jo,cb,gj,af,mk,taps,cbias,skip)

def front_kernel(t_ref,mk_ref,gain_ref,shift_ref,w_ref,bias_ref,tap_ref,cbias_ref,n_out,p_out,o_out,s_out,n_ref,p_ref):
    total=t_ref.shape[1]; width=t_ref.shape[2]; local=total-16
    step=48 if total%48==0 else 16
    gain=gain_ref[...]; shift=shift_ref[...]
    for r in range(total//step):
        at=pl.ds(r*step,step)
        x=t_ref[0,at,:].astype(F32)
        c=x-jnp.mean(x,axis=-1,keepdims=True)
        v=jnp.mean(c*c,axis=-1,keepdims=True)
        n_ref[at,:]=(c*lax.rsqrt(v+1e-05)*gain+shift).astype(BF)
    for s in range(3):
        cols=pl.ds(s*width,width)
        p_ref[:,cols]=mk_ref[0]*(lax.dot_general(n_ref[...],w_ref[cols,:],(((1,),(1,)),((),())),preferred_element_type=F32)+bias_ref[0:1,cols])
    n_out[0]=n_ref[16:,:]
    step=64 if local%64==0 else local; lanes=128
    @pl.loop(0,width//lanes)
    def _(j):
        def cols(s): return pl.ds(pl.multiple_of(s*width+j*lanes,lanes),lanes)
        tap=[[tap_ref[k:k+1,cols(s)] for k in range(3)] for s in range(3)]
        cbias=[cbias_ref[0:1,cols(s)] for s in range(3)]
        for s in range(3):
            p_out[0,0:16,cols(s)]=p_ref[0:16,cols(s)].astype(BF)
        for r in range(local//step):
            lo=r*step
            at=pl.ds(lo,step)
            conv=[]
            for s in range(3):
                mid=p_ref[16+lo:16+lo+step,cols(s)]
                p_out[0,16+lo:16+lo+step,cols(s)]=mid.astype(BF)
                conv.append(cbias[s]+tap[s][0]*p_ref[14+lo:14+lo+step,cols(s)]+tap[s][1]*p_ref[15+lo:15+lo+step,cols(s)]+tap[s][2]*mid)
            o_out[0,at,cols(0)]=conv[0].astype(BF)
            s_out[0,at,cols(0)]=(mk_ref[0,16+lo:16+lo+step,:]*conv[1]*conv[2]).astype(BF)

def front_part(tok,mk,gain,shift,w,bias,taps,cbias):
    blocks,total,width=tok.shape; wide=3*width; local=total-16
    def blk(rows,cols): return pl.BlockSpec((1,rows,cols),lambda b:(b,0,0))
    low=jax.ShapeDtypeStruct((blocks,local,width),BF)
    return pl.pallas_call(front_kernel,grid=(blocks,),
        in_specs=[blk(total,width),blk(total,1),whole((1,width)),whole((1,width)),whole((wide,width)),whole((1,wide)),whole((3,wide)),whole((1,wide))],
        out_specs=[blk(local,width),blk(total,wide),blk(local,width),blk(local,width)],
        out_shape=[low,jax.ShapeDtypeStruct((blocks,total,wide),BF),low,low],
        scratch_shapes=[pltpu.VMEM((total,width),BF),pltpu.VMEM((total,wide),F32)],
        cost_estimate=cost(7000*blocks*local*wide,22*blocks*local*wide),compiler_params=PAR)(tok,mk,gain,shift,w,bias,taps,cbias)

def net_places(emb,filt):
    second=-(-emb//8)*8
    return second,second+filt,second+2*filt

def filter_kernel_back(kg_ref,sh_ref,col_ref,hid_ref,m1_ref,m2_ref,f_ref,p1_ref,p2_ref,p3_ref,c1_ref,c2_ref,c3_ref,fr_ref,w2_ref,w3_ref,
                       colg_ref,net_ref):
    i=pl.program_id(0)
    fr=fr_ref[...]
    @pl.when(i==0)
    def _():
        colg_ref[...]=jnp.zeros_like(colg_ref)
        net_ref[...]=jnp.zeros_like(net_ref)
    emb=f_ref.shape[1]; filt=fr.shape[1]
    second_at,third_at,vec_at=net_places(emb,filt)
    def mul(a,b,da,db):
        def dot(u,v): return lax.dot_general(u,v,(((da,),(db,)),((),())),preferred_element_type=F32)
        ah,bh=a.astype(BF),b.astype(BF)
        al,bl=(a-ah.astype(F32)).astype(BF),(b-bh.astype(F32)).astype(BF)
        return dot(ah,bh)+(dot(ah,bl)+dot(al,bh))
    sg=kg_ref[...]*sh_ref[...]
    colg_ref[...]+=mul(sg,hid_ref[...],0,0)
    grad=mul(sg,col_ref[...],1,0)
    rate=jnp.zeros((1,fr.shape[1]),F32)
    for row,p_ref,c_ref,in_ref,w_ref,at in ((2,p3_ref,c3_ref,m2_ref,w3_ref,third_at),(1,p2_ref,c2_ref,m1_ref,w2_ref,second_at),(0,p1_ref,c1_ref,f_ref,None,0)):
        p=p_ref[...]
        turned=grad*c_ref[...]
        rate=rate+jnp.sum(turned*p,axis=0,keepdims=True)
        gp=turned*fr
        net_ref[vec_at+row:vec_at+row+1,:]+=jnp.sum(gp,axis=0,keepdims=True)
        net_ref[at:at+in_ref.shape[1],:]+=mul(in_ref[...],gp,0,0)
        if w_ref is not None: grad=mul(gp,w_ref[...],1,1)
    net_ref[vec_at+3:vec_at+4,:]+=rate

def filter_back(kg,sh,col,hid,m1,m2,feat,p1,p2,p3,c1,c2,c3,fr,w2,w3,multiple):
    length,ch=kg.shape; filt=hid.shape[1]; emb=feat.shape[1]; blk=512
    net=-(-(net_places(emb,filt)[2]+8)//multiple)*multiple
    def rows(c): return pl.BlockSpec((blk,c),lambda i:(i,0))
    def out(a,b): return jax.ShapeDtypeStruct((a,b),F32)
    return pl.pallas_call(filter_kernel_back,grid=(length//blk,),
        in_specs=[rows(ch),rows(ch),whole((ch,filt)),rows(filt),rows(filt),rows(filt),rows(emb),rows(filt),rows(filt),rows(filt),rows(filt),rows(filt),rows(filt),whole((1,filt)),whole((filt,filt)),whole((filt,filt))],
        out_specs=[whole((ch,filt)),whole((net,filt))],
        out_shape=[out(ch,filt),out(net,filt)],
        cost_estimate=cost(30000*length*ch,100*length*ch),compiler_params=PAR)(kg,sh,col,hid,m1,m2,feat,p1,p2,p3,c1,c2,c3,fr.reshape(1,-1),w2,w3)

def product(left, right):
    return jnp.dot(left, right, precision=lax.Precision.HIGHEST, preferred_element_type=jnp.float32)

def gelu_tanh(values):
    return jax.nn.gelu(values, approximate=True)

def filter_hidden(
    features,
    filter_entry_coefficients,
    filter_entry_offset,
    filter_second_coefficients,
    filter_second_offset,
    filter_third_coefficients,
    filter_third_offset,
    periodic_frequency,
):
    first = jnp.sin(
        periodic_frequency * (product(features, filter_entry_coefficients) + filter_entry_offset)
    )
    middle = jnp.sin(
        periodic_frequency * (product(first, filter_second_coefficients) + filter_second_offset)
    )
    return jnp.sin(
        periodic_frequency * (product(middle, filter_third_coefficients) + filter_third_offset)
    )

def modulation(length, model_width, offset, channels):
    standardized_values = jnp.arange(length).astype(jnp.float32) / (length - 1)
    slowest = math.log(0.01) / 1.5
    fastest = math.log(0.01) / 0.3
    columns = (offset + jnp.arange(channels)).astype(jnp.float32)
    decays = slowest + (fastest - slowest) * columns / (model_width - 1)
    return jnp.exp(-standardized_values[:, None] * jnp.abs(decays)[None, :]) + 0.05

def position_features(length, emb_width):
    band_count = (emb_width - 1) // 2
    places = np.arange(length, dtype=np.float64)
    band_rates = 0.0001 + (band_count - 1 - 0.0001) * np.arange(band_count) / (band_count - 1)
    phases = (2.0 * math.pi * places / length)[:, None] * band_rates[None, :]
    return np.concatenate(
        [(places / (length - 1))[:, None], np.cos(phases), -np.sin(phases)], axis=1
    ).astype(np.float32)


def pairs_of(count, mask):
    return [(i, i ^ mask) for i in range(count)]


def bit_of(me, bit):
    return (me >> bit) & 1


def grouped(bits):
    return [tuple(bits[i : i + 2]) for i in range(0, len(bits), 2)]


class Gather:
    flight = None

    def __init__(self, value, me, count, order, placed=True):
        self.placed = placed
        self.held, self.me, self.count, self.order = value, me, count, list(order)
        self.at = 0

    def give(self):
        return self.held

    def ways(self, given):
        return [(given, pairs_of(self.count, 1 << self.order[self.at]))]

    def receive(self, got):
        self.at += 1
        if self.at < len(self.order):
            self.held = jnp.concatenate([self.held, got[0]], axis=0)
        else:
            self.last = got[0]
            if self.placed:
                self.held = place_shards([self], self.me, self.count)

    @property
    def open(self):
        return self.at < len(self.order)


class Scatter:
    flight = None

    def __init__(self, value, me, count, order, keep):
        self.value, self.me, self.count, self.keep = value, me, count, keep
        self.order = [g if isinstance(g, tuple) else (g,) for g in order]
        self.rows, self.columns = value.shape[1:]
        self.left = [b for g in self.order for b in g]
        self.at = 0

    def give(self):
        group = self.order[self.at]
        size = 1 << len(group)
        low = 1 << sum(1 for b in self.left if b < group[0])
        cut = self.value.reshape(-1, size, low * self.rows, self.columns)
        at = (self.me >> group[0]) & (size - 1)
        self.mine = lax.dynamic_index_in_dim(cut, at, 1, keepdims=False)
        return tuple(
            lax.dynamic_index_in_dim(cut, at ^ m, 1, keepdims=False) for m in range(1, size)
        )

    def ways(self, given):
        group = self.order[self.at]
        self.left = [b for b in self.left if b not in group]
        return [
            (g, pairs_of(self.count, m << group[0])) for m, g in enumerate(given, start=1)
        ]

    def receive(self, got):
        self.at += 1
        self.value = self.mine.astype(F32)
        for g in got:
            self.value = self.value + g.astype(F32)
        if self.open:
            self.value = self.value.astype(self.keep)
        else:
            self.value = self.value.reshape(self.rows, self.columns)

    @property
    def open(self):
        return self.at < len(self.order)


class Swap:
    flight = None

    def __init__(self, value, me, count, bit):
        self.value, self.me, self.count, self.bit = value, me, count, bit
        self.open = True

    def give(self):
        return self.value

    def ways(self, given):
        return [(given, pairs_of(self.count, 1 << self.bit))]

    def receive(self, got):
        self.value = got[0]
        self.open = False


class Ring:
    flight = None

    def __init__(self, value, count, half, by):
        self.value, self.open = value, True
        self.pairs = []
        for i in range(count):
            group, r = divmod(i, half)
            self.pairs.append((i, group * half + (r + by) % half))

    def give(self):
        return self.value

    def ways(self, given):
        return [(given, self.pairs)]

    def receive(self, got):
        self.value = got[0]
        self.open = False


class Exchange:
    flight = None

    def __init__(self, value, add=True):
        self.value, self.open, self.add = value, True, add

    def give(self):
        return self.value

    def ways(self, given):
        return [(given, None)]

    def receive(self, got):
        self.value = jnp.sum(got[0], axis=0) if self.add else got[0]
        self.open = False


def send(*chains, state=()):
    chains = [c for c in chains if c.open]
    given = [c.give() for c in chains]
    tied = lax.optimization_barrier(tuple(state) + tuple(given))
    for c, g in zip(chains, tied[len(state) :]):
        c.flight = [
            lax.all_to_all(v, AXES, 0, 0, tiled=True)
            if pairs is None
            else lax.ppermute(v, AXES, pairs)
            for v, pairs in c.ways(g)
        ]
    return tied[: len(state)]


def meet(state, *chains):
    chains = [c for c in chains if c.flight]
    sizes = [len(c.flight) for c in chains]
    tied = lax.optimization_barrier(tuple(state) + tuple(v for c in chains for v in c.flight))
    at = len(state)
    for c, n in zip(chains, sizes):
        c.receive(tied[at : at + n])
        c.flight = None
        at += n
    return tied[: len(state)]


def drain(*chains):
    meet((), *chains)
    while any(c.open for c in chains):
        send(*chains)
        meet((), *chains)


def place_shards(chains, me, count):
    half = count // 2
    rows = chains[0].held.shape[0] // half
    widths = [c.held.shape[1] for c in chains]

    def from_device(order, i):
        return sum(((i >> p) & 1) << bit for p, bit in enumerate(order[:-1]))

    def kernel(me_ref, *refs):
        own = me_ref[0]
        out_ref = refs[-1]
        left = 0
        for n, c in enumerate(chains):
            columns = slice(left, left + widths[n])
            left += widths[n]
            for i in range(half):
                near = from_device(c.order, i)
                out_ref[jnp.bitwise_xor(own, near), :, columns] = refs[2 * n][i]
                other = near | (1 << c.order[-1])
                out_ref[jnp.bitwise_xor(own, other), :, columns] = refs[2 * n + 1][i]

    vmem = pl.BlockSpec(memory_space=pltpu.VMEM)
    operands = [v.reshape(half, rows, -1) for c in chains for v in (c.held, c.last)]
    return pl.pallas_call(
        kernel,
        in_specs=[SM] + [vmem] * len(operands),
        out_specs=vmem,
        out_shape=jax.ShapeDtypeStruct((count, rows, sum(widths)), chains[0].held.dtype),
        compiler_params=PAR,
    )(me.reshape(1).astype(jnp.int32), *operands)


def orders_of(count):
    bits = count.bit_length() - 1
    first = list(range(bits))
    second = list(range(bits))
    second[1], second[2] = second[2], second[1]
    return first, second


def normalise(values):
    centre = values - jnp.mean(values, axis=-1, keepdims=True)
    spread = jnp.mean(centre * centre, axis=-1, keepdims=True)
    rstd = lax.rsqrt(spread + 1e-05)
    return centre * rstd, rstd


def normalise_back(unit, rstd, incoming):
    return rstd * (
        incoming
        - jnp.mean(incoming, axis=-1, keepdims=True)
        - unit * jnp.mean(incoming * unit, axis=-1, keepdims=True)
    )


def dot_nt(left, right):
    return lax.dot_general(left, right, (((1,), (1,)), ((), ())), preferred_element_type=F32)


def dot_nn(left, right):
    return lax.dot_general(left, right, (((1,), (0,)), ((), ())), preferred_element_type=F32)


def dot_tn(left, right):
    return lax.dot_general(left, right, (((0,), (0,)), ((), ())), preferred_element_type=F32)


def per_device(
    block_input,
    slot_spans,
    output_adjoint,
    opening_scale_factor,
    opening_offset_vector,
    intake_coefficients,
    intake_offset,
    brief_filter_coefficients,
    brief_filter_offset,
    direct_path_factor,
    filter_final_coefficients,
    mixer_output_coefficients,
    mixer_output_offset,
    closing_scale_factor,
    closing_offset_vector,
    expand_coefficients,
    expand_offset,
    contract_coefficients,
    contract_offset,
    filter_entry_coefficients,
    filter_entry_offset,
    filter_second_coefficients,
    filter_second_offset,
    filter_third_coefficients,
    filter_third_offset,
    periodic_frequency,
):
    width = block_input.shape[2]
    local = block_input.shape[1]
    seq_count = lax.axis_size("seq")
    count = lax.axis_size("dp") * seq_count
    seq_index = lax.axis_index("seq")
    me = lax.axis_index("dp") * seq_count + seq_index
    half = seq_count // 2
    group_bits = half.bit_length() - 1
    rank = seq_index % half
    side = seq_index // half
    length = local * seq_count
    channels = width // half
    chan_start = rank * channels
    up, across = orders_of(count)
    down, back = up[::-1], across[::-1]
    tables = tuple(jnp.asarray(t) for t in dft_tables(length))

    vectors = (
        opening_scale_factor,
        opening_offset_vector,
        direct_path_factor,
        mixer_output_offset,
        closing_scale_factor,
        closing_offset_vector,
        contract_offset,
        intake_offset,
        brief_filter_offset,
        brief_filter_coefficients,
        expand_offset,
    )
    middle = width // 2
    far = half.bit_length() - 1
    intake_shard = intake_coefficients.T
    front = Gather(intake_shard[:, :middle], me, count, down, placed=False)
    rear = Gather(intake_shard[:, middle:], me, count, back, placed=False)
    bits = len(down)
    spread = list(range(1, bits)) + [0]
    final = Gather(filter_final_coefficients.T.astype(F32), me, count, spread)
    trade = Swap(
        lax.dynamic_index_in_dim(block_input, 1 - side, 0, keepdims=False), me, count, far
    )
    features = jnp.asarray(position_features(length, filter_entry_coefficients.shape[0]))
    send(final, front, rear)
    send(trade)
    later = jnp.concatenate(
        [expand_coefficients.T]
        + [
            contract_coefficients[q * width : (q + 1) * width].T
            for q in range(contract_coefficients.shape[0] // width)
        ]
        + [mixer_output_coefficients.T],
        axis=0,
    )
    frequency = periodic_frequency

    def layer(values, weights, offset):
        p = product(values, weights) + offset
        return p, jnp.sin(frequency * p), jnp.cos(frequency * p)

    p1, m1, c1 = layer(features, filter_entry_coefficients, filter_entry_offset)
    p1, m1, c1, later = meet((p1, m1, c1, later), final, front, rear)
    later = lax.all_gather(later, AXES, axis=0, tiled=False)
    (m1,) = send(final, front, rear, state=(m1,))
    p2, m2, c2 = layer(m1, filter_second_coefficients, filter_second_offset)
    p2, m2, c2 = meet((p2, m2, c2), final, front, rear)
    (m2,) = send(final, front, rear, state=(m2,))
    p3, hidden, c3 = layer(m2, filter_third_coefficients, filter_third_offset)
    pack = jnp.concatenate([v.astype(F32).reshape(-1) for v in vectors])
    used = pack.size
    pad = -used % 1024
    pack = jnp.concatenate([pack, jnp.zeros((pad,), F32)]).reshape(8, -1)
    p3, hidden, c3, pack = meet((p3, hidden, c3, pack), final)
    bundle = Gather(pack, me, count, spread)
    (hidden,) = send(final, bundle, state=(hidden,))
    shaping = modulation(length, width, chan_start, channels)
    (shaping,) = meet((shaping,), final, bundle, front, rear)
    (shaping,) = send(final, bundle, front, rear, state=(shaping,))
    own_rows = lax.dynamic_index_in_dim(block_input, side, 0, keepdims=False)
    (own_rows,) = meet((own_rows,), final, bundle, trade)
    drain(final)
    columns = lax.dynamic_slice_in_dim(final.held.reshape(width, -1), chan_start, channels, 0)
    (columns,) = send(bundle, state=(columns,))
    filter_kernel = (
        lax.dot_general(
            hidden,
            columns,
            (((1,), (1,)), ((), ())),
            precision=lax.Precision.HIGHEST,
            preferred_element_type=F32,
        )
        * shaping
    )
    (filter_kernel,) = meet((filter_kernel,), bundle)
    (filter_kernel,) = send(bundle, state=(filter_kernel,))
    kernel_spec = spectrum(filter_kernel, tables)
    tokens_low = jnp.concatenate([own_rows, trade.value], axis=0)
    kernel_spec, tokens_low = meet((kernel_spec, tokens_low), bundle, front, rear)
    blocks = tokens_low.reshape(2, local, width)
    ends = Ring(blocks[:, local - 16 :], count, half, 1)
    send(front, rear, bundle, ends)
    own_base = seq_index * local
    far_base = ((1 - side) * half + rank) * local
    span = lax.dynamic_index_in_dim(slot_spans, side, 0, keepdims=False)
    places = jnp.stack([own_base, far_base])[:, None] + jnp.arange(-16, local)
    mask_all = ((places >= span[0]) & (places < span[0] + span[1])).astype(F32)[:, :, None]
    row_mask = mask_all[:, 16:].reshape(-1, 1)
    tokens = tokens_low.astype(F32)
    (mask_all,) = meet((mask_all,), bundle, front, rear, ends)
    drain(bundle, front, rear)
    no_rows = jnp.zeros_like(ends.value[0])
    wrapped = jnp.stack(
        [
            jnp.where(side == 1, ends.value[1], no_rows),
            jnp.where(side == 0, ends.value[0], no_rows),
        ]
    )
    before = jnp.where(rank == 0, wrapped, ends.value)
    blocks = jnp.concatenate([before, blocks], axis=1)
    pack_full = bundle.held.reshape(count, -1)
    fields = []
    at = 0
    for v in vectors:
        part = pack_full[:, at : at + v.size]
        at += v.size
        if v.ndim == 1:
            fields.append(part.reshape(-1))
        else:
            fields.append(
                part.reshape(count, v.shape[0], -1).transpose(1, 0, 2).reshape(v.shape[0], -1)
            )
    (
        gain_one,
        shift_one,
        skip_gain,
        mix_bias,
        gain_two,
        shift_two,
        down_bias,
        intake_bias,
        conv_bias,
        conv_taps,
        up_bias,
    ) = fields
    intake_t = place_shards([front, rear], me, count).reshape(-1, width)
    trade_adj = Swap(
        lax.dynamic_index_in_dim(output_adjoint, 1 - side, 0, keepdims=False), me, count, far
    )
    send(trade_adj)

    rows = 2 * local
    normed_low, projected_all, outer_gate, signal = front_part(
        blocks,
        mask_all,
        gain_one.reshape(1, -1),
        shift_one.reshape(1, -1),
        intake_t,
        intake_bias.reshape(1, -1),
        conv_taps,
        conv_bias.reshape(1, -1),
    )
    normed_low = normed_low.reshape(rows, width)
    outer_gate = outer_gate.reshape(rows, width).astype(F32)
    signal = signal.reshape(rows, width)

    def traded(near, give):
        got = [near]
        for k in range(1, half):
            got.append(lax.ppermute(give(k), AXES, [(i, i ^ k) for i in range(count)]))
        if half == 2:
            return jnp.where(rank == 0, got[0], got[1]), jnp.where(rank == 0, got[1], got[0])
        stacked = jnp.take(jnp.stack(got), jnp.arange(half) ^ rank, axis=0)
        return tuple(stacked[k] for k in range(half))

    def to_channels(value):
        def give(k):
            return lax.dynamic_slice_in_dim(value, (rank ^ k) * channels, channels, 1)

        pieces = traded(give(0), give)
        first = [jnp.where(side == 0, p[:local], p[local:]) for p in pieces]
        second = [jnp.where(side == 0, p[local:], p[:local]) for p in pieces]
        return jnp.concatenate(first + second, axis=0)

    def to_rows(value):
        def give(k):
            first = lax.dynamic_slice_in_dim(value, (rank ^ k) * local, local, 0)
            second = lax.dynamic_slice_in_dim(value, (half + (rank ^ k)) * local, local, 0)
            return jnp.concatenate(
                [jnp.where(side == 0, first, second), jnp.where(side == 0, second, first)], axis=0
            )

        return jnp.concatenate(traded(give(0), give), axis=1)

    def blocks_of(value):
        return value.reshape(2, local, -1)

    paired = half == 2 and local % (2 * length // RADIX) == 0
    place = jnp.stack([rank, side]).astype(jnp.int32)

    def halves(value):
        near = lax.dynamic_slice_in_dim(value, rank * channels, channels, 1)
        given = lax.dynamic_slice_in_dim(value, (1 - rank) * channels, channels, 1)
        return near, lax.ppermute(given, AXES, pairs_of(count, 1))

    def joined_halves(keep, give):
        got = lax.ppermute(give, AXES, pairs_of(count, 1))
        return jnp.where(
            rank == 0,
            jnp.concatenate([keep, got], axis=1),
            jnp.concatenate([got, keep], axis=1),
        )

    if paired:
        sig_spec, keep, give = paired_conv(place, *halves(signal), kernel_spec, tables)
        carried = joined_halves(keep, give).astype(F32)
    else:
        sig_spec, carried_cols = long_conv(to_channels(signal), kernel_spec, tables)
        carried = to_rows(carried_cols.astype(BF)).astype(F32)
    signal_wide = signal.astype(F32)
    joined = carried + skip_gain * signal_wide
    joined_low = joined.astype(BF)
    gated_mix = (joined * outer_gate).astype(BF)
    (gated_mix,) = meet((gated_mix,), trade_adj)
    own_adj = lax.dynamic_index_in_dim(output_adjoint, side, 0, keepdims=False)
    adjoint = jnp.concatenate([own_adj, trade_adj.value], axis=0)
    ff_rows = expand_coefficients.shape[1]
    mix_rows = mixer_output_coefficients.shape[1]
    if ff_rows % 16 == 0:
        up_t = later
    else:
        up_t = later[:, :ff_rows]
    mix_t = later[:, later.shape[1] - mix_rows :].reshape(-1, width)
    folds = contract_coefficients.shape[0] // width
    down_t = (
        later[:, ff_rows : later.shape[1] - mix_rows]
        .reshape(count, folds, -1, width)
        .transpose(1, 0, 2, 3)
        .reshape(folds, width, width)
    )
    residual = tokens + dot_nt(gated_mix, mix_t) + mix_bias
    unit_two, rstd_two = normalise(residual)
    second_low = (unit_two * gain_two + shift_two).astype(BF)
    grad_out = row_mask * adjoint.astype(F32)
    grad_low = grad_out.astype(BF)
    down_proj, grad_second, up_grad, down_grad, up_bias_grad = feed_forward(
        second_low, grad_low, up_t, down_t, up_bias
    )
    up_bias_grad = up_bias_grad.reshape(-1)
    output = (row_mask * (residual + down_proj + down_bias)).astype(BF)

    up_sum = Scatter(up_grad.reshape(count, -1, width), me, count, across, BF)
    down_sum = Scatter(down_grad.reshape(count, -1, down_grad.shape[1]), me, count, up, BF)
    (grad_second,) = send(up_sum, down_sum, state=(grad_second,))
    down_bias_grad = jnp.sum(grad_out, axis=0)
    gain_two_grad = jnp.sum(grad_second * unit_two, axis=0)
    shift_two_grad = jnp.sum(grad_second, axis=0)
    grad_residual = grad_out + normalise_back(unit_two, rstd_two, grad_second * gain_two)
    mix_bias_grad = jnp.sum(grad_residual, axis=0)
    resid_low = grad_residual.astype(BF)
    mix_grad = dot_tn(resid_low, gated_mix).astype(BF)
    grad_gated = dot_nn(resid_low, mix_t)
    grad_joined = grad_gated * outer_gate
    grad_joined_low = grad_joined.astype(BF)
    skip_grad = jnp.sum(grad_joined * signal_wide, axis=0)
    (grad_joined_low, mix_grad) = meet((grad_joined_low, mix_grad), up_sum, down_sum)
    (grad_joined_low,) = send(up_sum, down_sum, state=(grad_joined_low,))
    if paired:
        keep, give, kernel_grad = paired_back(
            place, *halves(grad_joined_low), kernel_spec, sig_spec, tables
        )
        keep, give, kernel_grad = meet((keep, give, kernel_grad), up_sum, down_sum)
        keep, give = send(up_sum, down_sum, state=(keep, give))
        conv_back_low = joined_halves(keep, give)
    else:
        conv_back_cols, kernel_grad = long_back(
            to_channels(grad_joined_low), kernel_spec, sig_spec, tables
        )
        conv_back_cols, kernel_grad = meet((conv_back_cols, kernel_grad), up_sum, down_sum)
        (conv_back_cols,) = send(up_sum, down_sum, state=(conv_back_cols,))
        conv_back_low = to_rows(conv_back_cols.astype(BF))
    conv_back = conv_back_low.astype(F32)
    first = blocks_of(grad_gated)[:, :2]
    first_signal = blocks_of(row_mask)[:, :2] * (
        blocks_of(conv_back)[:, :2] + skip_gain * blocks_of(grad_joined_low)[:, :2].astype(F32)
    )
    near = projected_all[:, 14:18, width:].astype(F32)
    first_gates = conv_bias[width:] + sum(
        conv_taps[k, width:] * near[:, k : k + 2] for k in range(3)
    )
    starts = Ring(
        jnp.concatenate(
            [
                first * blocks_of(joined_low)[:, :2].astype(F32),
                first_signal * first_gates[:, :, width:],
                first_signal * first_gates[:, :, :width],
            ],
            axis=2,
        ),
        count,
        half,
        -1,
    )
    send(starts)
    (conv_back_low,) = meet((conv_back_low,), starts)
    starts = starts.value
    trade_out = Swap(output[local:], me, count, far)
    wrapped_after = jnp.stack(
        [jnp.where(side == 0, starts[1], 0.0), jnp.where(side == 1, starts[0], 0.0)]
    )
    after = jnp.where(rank == half - 1, wrapped_after, starts)
    after = jnp.concatenate([after, jnp.zeros((2, 6, after.shape[2]), F32)], axis=1)
    grad_projected, sums = tail_back(
        projected_all,
        blocks_of(grad_gated),
        blocks_of(joined_low),
        blocks_of(conv_back_low),
        blocks_of(grad_joined_low),
        after,
        blocks_of(row_mask),
        conv_taps,
        conv_bias.reshape(1, -1),
        skip_gain.reshape(1, -1),
    )
    conv_bias_grad = sums[0]
    taps_grad = sums[1:4]
    intake_bias_grad = sums[4]
    projected_low = grad_projected.reshape(rows, -1)
    (projected_low,) = meet((projected_low,), up_sum, down_sum)
    (projected_low,) = send(
        up_sum, down_sum, trade_out, state=(projected_low,)
    )
    intake_grad = dot_tn(projected_low, normed_low).astype(BF).reshape(count, -1, width)
    intake_grad, projected_low = meet((intake_grad, projected_low))
    both_grad = jnp.concatenate([intake_grad, mix_grad.reshape(count, -1, width)], axis=1)
    front_sum = Scatter(both_grad[:, :, :middle], me, count, up, BF)
    rear_sum = Scatter(both_grad[:, :, middle:], me, count, across, BF)
    (projected_low,) = send(front_sum, rear_sum, state=(projected_low,))
    unit_one, rstd_one = normalise(tokens)
    grad_normed = dot_nn(projected_low, intake_t)
    gain_one_grad = jnp.sum(grad_normed * unit_one, axis=0)
    shift_one_grad = jnp.sum(grad_normed, axis=0)
    tokens_grad = (
        grad_residual + normalise_back(unit_one, rstd_one, grad_normed * gain_one)
    ).astype(BF)
    tokens_grad, kernel_grad = meet(
        (tokens_grad, kernel_grad), up_sum, down_sum, front_sum, rear_sum
    )
    (kernel_grad,) = send(
        up_sum, down_sum, front_sum, rear_sum, state=(kernel_grad,)
    )

    vector_grads = (
        gain_one_grad,
        shift_one_grad,
        skip_grad,
        mix_bias_grad,
        gain_two_grad,
        shift_two_grad,
        down_bias_grad,
        intake_bias_grad,
        conv_bias_grad,
        taps_grad,
        up_bias_grad,
    )
    pieces = []
    for g in vector_grads:
        if g.ndim == 1:
            pieces.append(g.reshape(count, -1))
        else:
            pieces.append(
                g.reshape(g.shape[0], count, -1).transpose(1, 0, 2).reshape(count, -1)
            )
    packed = jnp.concatenate(pieces + [jnp.zeros((count, pad), F32)], axis=1)
    bundle_sum = Exchange(packed.reshape(count, 8, -1))
    trade_tokens = Swap(tokens_grad[local:], me, count, far)
    (kernel_grad,) = send(bundle_sum, trade_tokens, state=(kernel_grad,))
    column_grad, net = filter_back(
        kernel_grad,
        shaping,
        columns,
        hidden,
        m1,
        m2,
        features,
        p1,
        p2,
        p3,
        c1,
        c2,
        c3,
        frequency,
        filter_second_coefficients,
        filter_third_coefficients,
        8 * count,
    )
    column_grad, net = meet(
        (column_grad, net), bundle_sum, front_sum, rear_sum, up_sum, down_sum, trade_out
    )
    filter_full = lax.dynamic_update_slice_in_dim(
        jnp.zeros((width, hidden.shape[1]), F32), column_grad, chan_start, 0
    )
    emb, filt = filter_entry_coefficients.shape
    share = filter_full.shape[0] // count
    final_sum = Exchange(
        jnp.concatenate(
            [filter_full.reshape(count, share, filt), net.reshape(count, -1, filt)], axis=1
        )
    )
    (filter_full,) = send(final_sum, state=(filter_full,))
    send(front_sum, rear_sum)
    meet((), front_sum, rear_sum, trade_tokens)
    send(front_sum, rear_sum)
    meet((), front_sum, rear_sum, final_sum)
    final_grad = final_sum.value[:share]
    net_part = final_sum.value[share:]
    net_all = Exchange(jnp.broadcast_to(net_part, (count,) + net_part.shape), add=False)
    send(net_all)
    send(front_sum, rear_sum)
    drain(net_all, bundle_sum, final_sum, front_sum, rear_sum, up_sum, down_sum, trade_tokens)
    summed = bundle_sum.value.reshape(-1)
    small = []
    at = 0
    for v in vectors:
        small.append(summed[at : at + v.size].reshape(v.shape))
        at += v.size
    total = net_all.value.reshape(-1, filt)
    second_at, third_at, vec_at = net_places(emb, filt)
    net_out = (
        total[:emb],
        total[vec_at],
        total[second_at : second_at + filt],
        total[vec_at + 1],
        total[third_at : third_at + filt],
        total[vec_at + 2],
        total[vec_at + 3],
    )
    both_shard = jnp.concatenate([front_sum.value, rear_sum.value], axis=1)
    intake_rows = intake_grad.shape[1]
    intake_shard_grad = both_shard[:intake_rows]

    def at_home(near, far_part):
        held = jnp.zeros((2,) + near.shape, near.dtype)
        held = lax.dynamic_update_slice_in_dim(held, near[None], side, 0)
        return lax.dynamic_update_slice_in_dim(held, far_part[None], 1 - side, 0)

    output_home = at_home(output[:local], trade_out.value)
    tokens_home = at_home(tokens_grad[:local], trade_tokens.value)
    return (
        output_home,
        tokens_home,
        small[0],
        small[1],
        intake_shard_grad.T,
        small[7],
        small[9],
        small[8],
        small[2],
        final_grad.T,
        both_shard[intake_rows:].T,
        small[3],
        small[4],
        small[5],
        up_sum.value.T,
        small[10],
        down_sum.value.T,
        small[6],
    ) + net_out

def solution(mesh):
    in_specs = (
        P("dp", "seq", None),
        P("dp", None),
        P("dp", "seq", None),
        P(("dp", "seq")),
        P(("dp", "seq")),
        P(None, ("dp", "seq")),
        P(("dp", "seq")),
        P(None, ("dp", "seq")),
        P(("dp", "seq")),
        P(("dp", "seq")),
        P(None, ("dp", "seq")),
        P(None, ("dp", "seq")),
        P(("dp", "seq")),
        P(("dp", "seq")),
        P(("dp", "seq")),
        P(None, ("dp", "seq")),
        P(("dp", "seq")),
        P(None, ("dp", "seq")),
        P(("dp", "seq")),
        P(),
        P(),
        P(),
        P(),
        P(),
        P(),
        P(),
    )
    out_specs = (
        P("dp", "seq", None),
        P("dp", "seq", None),
        P(("dp", "seq")),
        P(("dp", "seq")),
        P(None, ("dp", "seq")),
        P(("dp", "seq")),
        P(None, ("dp", "seq")),
        P(("dp", "seq")),
        P(("dp", "seq")),
        P(None, ("dp", "seq")),
        P(None, ("dp", "seq")),
        P(("dp", "seq")),
        P(("dp", "seq")),
        P(("dp", "seq")),
        P(None, ("dp", "seq")),
        P(("dp", "seq")),
        P(None, ("dp", "seq")),
        P(("dp", "seq")),
        P(),
        P(),
        P(),
        P(),
        P(),
        P(),
        P(),
    )
    return jax.shard_map(
        per_device, mesh=mesh, in_specs=in_specs, out_specs=out_specs, check_vma=False
    )
```
